32 devices in a mesh: seq: 4 (over x, core), tensor: 4 (over z), dp: 2 (over y).
Axes of the slice: x: 2, y: 2, z: 4, core: 2. Of those that a mesh axis runs over, the one named last changes fastest.
Arguments:
- ssm_input: bfloat16 [2, 1024, 4096], P('dp', 'seq', 'tensor'), may hold values from -6 to 6
- b_input: bfloat16 [2, 1024, 512], P('dp', 'seq', 'tensor'), may hold values from -0.125 to 0.125
- c_input: bfloat16 [2, 1024, 512], P('dp', 'seq', 'tensor'), may hold values from -0.125 to 0.125
- step_size: float32 [2, 64, 1024], P('dp', 'tensor', 'seq'), may hold values from 0 to 1024, as said below
- decay_rate: float32 [64], P('tensor'), may hold values from 0 to 1, as said below
- skip_gain: float32 [64], P('tensor'), may hold values from 0.5 to 2
- resets: int32 [2, 4], P('dp', 'seq'), may hold values 0 or 1
- out_grad: bfloat16 [2, 1024, 4096], P('dp', 'seq'), may hold values from -6 to 6
- out_weight: bfloat16 [4096, 4096], P(('seq', 'dp'), 'tensor'), may hold values from -0.09375 to 0.09375
Outputs:
- grad_input: bfloat16 [2, 1024, 4096], P('dp', 'seq', 'tensor')
- grad_b: float32 [2, 1024, 512], P('dp', 'seq', 'tensor')
- grad_c: float32 [2, 1024, 512], P('dp', 'seq', 'tensor')
- grad_weight: float32 [4096, 4096], P(('seq', 'dp'), 'tensor')
The draws below stay inside these ranges and needn't reach their ends.
Inputs may be any that keep to these rules, and one draw needn't show every extreme that they name: `step_size`: positive per-position steps. `decay_rate`: positive per-head rates.
All inputs are finite; a program needn't handle non-finite values. No bound on the sum of `resets` on one device may be relied on, other than what follows from the above.
Results may differ from the reference program's by a relative error of at most 0.017.
Values may be sent and summed in bfloat16 or wider, within the bound.
No kernel may reach another device: no remote copies, remote signals or barrier semaphores. Data moves between devices by JAX's collectives and lax.ppermute only.
A program may use at most 128 MiB of HBM per device.

```python
import math
import jax
import jax.numpy as jnp
from jax import lax

D = 4096
P_SIZE = 64
N = 128
HEADS_DEV = 16
Q = 256
GROUPS = 4
HEADS = 64
SEQUENCE_LENGTH = 1024
DIALOGUE_BATCH = 2
NBLOCKS = 4


def draw_decay_rate(key, part):
    pick_key, slow_key, fast_key = jax.random.split(key, 3)
    slow_share = 0.5
    slow_flag = jax.random.uniform(pick_key, (HEADS,)) < slow_share
    slow_rate = jnp.exp(jax.random.uniform(slow_key, (HEADS,), minval=math.log(0.2 / SEQUENCE_LENGTH), maxval=math.log(2.0 / SEQUENCE_LENGTH)))
    fast_rate = jnp.exp(jax.random.uniform(fast_key, (HEADS,), minval=math.log(0.02), maxval=math.log(0.06)))
    return jnp.where(slow_flag, slow_rate, fast_rate).astype(jnp.float32)


def draw_step_size(key, part):
    baseline_key, spike_random_key, amplitude_key = jax.random.split(key, 3)
    baseline_step_count = jax.random.uniform(baseline_key, (DIALOGUE_BATCH, HEADS, SEQUENCE_LENGTH), minval=0.5, maxval=1.5)
    spike_indicator = jax.random.uniform(spike_random_key, (DIALOGUE_BATCH, 1, SEQUENCE_LENGTH)) < 3.0 / SEQUENCE_LENGTH
    spike_magnitude = jax.random.uniform(amplitude_key, (DIALOGUE_BATCH, 1, SEQUENCE_LENGTH), minval=0.2, maxval=0.6) * SEQUENCE_LENGTH
    return jnp.where(spike_indicator, baseline_step_count + spike_magnitude, baseline_step_count).astype(jnp.float32)


def set_ends(result, stream_key, smallest, largest):
    shape = result.shape
    place = [jax.random.randint(jax.random.fold_in(stream_key, axis), (), 0, shape[axis]) for axis in range(len(shape))]
    result = result.at[tuple(place)].set(smallest)
    longest = shape.index(max(shape))
    place[longest] = (place[longest] + 1) % shape[longest]
    return result.at[tuple(place)].set(largest)


def block_scale(key, dims, pieces, smallest, top_value):
    factor_of, own = 1.0, jax.random.fold_in(key, 6)
    for axis_at, parts in pieces:
        heights = jnp.exp(jax.random.uniform(jax.random.fold_in(own, axis_at), (parts,), jnp.float32, smallest / len(pieces), top_value / len(pieces)))
        factor_of = factor_of * jnp.repeat(heights, dims[axis_at] // parts).reshape([-1 if axis == axis_at else 1 for axis in range(len(dims))])
    return factor_of


def noise(own_key, extent, scale, limit, pieces=(), kind=jnp.bfloat16):
    array = scale * jax.random.normal(own_key, extent, jnp.float32)
    if pieces:
        array = array * block_scale(own_key, extent, pieces, -0.22, 0.18)
    return jnp.clip(array, -limit, limit).astype(kind)


def setup_inputs(seed: int = 0) -> dict:
    keys = jax.random.split(jax.random.key(seed), 10)
    return {
        "ssm_input": noise(keys[0], (DIALOGUE_BATCH, SEQUENCE_LENGTH, HEADS * P_SIZE), 1.0, 6.0, ((0, 2), (1, 4), (2, 4))),
        "b_input": noise(keys[1], (DIALOGUE_BATCH, SEQUENCE_LENGTH, GROUPS * N), (N * 16) ** -0.5, 0.125, ((0, 2), (1, 4), (2, 4))),
        "c_input": noise(keys[2], (DIALOGUE_BATCH, SEQUENCE_LENGTH, GROUPS * N), (N * 16) ** -0.5, 0.125, ((0, 2), (1, 4), (2, 4))),
        "step_size": draw_step_size(jax.random.fold_in(keys[9], 71), 0),
        "decay_rate": draw_decay_rate(jax.random.fold_in(keys[9], 71), 0),
        "skip_gain": jnp.clip(jnp.exp(math.log(2.0) - 1.3862944 * jax.random.uniform(keys[5], (HEADS,), jnp.float32) ** block_scale(keys[5], (HEADS,), ((0, 4),), -0.2, 0.2)), 0.5, 2.0),
        "resets": set_ends((jax.random.randint(keys[6], (DIALOGUE_BATCH, NBLOCKS), 0, 8) < 1).astype(jnp.int32), jax.random.fold_in(keys[6], 1), 0, 1),
        "out_grad": noise(keys[7], (DIALOGUE_BATCH, SEQUENCE_LENGTH, D), 1.0, 6.0, ((0, 2), (1, 4))),
        "out_weight": noise(keys[8], (D, HEADS * P_SIZE), (HEADS * P_SIZE) ** -0.5, 0.09375, ((0, 8), (1, 4))),
    }


def contract(pattern, former, latter):
    return jnp.einsum(pattern, former.astype(jnp.float32), latter.astype(jnp.float32))


def block_tables(step_rows, head_rates):
    log_decay = jnp.cumsum(-step_rows * head_rates[..., None], axis=-1)
    last_log = log_decay[..., -1:]
    damping = jnp.exp(last_log[..., 0])
    to_end = jnp.moveaxis(jnp.exp(last_log - log_decay), -1, 0)[..., None]
    from_start = jnp.moveaxis(jnp.exp(log_decay), -1, 0)[..., None]
    positions = jnp.arange(log_decay.shape[-1])
    causal = positions[:, None] >= positions[None, :]
    spread = log_decay[..., :, None] - log_decay[..., None, :]
    weights = jnp.where(causal, jnp.exp(jnp.minimum(spread, 0.0)), 0.0)
    return damping, to_end, from_start, weights


def block_sums(inputs, b_rows, c_rows, grad_rows, to_end, from_start):
    weighted_in = (inputs.astype(jnp.float32) * to_end).astype(jnp.bfloat16)
    weighted_grad = (grad_rows.astype(jnp.float32) * from_start).astype(jnp.bfloat16)
    carried = contract('qgkp,qgn->gkpn', weighted_in, b_rows)
    adjoint = contract('qgkp,qgn->gkpn', weighted_grad, c_rows)
    return carried, adjoint, weighted_in, weighted_grad


def block_grads(inputs, b_rows, c_rows, grad_rows, skip_rows, to_end, from_start, weights, weighted_in, weighted_grad, state_in, adjoint_out):
    scores = contract('ign,jgn->gij', c_rows, b_rows)
    mixing = (weights * scores[:, None]).astype(jnp.bfloat16)
    skip_term = skip_rows[None, :, :, None]
    output = contract('gkij,jgkp->igkp', mixing, inputs) + from_start * contract('gkpn,ign->igkp', state_in, c_rows) + skip_term * inputs.astype(jnp.float32)
    grad_in = contract('gkij,igkp->jgkp', mixing, grad_rows) + to_end * contract('gkpn,jgn->jgkp', adjoint_out, b_rows) + skip_term * grad_rows.astype(jnp.float32)
    products = contract('igkp,jgkp->gkij', grad_rows, inputs)
    paired = (weights * products).astype(jnp.bfloat16)
    grad_b = contract('gkij,ign->jgn', paired, c_rows) + contract('jgkp,gkpn->jgn', weighted_in, adjoint_out)
    grad_c = contract('gkij,jgn->ign', paired, b_rows) + contract('igkp,gkpn->ign', weighted_grad, state_in)
    return output.astype(jnp.bfloat16), grad_in.astype(jnp.bfloat16), grad_b, grad_c


def forward_step(running, sliced):
    kept, carried, damping = sliced
    state_in = kept * running
    return damping[..., None, None] * state_in + carried, state_in


def backward_step(running, sliced):
    kept, adjoint, damping = sliced
    return kept * (damping[..., None, None] * running + adjoint), running


def reference(ssm_input, b_input, c_input, step_size, decay_rate, skip_gain, resets, out_grad, out_weight):
    head_rates = decay_rate.reshape(GROUPS, HEADS_DEV)
    skip_rows = skip_gain.reshape(GROUPS, HEADS_DEV)
    grad_weight = jnp.zeros((D, HEADS * P_SIZE), jnp.float32)
    all_in, all_b, all_c = [], [], []
    for batch_row in range(DIALOGUE_BATCH):
        inputs = ssm_input[batch_row].reshape(NBLOCKS, Q, GROUPS, HEADS_DEV, P_SIZE)
        b_rows = b_input[batch_row].reshape(NBLOCKS, Q, GROUPS, N)
        c_rows = c_input[batch_row].reshape(NBLOCKS, Q, GROUPS, N)
        step_rows = step_size[batch_row].reshape(GROUPS, HEADS_DEV, NBLOCKS, Q).transpose(2, 0, 1, 3)
        incoming = out_grad[batch_row].reshape(NBLOCKS, Q, D)
        keep_rows = (1 - resets[batch_row]).astype(jnp.float32)

        def head_grads(out_rows):
            return jnp.dot(out_rows, out_weight, preferred_element_type=jnp.float32).astype(jnp.bfloat16).reshape(Q, GROUPS, HEADS_DEV, P_SIZE)

        def first_pass(sliced):
            in_rows, brow_block, crow_block, step_block, out_rows = sliced
            damping, to_end, from_start, weights = block_tables(step_block, head_rates)
            carried, adjoint, weighted_in, weighted_grad = block_sums(in_rows, brow_block, crow_block, head_grads(out_rows), to_end, from_start)
            return damping, carried, adjoint

        decays, carried, adjoint = lax.map(first_pass, (inputs, b_rows, c_rows, step_rows, incoming))
        zero_state = jnp.zeros((GROUPS, HEADS_DEV, P_SIZE, N), jnp.float32)
        final_state, states = lax.scan(forward_step, zero_state, (keep_rows, carried, decays))
        final_adjoint, adjoints = lax.scan(backward_step, zero_state, (keep_rows, adjoint, decays), reverse=True)

        def second_pass(accumulated, sliced):
            in_rows, brow_block, crow_block, step_block, out_rows, state_block, adjoint_block = sliced
            grad_rows = head_grads(out_rows)
            damping, to_end, from_start, weights = block_tables(step_block, head_rates)
            carried_now, adjoint_now, weighted_in, weighted_grad = block_sums(in_rows, brow_block, crow_block, grad_rows, to_end, from_start)
            output, grad_in, grad_b, grad_c = block_grads(in_rows, brow_block, crow_block, grad_rows, skip_rows, to_end, from_start, weights, weighted_in, weighted_grad, state_block.astype(jnp.bfloat16), adjoint_block.astype(jnp.bfloat16))
            accumulated = accumulated + jnp.dot(out_rows.T, output.reshape(Q, HEADS * P_SIZE), preferred_element_type=jnp.float32)
            return accumulated, (grad_in, grad_b, grad_c)

        grad_weight, (grad_in, grad_b, grad_c) = lax.scan(second_pass, grad_weight, (inputs, b_rows, c_rows, step_rows, incoming, states, adjoints))
        all_in.append(grad_in.reshape(SEQUENCE_LENGTH, HEADS * P_SIZE))
        all_b.append(grad_b.reshape(SEQUENCE_LENGTH, GROUPS * N))
        all_c.append(grad_c.reshape(SEQUENCE_LENGTH, GROUPS * N))
    return jnp.stack(all_in), jnp.stack(all_b), jnp.stack(all_c), grad_weight
```

```python
import functools

import jax
import jax.numpy as jnp
from jax import lax
from jax.experimental import pallas as pl
from jax.experimental.pallas import tpu as pltpu
from jax.sharding import PartitionSpec as P

P_SIZE = 64
N = 128
Q = 256
HALF = 128
PAIR = 2 * P_SIZE
CHUNKS = 2
BF = jnp.bfloat16
F32 = jnp.float32

VMEM = pl.BlockSpec(memory_space=pltpu.VMEM)
SMEM = pl.BlockSpec(memory_space=pltpu.SMEM)


def call(kernel, args, outs, flops=0, scalars=0, mib=24):
    out_shape = [jax.ShapeDtypeStruct(shape, kind) for shape, kind in outs]
    moved = sum(a.size * a.dtype.itemsize for a in list(args) + out_shape)
    return pl.pallas_call(
        kernel,
        out_shape=out_shape,
        in_specs=[SMEM] * scalars + [VMEM] * (len(args) - scalars),
        out_specs=[VMEM] * len(outs),
        cost_estimate=pl.CostEstimate(flops=flops, bytes_accessed=moved, transcendentals=0),
        compiler_params=pltpu.CompilerParams(vmem_limit_bytes=mib * 2**20),
    )(*args)


def dot(a, b, left, right):
    return lax.dot_general(a, b, (((left,), (right,)), ((), ())), preferred_element_type=F32)


def first_head(rows=Q):
    return lax.broadcasted_iota(jnp.int32, (rows, PAIR), 1) < P_SIZE


def spread(table, pair, first):
    return jnp.where(first, table[:, 2 * pair : 2 * pair + 1], table[:, 2 * pair + 1 : 2 * pair + 2])


def gains(skip_ref, head):
    first = lax.broadcasted_iota(jnp.int32, (1, PAIR), 1) < P_SIZE
    return jnp.where(first, skip_ref[head], skip_ref[head + 1])


def tables_kernel(rate_ref, x_ref, b_ref, step_ref, state_ref, weighted_ref, rows_ref, cols_ref, decay_ref):
    heads = step_ref.shape[0]
    head_id = lax.broadcasted_iota(jnp.int32, (heads, Q), 0)
    lane = lax.broadcasted_iota(jnp.int32, (heads, Q), 1)
    rate = jnp.zeros((heads, Q), F32)
    for head in range(heads):
        rate = jnp.where(head_id == head, rate_ref[head], rate)
    log = -step_ref[...] * rate
    shift = 1
    while shift < Q:
        log = log + jnp.where(lane >= shift, pltpu.roll(log, shift, 1), 0.0)
        shift *= 2
    rows_ref[...] = log
    cols = log.T
    cols_ref[...] = cols
    first = first_head()
    for pair in range(heads // 2):
        at = slice(pair * PAIR, (pair + 1) * PAIR)
        log_pair = spread(cols, pair, first)
        last = log_pair[Q - 1 : Q, :]
        weighted_ref[:, at] = (x_ref[:, at].astype(F32) * jnp.exp(last - log_pair)).astype(BF)
        decay_ref[:, at] = jnp.broadcast_to(jnp.exp(last), (8, PAIR))
    state_ref[...] = dot(b_ref[...], weighted_ref[...], 0, 0)


def local_output_kernel(skip_ref, x_ref, b_ref, c_ref, rows_ref, cols_ref, out_ref):
    heads = rows_ref.shape[0]
    scores = dot(c_ref[...], b_ref[...], 1, 1)
    at_row = lax.broadcasted_iota(jnp.int32, (HALF, HALF), 0)
    at_lane = lax.broadcasted_iota(jnp.int32, (HALF, HALF), 1)
    causal = at_row >= at_lane
    first = first_head()
    zero = jnp.zeros((Q, PAIR), BF)
    for pair in range(heads // 2):
        at = slice(pair * PAIR, (pair + 1) * PAIR)
        x_pair = x_ref[:, at]
        skip = gains(skip_ref, 2 * pair) * x_pair.astype(F32)
        top, bottom = skip[:HALF], skip[HALF:]
        for side in range(2):
            head = 2 * pair + side
            x_head = jnp.where(first, x_pair, zero) if side == 0 else jnp.where(first, zero, x_pair)
            col = cols_ref[:, head : head + 1]
            row = rows_ref[head : head + 1, :]

            def mix(i, j):
                span = col[i * HALF : (i + 1) * HALF] - row[:, j * HALF : (j + 1) * HALF]
                weight = jnp.exp(jnp.minimum(span, 0.0))
                if i == j:
                    weight = jnp.where(causal, weight, 0.0)
                return (weight * scores[i * HALF : (i + 1) * HALF, j * HALF : (j + 1) * HALF]).astype(BF)

            top += dot(mix(0, 0), x_head[:HALF], 1, 0)
            bottom += dot(jnp.concatenate([mix(1, 0), mix(1, 1)], axis=1), x_head, 1, 0)
        out_ref[:HALF, at] = top
        out_ref[HALF:, at] = bottom


def output_kernel(local_ref, c_ref, cols_ref, state_ref, out_ref):
    first = first_head()
    cols = cols_ref[...]
    for pair in range(out_ref.shape[1] // PAIR):
        at = slice(pair * PAIR, (pair + 1) * PAIR)
        term = dot(c_ref[...], state_ref[:, at], 1, 0)
        out_ref[:, at] = (local_ref[:, at] + jnp.exp(spread(cols, pair, first)) * term).astype(BF)


def head_partial_kernel(blocks, index_ref, *refs):
    grads, weights, outs = refs[: -blocks - 0], None, None
    count = (len(refs) - blocks) // 2
    grads, weights, outs = refs[:count], refs[count : count + blocks], refs[count + blocks :]
    depth = weights[0].shape[0]
    for number in reversed(range(count)):
        total = None
        for block in range(blocks):
            columns = pl.ds(pl.multiple_of(index_ref[block] * depth, depth), depth)
            term = dot(grads[number][:, columns], weights[block][...], 1, 0)
            total = term if total is None else total + term
        outs[number][...] = total.astype(outs[number].dtype)


def adjoint_kernel(others, own_ref, *refs):
    parts, (c_ref, cols_ref, head_ref, weighted_ref, adjoint_ref) = refs[:others], refs[others:]
    first = first_head()
    cols = cols_ref[...]
    for pair in range(head_ref.shape[1] // PAIR):
        at = slice(pair * PAIR, (pair + 1) * PAIR)
        total = own_ref[:, at]
        for part in parts:
            total = total + part[:, at].astype(F32)
        head = total.astype(BF)
        head_ref[:, at] = head
        weighted_ref[:, at] = (head.astype(F32) * jnp.exp(spread(cols, pair, first))).astype(BF)
    adjoint_ref[...] = dot(c_ref[...], weighted_ref[...], 0, 0)


def local_grads_kernel(
    skip_ref, x_ref, grad_ref, b_ref, c_ref, rows_ref, cols_ref, weighted_ref, state_ref, in_ref, paired_ref, c_out_ref
):
    heads = rows_ref.shape[0]
    scores = dot(b_ref[...], c_ref[...], 1, 1)
    at_row = lax.broadcasted_iota(jnp.int32, (HALF, HALF), 0)
    at_lane = lax.broadcasted_iota(jnp.int32, (HALF, HALF), 1)
    causal = at_lane >= at_row
    first = first_head()
    zero = jnp.zeros((Q, PAIR), BF)
    paired_ref[...] = jnp.zeros_like(paired_ref)
    for pair in range(heads // 2):
        at = slice(pair * PAIR, (pair + 1) * PAIR)
        x_pair = x_ref[:, at]
        g_pair = grad_ref[:, at]
        skip = gains(skip_ref, 2 * pair) * g_pair.astype(F32)
        top, bottom = skip[:HALF], skip[HALF:]
        for side in range(2):
            head = 2 * pair + side
            g_head = jnp.where(first, g_pair, zero) if side == 0 else jnp.where(first, zero, g_pair)
            col = cols_ref[:, head : head + 1]
            row = rows_ref[head : head + 1, :]

            def weigh(j, i):
                span = row[:, i * HALF : (i + 1) * HALF] - col[j * HALF : (j + 1) * HALF]
                weight = jnp.exp(jnp.minimum(span, 0.0))
                return jnp.where(causal, weight, 0.0) if i == j else weight

            early = jnp.concatenate([weigh(0, 0), weigh(0, 1)], axis=1)
            late = weigh(1, 1)
            top += dot((early * scores[:HALF]).astype(BF), g_head, 1, 0)
            bottom += dot((late * scores[HALF:, HALF:]).astype(BF), g_head[HALF:], 1, 0)
            paired_ref[:HALF, :] += early * dot(x_pair[:HALF], g_head, 1, 1)
            paired_ref[HALF:, HALF:] += late * dot(x_pair[HALF:], g_head[HALF:], 1, 1)
        in_ref[:HALF, at] = top
        in_ref[HALF:, at] = bottom
    c_out_ref[...] = dot(weighted_ref[...], state_ref[...], 1, 1)


def final_kernel(parts, *refs):
    b_ref, c_ref, cols_ref, weighted_ref = refs[:4]
    locals_, pairs, c_parts, adjoints = (refs[4 + i * parts : 4 + (i + 1) * parts] for i in range(4))
    in_ref, grad_b_ref, grad_c_ref = refs[4 + 4 * parts :]
    first = first_head()
    cols = cols_ref[...]
    paired = functools.reduce(jnp.add, [ref[...] for ref in pairs]).astype(BF)
    grad_b = dot(paired, c_ref[...], 1, 0)
    grad_c = dot(paired, b_ref[...], 0, 0)
    for part in range(parts):
        grad_c += c_parts[part][...]
        width = locals_[part].shape[1]
        grad_b += dot(weighted_ref[:, part * width : (part + 1) * width], adjoints[part][...], 1, 1)
        for number in range(width // PAIR):
            at = slice(number * PAIR, (number + 1) * PAIR)
            pair = part * (width // PAIR) + number
            whole = slice(pair * PAIR, (pair + 1) * PAIR)
            log_pair = spread(cols, pair, first)
            to_end = jnp.exp(log_pair[Q - 1 : Q, :] - log_pair)
            term = dot(b_ref[...], adjoints[part][:, at], 1, 0)
            in_ref[:, whole] = (locals_[part][:, at] + to_end * term).astype(BF)
    grad_b_ref[...] = grad_b
    grad_c_ref[...] = grad_c


def weight_partial_kernel(count, index_ref, *refs):
    grads, outputs, (sent_ref, kept_ref) = refs[:count], refs[count : 2 * count], refs[2 * count :]
    depth = sent_ref.shape[0]
    for slot, target in ((1, sent_ref), (0, kept_ref)):
        columns = pl.ds(pl.multiple_of(index_ref[slot] * depth, depth), depth)
        total = None
        for grad, output in zip(grads, outputs):
            term = dot(grad[:, columns], output[...], 0, 0)
            total = term if total is None else total + term
        target[...] = total.astype(target.dtype)


def body(
    ssm_input, b_input, c_input, step_size, decay_rate, skip_gain, resets, out_grad, out_weight
):
    seq, dp = lax.axis_size("seq"), lax.axis_size("dp")
    chips = seq // 2
    me, dialogue = lax.axis_index("seq"), lax.axis_index("dp")
    chip, core = me // 2, me % 2
    heads = decay_rate.shape[0]
    wide = heads * P_SIZE
    width = wide // CHUNKS
    chunk_heads = heads // CHUNKS
    depth = out_weight.shape[0]
    span = 2 * dp * depth
    assert ssm_input.shape[1] == Q and dp == 2 and seq % 2 == 0

    across = [(i, i ^ 1) for i in range(seq)]

    def core_swap(value):
        return lax.ppermute(value, "seq", across)

    def chip_shift(value, by):
        return lax.ppermute(value, "seq", [(i, (i + 2 * by) % seq) for i in range(seq)])

    def dialogue_swap(value):
        return lax.ppermute(value, "dp", [(0, 1), (1, 0)])

    x, b_rows, c_rows, steps, incoming = (
        ssm_input[0], b_input[0], c_input[0], step_size[0], out_grad[0]
    )
    keep = (1 - resets[0, 0]).astype(F32)
    chunk = lambda value, part: value[:, part * width : (part + 1) * width]

    weights = []
    for part in range(CHUNKS):
        own = chunk(out_weight, part)
        other = dialogue_swap(own)
        weights.append([own, other, core_swap(own), core_swap(other)])
    rows_of = [core * dp + dialogue, core * dp + 1 - dialogue, (1 - core) * dp + dialogue, (1 - core) * dp + 1 - dialogue]
    weight_index = jnp.stack(rows_of).astype(jnp.int32)

    own_columns = lax.dynamic_slice_in_dim(incoming, chip * span, span, axis=1)
    columns = [own_columns]
    for by in range(1, chips):
        there = (chip + by) % chips
        columns.append(chip_shift(lax.dynamic_slice_in_dim(incoming, there * span, span, axis=1), by))

    state, weighted_in, log_rows, log_cols, decay = call(
        tables_kernel,
        (decay_rate, x, b_rows, steps),
        [((N, wide), F32), ((Q, wide), BF), ((heads, Q), F32), ((Q, heads), F32), ((8, wide), F32)],
        scalars=1,
    )
    through = keep * decay[:1]
    entering = jnp.zeros((N, wide), BF)
    for hop in range(chips):
        leaving = through * entering.astype(F32) + state
        from_even = core_swap(leaving.astype(BF))
        if hop < chips - 1:
            total = (through * from_even.astype(F32) + state).astype(BF)
            entering = lax.ppermute(
                total, "seq", [(2 * i + 1, 2 * i + 2) for i in range(chips - 1)]
            )
    state_in = (keep * jnp.where(core == 1, from_even, entering).astype(F32)).astype(BF)
    local_output, = call(
        local_output_kernel,
        (skip_gain, x, b_rows, c_rows, log_rows, log_cols),
        [((Q, wide), F32)],
        flops=2 * heads * Q * Q * P_SIZE,
        scalars=1,
    )
    outputs = []
    for part in range(CHUNKS):
        cols = log_cols[:, part * chunk_heads : (part + 1) * chunk_heads]
        output, = call(
            output_kernel,
            (chunk(local_output, part), c_rows, cols, chunk(state_in, part)),
            [((Q, width), BF)],
            flops=2 * Q * N * width,
        )
        mine = [output] + [chip_shift(output, by) for by in range(1, chips)]
        outputs.append(mine + [core_swap(piece) for piece in mine])

    half = dp * depth
    own_half = [lax.dynamic_slice_in_dim(piece, core * half, half, axis=1) for piece in columns]
    other_half = [
        core_swap(lax.dynamic_slice_in_dim(piece, (1 - core) * half, half, axis=1)) for piece in columns
    ]
    dialogue_index = jnp.stack([dialogue, 1 - dialogue]).astype(jnp.int32)
    weight_grads = []
    for part in range(CHUNKS):
        sent, kept = call(
            functools.partial(weight_partial_kernel, 2 * chips),
            (dialogue_index, *own_half, *other_half, *outputs[part]),
            [((depth, width), BF), ((depth, width), F32)],
            flops=2 * seq * Q * half * width,
            scalars=1,
        )
        weight_grads.append(kept + dialogue_swap(sent).astype(F32))
    grad_weight = jnp.concatenate(weight_grads, axis=1)

    locals_, pairs, c_parts, adjoints_out = [], [], [], []
    for part in range(CHUNKS):
        partials = call(
            functools.partial(head_partial_kernel, len(weights[part])),
            (weight_index, *columns, *weights[part]),
            [((Q, width), F32)] + [((Q, width), BF)] * (chips - 1),
            flops=2 * chips * Q * span * width,
            scalars=1,
        )
        returned = [chip_shift(partials[by], -by) for by in range(1, chips)]
        cols = log_cols[:, part * chunk_heads : (part + 1) * chunk_heads]
        rows = log_rows[part * chunk_heads : (part + 1) * chunk_heads]
        head_grad, weighted_grad, adjoint = call(
            functools.partial(adjoint_kernel, chips - 1),
            (partials[0], *returned, c_rows, cols),
            [((Q, width), BF), ((Q, width), BF), ((N, width), F32)],
            flops=2 * Q * N * width,
        )
        decayed = chunk(decay[:1], part)
        entering = jnp.zeros((N, width), BF)
        for hop in range(chips):
            leaving = keep * (decayed * entering.astype(F32) + adjoint)
            from_odd = core_swap(leaving.astype(BF))
            if hop < chips - 1:
                total = (keep * (decayed * from_odd.astype(F32) + adjoint)).astype(BF)
                entering = lax.ppermute(
                    total, "seq", [(2 * i + 2, 2 * i + 1) for i in range(chips - 1)]
                )
        adjoints_out.append(jnp.where(core == 0, from_odd, entering))
        local_in, paired, c_part = call(
            local_grads_kernel,
            (
                skip_gain[part * chunk_heads : (part + 1) * chunk_heads],
                chunk(x, part),
                head_grad,
                b_rows,
                c_rows,
                rows,
                cols,
                weighted_grad,
                chunk(state_in, part),
            ),
            [((Q, width), F32), ((Q, Q), F32), ((Q, N), F32)],
            flops=4 * chunk_heads * Q * Q * P_SIZE,
            scalars=1,
        )
        locals_.append(local_in)
        pairs.append(paired)
        c_parts.append(c_part)
    grad_in, grad_b, grad_c = call(
        functools.partial(final_kernel, CHUNKS),
        (b_rows, c_rows, log_cols, weighted_in, *locals_, *pairs, *c_parts, *adjoints_out),
        [((Q, wide), BF), ((Q, N), F32), ((Q, N), F32)],
        flops=4 * Q * N * wide,
    )
    return grad_in[None], grad_b[None], grad_c[None], grad_weight


def solution(mesh):
    in_specs = (
        P("dp", "seq", "tensor"),
        P("dp", "seq", "tensor"),
        P("dp", "seq", "tensor"),
        P("dp", "tensor", "seq"),
        P("tensor"),
        P("tensor"),
        P("dp", "seq"),
        P("dp", "seq", None),
        P(("seq", "dp"), "tensor"),
    )
    out_specs = (
        P("dp", "seq", "tensor"),
        P("dp", "seq", "tensor"),
        P("dp", "seq", "tensor"),
        P(("seq", "dp"), "tensor"),
    )
    return jax.shard_map(body, mesh=mesh, in_specs=in_specs, out_specs=out_specs, check_vma=False)
```

```python
import functools

import jax
import jax.numpy as jnp
import numpy as np
from jax import lax
from jax.experimental import pallas as pl
from jax.experimental.pallas import tpu as pltpu
from jax.sharding import PartitionSpec as P

P_SIZE = 64
N = 128
Q = 256
HALF = 128
PAIR = 2 * P_SIZE
CHUNKS = 2
PARITY, CORE, ODD, CHIP = 4, 6, 7, 8
BF = jnp.bfloat16
F32 = jnp.float32

SMEM = pl.BlockSpec(memory_space=pltpu.SMEM)
ANY = pl.BlockSpec(memory_space=pl.ANY)
FREE = pl.CostEstimate(flops=0, bytes_accessed=0, transcendentals=0)
LIMIT = pltpu.CompilerParams(vmem_limit_bytes=16 * 2**20)


def name_of(kernel):
    return getattr(kernel, "func", kernel).__name__


def whole(shape):
    return pl.BlockSpec(shape, lambda *_: (0,) * len(shape))


def columns_of(array, width, part):
    return array, pl.BlockSpec((array.shape[0], width), lambda *_: (0, part))


def call(kernel, scalars, arrays, outs, after=(), aliases=None):
    pairs = [item if isinstance(item, tuple) else (item, whole(item.shape)) for item in arrays]
    outs = [item if len(item) == 3 else (*item, whole(item[0])) for item in outs]
    count = len(scalars)

    def run(*refs):
        kernel(*refs[: count + len(pairs)], *refs[count + len(pairs) + len(after) :])

    return pl.pallas_call(
        run,
        grid=(1,),
        out_shape=[jax.ShapeDtypeStruct(shape, kind) for shape, kind, _ in outs],
        in_specs=[SMEM] * count + [spec for _, spec in pairs] + [ANY] * len(after),
        out_specs=[spec for _, _, spec in outs],
        input_output_aliases=aliases or {},
        cost_estimate=FREE,
        compiler_params=LIMIT,
        name=name_of(kernel),
    )(*scalars, *[array for array, _ in pairs], *after)


def column_call(kernel, at, ids, grads, others, span, outs, after=()):
    def run(*refs):
        kernel(*refs[: 2 + len(others)], *refs[2 + len(others) + len(after) :])

    return pl.pallas_call(
        run,
        out_shape=[jax.ShapeDtypeStruct(shape, kind) for shape, kind in outs],
        grid_spec=pltpu.PrefetchScalarGridSpec(
            num_scalar_prefetch=1,
            grid=(1,),
            in_specs=[pl.BlockSpec((Q, span), lambda i, ids_ref: (0, ids_ref[at]))]
            + [whole(other.shape) for other in others]
            + [ANY] * len(after),
            out_specs=[whole(shape) for shape, _ in outs],
        ),
        cost_estimate=FREE,
        compiler_params=LIMIT,
        name=name_of(kernel),
    )(ids, grads, *others, *after)


def dot(a, b, left, right):
    return lax.dot_general(a, b, (((left,), (right,)), ((), ())), preferred_element_type=F32)


def first_head(rows=Q):
    return lax.broadcasted_iota(jnp.int32, (rows, PAIR), 1) < P_SIZE


def spread(table, pair, first):
    return jnp.where(first, table[:, 2 * pair : 2 * pair + 1], table[:, 2 * pair + 1 : 2 * pair + 2])


def gains(skip_ref, head):
    first = lax.broadcasted_iota(jnp.int32, (1, PAIR), 1) < P_SIZE
    return jnp.where(first, skip_ref[head], skip_ref[head + 1])


def tables_kernel(
    rate_ref, resets_ref, x_ref, b_ref, step_ref, state_ref, left_ref, right_ref, weighted_ref, rows_ref, cols_ref, through_ref
):
    heads = step_ref.shape[0]
    keep = (1 - resets_ref[0, 0]).astype(F32)
    head_id = lax.broadcasted_iota(jnp.int32, (heads, Q), 0)
    lane = lax.broadcasted_iota(jnp.int32, (heads, Q), 1)
    rate = jnp.zeros((heads, Q), F32)
    for head in range(heads):
        rate = jnp.where(head_id == head, rate_ref[head], rate)
    log = -step_ref[...] * rate
    shift = 1
    while shift < Q:
        log = log + jnp.where(lane >= shift, pltpu.roll(log, shift, 1), 0.0)
        shift *= 2
    rows_ref[...] = log
    cols = log.T
    cols_ref[...] = cols
    first = first_head()
    for pair in range(heads // 2):
        at = slice(pair * PAIR, (pair + 1) * PAIR)
        log_pair = spread(cols, pair, first)
        last = log_pair[Q - 1 : Q, :]
        weighted_ref[:, at] = (x_ref[:, at].astype(F32) * jnp.exp(last - log_pair)).astype(BF)
        through_ref[:, at] = jnp.broadcast_to(keep * jnp.exp(last), (8, PAIR))
    state = dot(b_ref[...], weighted_ref[...], 0, 0)
    state_ref[...] = state
    middle = left_ref.shape[1]
    left_ref[...] = state[:, :middle].astype(BF)
    right_ref[...] = state[:, middle:].astype(BF)


def local_output_kernel(skip_ref, x_ref, b_ref, c_ref, rows_ref, cols_ref, out_ref):
    heads = rows_ref.shape[0]
    scores = dot(c_ref[...], b_ref[...], 1, 1)
    at_row = lax.broadcasted_iota(jnp.int32, (HALF, HALF), 0)
    at_lane = lax.broadcasted_iota(jnp.int32, (HALF, HALF), 1)
    causal = at_row >= at_lane
    first = first_head()
    zero = jnp.zeros((Q, PAIR), BF)
    for pair in range(heads // 2):
        at = slice(pair * PAIR, (pair + 1) * PAIR)
        x_pair = x_ref[:, at]
        skip = gains(skip_ref, 2 * pair) * x_pair.astype(F32)
        top, bottom = skip[:HALF], skip[HALF:]
        for side in range(2):
            head = 2 * pair + side
            x_head = jnp.where(first, x_pair, zero) if side == 0 else jnp.where(first, zero, x_pair)
            col = cols_ref[:, head : head + 1]
            row = rows_ref[head : head + 1, :]

            def mix(i, j):
                span = col[i * HALF : (i + 1) * HALF] - row[:, j * HALF : (j + 1) * HALF]
                weight = jnp.exp(jnp.minimum(span, 0.0))
                if i == j:
                    weight = jnp.where(causal, weight, 0.0)
                return (weight * scores[i * HALF : (i + 1) * HALF, j * HALF : (j + 1) * HALF]).astype(BF)

            top += dot(mix(0, 0), x_head[:HALF], 1, 0)
            bottom += dot(jnp.concatenate([mix(1, 0), mix(1, 1)], axis=1), x_head, 1, 0)
        out_ref[:HALF, at] = top
        out_ref[HALF:, at] = bottom


def output_kernel(offset, ids_ref, resets_ref, local_ref, c_ref, cols_ref, before_ref, even_ref, out_ref, state_ref):
    first = first_head()
    cols = cols_ref[...]
    keep = (1 - resets_ref[0, 0]).astype(F32)
    state = jnp.where(ids_ref[CORE] == 1, even_ref[...].astype(F32), before_ref[...].astype(F32))
    state_ref[...] = (keep * state).astype(BF)
    for pair in range(out_ref.shape[1] // PAIR):
        at = slice(pair * PAIR, (pair + 1) * PAIR)
        term = dot(c_ref[...], state_ref[:, at], 1, 0)
        out_ref[:, at] = (local_ref[:, at] + jnp.exp(spread(cols, offset + pair, first)) * term).astype(BF)


def block_of(ids_ref, grad_ref, slot):
    depth = grad_ref.shape[1] // 4
    return grad_ref[:, pl.ds(pl.multiple_of(ids_ref[slot] * depth, depth), depth)]


def send_kernel(ids_ref, grad_ref, mine_ref, other_ref):
    mine_ref[...] = block_of(ids_ref, grad_ref, PARITY)
    other_ref[...] = block_of(ids_ref, grad_ref, PARITY + 1)


def assemble_kernel(half, ids_ref, grad_ref, *refs):
    pieces, out_ref = refs[:-1], refs[-1]
    depth = out_ref.shape[1] // 2
    even = ids_ref[ODD] == 0
    for slot in range(2):
        columns = slice(slot * depth, (slot + 1) * depth)
        out_ref[:Q, columns] = block_of(ids_ref, grad_ref, 2 * half + slot)
        for number in range(len(pieces) // 2):
            near, far = pieces[2 * number], pieces[2 * number + 1]
            first, second = (near, far) if slot == 0 else (far, near)
            out_ref[(number + 1) * Q : (number + 2) * Q, columns] = jnp.where(even, first[...], second[...])


def combine_kernel(through_ref, state_ref, *refs):
    parts, out_ref = refs[:-1], refs[-1]
    width = out_ref.shape[1] // len(parts)
    for number, part in enumerate(parts):
        at = slice(number * width, (number + 1) * width)
        out_ref[:, at] = (through_ref[:1, at] * part[...].astype(F32) + state_ref[:, at]).astype(BF)


def head_partial_kernel(mine_ref, other_ref, *refs):
    weights, outs = refs[:4], refs[4:]
    depth = weights[0].shape[0]
    for number in reversed(range(len(outs))):
        rows = slice(number * Q, (number + 1) * Q)
        total = None
        for block, weight in enumerate(weights):
            half = mine_ref if block < 2 else other_ref
            term = dot(half[rows, (block % 2) * depth : (block % 2 + 1) * depth], weight[...], 1, 0)
            total = term if total is None else total + term
        outs[number][...] = total.astype(outs[number].dtype)


def adjoint_kernel(others, offset, resets_ref, own_ref, *refs):
    parts, (c_ref, cols_ref, head_ref, weighted_ref, adjoint_ref, sent_ref) = refs[:others], refs[others:]
    first = first_head()
    cols = cols_ref[...]
    keep = (1 - resets_ref[0, 0]).astype(F32)
    for pair in range(head_ref.shape[1] // PAIR):
        at = slice(pair * PAIR, (pair + 1) * PAIR)
        total = own_ref[:, at]
        for part in parts:
            total = total + part[:, at].astype(F32)
        head = total.astype(BF)
        head_ref[:, at] = head
        weighted_ref[:, at] = (head.astype(F32) * jnp.exp(spread(cols, offset + pair, first))).astype(BF)
    adjoint = keep * dot(c_ref[...], weighted_ref[...], 0, 0)
    adjoint_ref[...] = adjoint
    sent_ref[...] = adjoint.astype(BF)


def chip_total_kernel(ids_ref, own_ref, partner_ref, through_ref, partner_through_ref, *refs):
    entering, out_ref = refs[:-1], refs[-1]
    even = ids_ref[CORE] == 0
    own, partner = own_ref[...], partner_ref[...].astype(F32)
    mine, theirs = through_ref[:1], partner_through_ref[:1]
    total = jnp.where(even, mine * partner + own, theirs * own + partner)
    for value in entering:
        total += mine * theirs * value[...].astype(F32)
    out_ref[...] = total.astype(BF)


def local_grads_kernel(
    offset, skip_ref, x_ref, grad_ref, b_ref, c_ref, rows_ref, cols_ref, weighted_ref, state_ref, in_ref, paired_ref, c_out_ref
):
    heads = x_ref.shape[1] // P_SIZE
    scores = dot(b_ref[...], c_ref[...], 1, 1)
    at_row = lax.broadcasted_iota(jnp.int32, (HALF, HALF), 0)
    at_lane = lax.broadcasted_iota(jnp.int32, (HALF, HALF), 1)
    causal = at_lane >= at_row
    first = first_head()
    zero = jnp.zeros((Q, PAIR), BF)
    paired_ref[...] = jnp.zeros_like(paired_ref)
    for pair in range(heads // 2):
        at = slice(pair * PAIR, (pair + 1) * PAIR)
        x_pair = x_ref[:, at]
        g_pair = grad_ref[:, at]
        skip = gains(skip_ref, offset + 2 * pair) * g_pair.astype(F32)
        top, bottom = skip[:HALF], skip[HALF:]
        for side in range(2):
            head = offset + 2 * pair + side
            g_head = jnp.where(first, g_pair, zero) if side == 0 else jnp.where(first, zero, g_pair)
            col = cols_ref[:, head : head + 1]
            row = rows_ref[head : head + 1, :]

            def weigh(j, i):
                span = row[:, i * HALF : (i + 1) * HALF] - col[j * HALF : (j + 1) * HALF]
                weight = jnp.exp(jnp.minimum(span, 0.0))
                return jnp.where(causal, weight, 0.0) if i == j else weight

            early = jnp.concatenate([weigh(0, 0), weigh(0, 1)], axis=1)
            late = weigh(1, 1)
            top += dot((early * scores[:HALF]).astype(BF), g_head, 1, 0)
            bottom += dot((late * scores[HALF:, HALF:]).astype(BF), g_head[HALF:], 1, 0)
            paired_ref[:HALF, :] += early * dot(x_pair[:HALF], g_head, 1, 1)
            paired_ref[HALF:, HALF:] += late * dot(x_pair[HALF:], g_head[HALF:], 1, 1)
        in_ref[:HALF, at] = top
        in_ref[HALF:, at] = bottom
    c_out_ref[...] = dot(weighted_ref[...], state_ref[...], 1, 1)


def group_sums_kernel(parts, b_ref, c_ref, *refs):
    pairs, c_parts, (grad_b_ref, grad_c_ref) = refs[:parts], refs[parts : 2 * parts], refs[2 * parts :]
    paired = functools.reduce(jnp.add, [ref[...] for ref in pairs]).astype(BF)
    grad_b_ref[...] = dot(paired, c_ref[...], 1, 0)
    grad_c_ref[...] = functools.reduce(jnp.add, [ref[...] for ref in c_parts], dot(paired, b_ref[...], 0, 0))


def final_kernel(
    offset, ids_ref, b_ref, cols_ref, sums_ref, local_ref, weighted_ref, through_ref, after_ref, partner_ref, *refs
):
    in_ref, grad_b_ref = refs[-2:]
    first = first_head()
    cols = cols_ref[...]
    entering = after_ref[...].astype(F32)
    inner = through_ref[:1] * entering + partner_ref[...].astype(F32)
    adjoint = jnp.where(ids_ref[CORE] == 1, entering, inner).astype(BF)
    grad_b_ref[...] = sums_ref[...] + dot(weighted_ref[...], adjoint, 1, 1)
    for number in range(local_ref.shape[1] // PAIR):
        at = slice(number * PAIR, (number + 1) * PAIR)
        log_pair = spread(cols, offset + number, first)
        to_end = jnp.exp(log_pair[Q - 1 : Q, :] - log_pair)
        term = dot(b_ref[...], adjoint[:, at], 1, 0)
        in_ref[:, at] = (local_ref[:, at] + to_end * term).astype(BF)


def add_kernel(kept_ref, came_ref, sum_ref, token_ref):
    sum_ref[...] = kept_ref[...] + came_ref[...].astype(F32)
    token_ref[...] = jnp.zeros_like(token_ref)


def weight_partial_kernel(count, mine_ref, other_ref, *refs):
    outputs, (sent_ref, kept_ref) = refs[:count], refs[count:]
    depth = sent_ref.shape[0]
    for slot, target in ((1, sent_ref), (0, kept_ref)):
        columns = slice(slot * depth, (slot + 1) * depth)
        total = None
        for number, output in enumerate(outputs):
            half = mine_ref if number < count // 2 else other_ref
            rows = slice(number % (count // 2) * Q, (number % (count // 2) + 1) * Q)
            term = dot(half[rows, columns], output[...], 0, 0)
            total = term if total is None else total + term
        target[...] = total.astype(target.dtype)


def body(
    ssm_input, b_input, c_input, step_size, decay_rate, skip_gain, resets, out_grad, out_weight
):
    seq, dp, planes = lax.axis_size("seq"), lax.axis_size("dp"), lax.axis_size("tensor")
    chips = seq // 2
    me = lax.axis_index(("seq", "tensor", "dp"))
    heads = decay_rate.shape[0]
    wide = heads * P_SIZE
    width = wide // CHUNKS
    chunk_heads = heads // CHUNKS
    depth = out_weight.shape[0]
    span = 4 * depth
    assert ssm_input.shape[1] == Q and dp == 2 and seq % 2 == 0 and planes % 2 == 0
    def later(value, other):
        return lax.optimization_barrier((value, other))[0]

    across = [(i, i ^ 1) for i in range(seq)]

    def core_swap(value):
        return lax.ppermute(value, "seq", across)

    def chip_shift(value, by):
        return lax.ppermute(value, "seq", [(i, (i + 2 * by) % seq) for i in range(seq)])

    def plane_swap(value):
        return lax.ppermute(value, "tensor", [(i, i ^ 1) for i in range(planes)])

    def dialogue_swap(value):
        return lax.ppermute(value, "dp", [(0, 1), (1, 0)])

    x, b_rows, c_rows, steps, incoming = (
        ssm_input[0], b_input[0], c_input[0], step_size[0], out_grad[0]
    )
    table = []
    for at in range(seq * planes * dp):
        chip, core, odd, dialogue = at // (2 * planes * dp), at // (planes * dp) % 2, at // dp % 2, at % dp
        order = [core * 2 + dialogue, core * 2 + 1 - dialogue, (1 - core) * 2 + dialogue, (1 - core) * 2 + 1 - dialogue]
        table.append(order + [order[odd], order[2 + odd], core, odd] + [(chip + by) % chips for by in range(chips)])
    ids = lax.dynamic_index_in_dim(np.array(table, np.int32), me, keepdims=False)
    part_of = lambda array, part: columns_of(array, width, part)

    weight_other = dialogue_swap(out_weight)
    weights = [out_weight, weight_other, core_swap(out_weight)]

    to_send = [
        column_call(send_kernel, CHIP + by, ids, incoming, [], span, [((Q, depth), BF)] * 2)
        for by in range(1, chips)
    ]

    def exchange(pieces, other=None):
        got = []
        for by in range(1, chips):
            near = chip_shift(pieces[by - 1], by)
            got += [near, plane_swap(near if other is None else later(near, other))]
        return got

    state, left, right, weighted_in, log_rows, log_cols, through = call(
        tables_kernel,
        (decay_rate, resets),
        (x, b_rows, steps),
        [((N, wide), F32), ((N, wide // 2), BF), ((N, wide // 2), BF), ((Q, wide), BF)]
        + [((heads, Q), F32), ((Q, heads), F32), ((8, wide), F32)],
        after=[pieces[1] for pieces in to_send],
    )
    local_output, = call(
        local_output_kernel,
        (skip_gain,),
        (x, b_rows, c_rows, log_rows, log_cols),
        [((Q, wide), F32)],
    )
    other_pieces = exchange([pieces[1] for pieces in to_send], local_output)
    even = [core_swap(left), core_swap(right)]
    through_partner = core_swap(through)
    before = jnp.zeros((N, wide), BF)
    late = [pieces[0] for pieces in to_send]
    for hop in range(1, chips):
        total, = call(
            combine_kernel, (), (through, state, *even), [((N, wide), BF)],
            after=other_pieces[::2] if hop == 1 else (),
        )
        if hop == 1:
            total, late = lax.optimization_barrier((total, late))
        before = lax.ppermute(total, "seq", [(2 * i + 1, 2 * i + 2) for i in range(chips - 1)])
        leaving, = call(combine_kernel, (), (through, state, before), [((N, wide), BF)], after=[through_partner])
        even = [core_swap(leaving)]
    mine_pieces = exchange(late)
    outputs, states = [], []
    for part in range(CHUNKS):
        output, state_in = call(
            functools.partial(output_kernel, part * chunk_heads // 2),
            (ids, resets),
            (part_of(local_output, part), c_rows, log_cols, part_of(before, part), part_of(even[0], part)),
            [((Q, width), BF), ((N, width), BF)],
            after=[weights[2], weight_other, *mine_pieces[::2], *other_pieces] if part == 0 else [outputs[0][0]],
        )
        states.append(state_in)
        outputs.append([output] + [chip_shift(output, by) for by in range(1, chips)])

    half = [((chips * Q, span // 2), BF)]
    other, = column_call(functools.partial(assemble_kernel, 1), CHIP, ids, incoming, other_pieces, span, half)
    partner = core_swap(other)
    mine, = column_call(
        functools.partial(assemble_kernel, 0), CHIP, ids, incoming, mine_pieces, span, half,
        after=[partner, outputs[-1][0], *outputs[0][1:]],
    )
    weights.append(core_swap(later(weight_other, outputs[-1][0])))

    partials, returned = [], []
    for part in range(CHUNKS):
        partials.append(
            call(
                head_partial_kernel,
                (),
                (mine, other, *[part_of(weight, part) for weight in weights]),
                [((Q, width), F32)] + [((Q, width), BF)] * (chips - 1),
                after=[partial[0] for partial in partials],
            )
        )
        returned.append([chip_shift(partials[part][by], -by) for by in range(1, chips)])

    grad_weight, tokens = None, []
    for part in range(CHUNKS):
        pieces = outputs[part] + [core_swap(outputs[part][0])]
        pieces += [core_swap(later(piece, partials[-1][0])) for piece in outputs[part][1:]]
        sent, kept = call(
            functools.partial(weight_partial_kernel, 2 * chips),
            (),
            (mine, partner, *pieces),
            [((depth, width), BF), ((depth, width), F32)],
            after=[partial[0] for partial in partials],
        )
        grad_weight, token = call(
            add_kernel,
            (),
            (kept, dialogue_swap(sent)),
            [
                ((depth, wide), F32, pl.BlockSpec((depth, width), lambda *_, part=part: (0, part))),
                ((8, 128), F32),
            ],
            after=() if part == 0 else (grad_weight,),
            aliases=None if part == 0 else {2: 0},
        )
        tokens.append(token)

    locals_, pairs, c_parts, after, odd, totals = [], [], [], [], [], []
    for part in range(CHUNKS):
        head_grad, weighted_grad, adjoint, adjoint_sent = call(
            functools.partial(adjoint_kernel, chips - 1, part * chunk_heads // 2),
            (resets,),
            (partials[part][0], *returned[part], c_rows, log_cols),
            [((Q, width), BF), ((Q, width), BF), ((N, width), F32), ((N, width), BF)],
            after=[through_partner, *locals_, *totals],
        )
        adjoint_partner = core_swap(adjoint_sent)
        entering = []
        for hop in range(1, chips):
            total, = call(
                chip_total_kernel,
                (ids,),
                (adjoint, adjoint_partner, part_of(through, part), part_of(through_partner, part), *entering),
                [((N, width), BF)],
            )
            totals.append(total)
            entering = [lax.ppermute(total, "seq", [(i, i - 2) for i in range(2, seq)])]
        after += entering
        odd.append(adjoint_partner)
        local_in, paired, c_part = call(
            functools.partial(local_grads_kernel, part * chunk_heads),
            (skip_gain,),
            (part_of(x, part), head_grad, b_rows, c_rows, log_rows, log_cols, weighted_grad, states[part]),
            [((Q, width), F32), ((Q, Q), F32), ((Q, N), F32)],
        )
        locals_.append(local_in)
        pairs.append(paired)
        c_parts.append(c_part)
    grad_b, grad_c = call(
        functools.partial(group_sums_kernel, CHUNKS),
        (),
        (b_rows, c_rows, *pairs, *c_parts),
        [((Q, N), F32), ((Q, N), F32)],
        after=tokens[:-1],
    )
    grad_in = None
    for part in range(CHUNKS):
        grad_in, grad_b = call(
            functools.partial(final_kernel, part * chunk_heads // 2),
            (ids,),
            (
                b_rows, log_cols, grad_b, locals_[part], part_of(weighted_in, part), part_of(through_partner, part),
                after[part], odd[part],
            ),
            [
                ((Q, wide), BF, pl.BlockSpec((Q, width), lambda *_, part=part: (0, part))),
                ((Q, N), F32),
            ],
            after=() if part == 0 else (grad_in,),
            aliases=None if part == 0 else {9: 0},
        )
    return grad_in[None], grad_b[None], grad_c[None], grad_weight


def solution(mesh):
    in_specs = (
        P("dp", "seq", "tensor"),
        P("dp", "seq", "tensor"),
        P("dp", "seq", "tensor"),
        P("dp", "tensor", "seq"),
        P("tensor"),
        P("tensor"),
        P("dp", "seq"),
        P("dp", "seq", None),
        P(("seq", "dp"), "tensor"),
    )
    out_specs = (
        P("dp", "seq", "tensor"),
        P("dp", "seq", "tensor"),
        P("dp", "seq", "tensor"),
        P(("seq", "dp"), "tensor"),
    )
    return jax.shard_map(body, mesh=mesh, in_specs=in_specs, out_specs=out_specs, check_vma=False)
```

```python
import functools

import jax
import jax.numpy as jnp
import numpy as np
from jax import lax
from jax.experimental import pallas as pl
from jax.experimental.pallas import tpu as pltpu
from jax.sharding import PartitionSpec as P

P_SIZE = 64
N = 128
Q = 256
HALF = 128
PAIR = 2 * P_SIZE
SHARES = (6, 10)
CUTS = 1
BACK = 1
PARITY, CORE, ODD, CHIP = 4, 6, 7, 8
BF = jnp.bfloat16
F32 = jnp.float32

SMEM = pl.BlockSpec(memory_space=pltpu.SMEM)
ANY = pl.BlockSpec(memory_space=pl.ANY)
FREE = pl.CostEstimate(flops=0, bytes_accessed=0, transcendentals=0)
LIMIT = pltpu.CompilerParams(vmem_limit_bytes=16 * 2**20)


def name_of(kernel):
    return getattr(kernel, "func", kernel).__name__


def whole(shape):
    return pl.BlockSpec(shape, lambda *_: (0,) * len(shape))


def columns_of(array, width, part):
    return array, pl.BlockSpec((array.shape[0], width), lambda *_: (0, part))


def call(kernel, scalars, arrays, outs, after=(), aliases=None):
    pairs = [item if isinstance(item, tuple) else (item, whole(item.shape)) for item in arrays]
    outs = [item if len(item) == 3 else (*item, whole(item[0])) for item in outs]
    count = len(scalars)

    def run(*refs):
        kernel(*refs[: count + len(pairs)], *refs[count + len(pairs) + len(after) :])

    return pl.pallas_call(
        run,
        grid=(1,),
        out_shape=[jax.ShapeDtypeStruct(shape, kind) for shape, kind, _ in outs],
        in_specs=[SMEM] * count + [spec for _, spec in pairs] + [ANY] * len(after),
        out_specs=[spec for _, _, spec in outs],
        input_output_aliases=aliases or {},
        cost_estimate=FREE,
        compiler_params=LIMIT,
        name=name_of(kernel),
    )(*scalars, *[array for array, _ in pairs], *after)


def column_call(kernel, at, ids, grads, others, span, outs, after=()):
    def run(*refs):
        kernel(*refs[: 2 + len(others)], *refs[2 + len(others) + len(after) :])

    return pl.pallas_call(
        run,
        out_shape=[jax.ShapeDtypeStruct(shape, kind) for shape, kind in outs],
        grid_spec=pltpu.PrefetchScalarGridSpec(
            num_scalar_prefetch=1,
            grid=(1,),
            in_specs=[pl.BlockSpec((Q, span), lambda i, ids_ref: (0, ids_ref[at]))]
            + [whole(other.shape) for other in others]
            + [ANY] * len(after),
            out_specs=[whole(shape) for shape, _ in outs],
        ),
        cost_estimate=FREE,
        compiler_params=LIMIT,
        name=name_of(kernel),
    )(ids, grads, *others, *after)


def dot(a, b, left, right):
    return lax.dot_general(a, b, (((left,), (right,)), ((), ())), preferred_element_type=F32)


def first_head(rows=Q):
    return lax.broadcasted_iota(jnp.int32, (rows, PAIR), 1) < P_SIZE


def spread(table, pair, first):
    return jnp.where(first, table[:, 2 * pair : 2 * pair + 1], table[:, 2 * pair + 1 : 2 * pair + 2])


def gains(skip_ref, head):
    first = lax.broadcasted_iota(jnp.int32, (1, PAIR), 1) < P_SIZE
    return jnp.where(first, skip_ref[head], skip_ref[head + 1])


def tables_kernel(
    rate_ref, resets_ref, x_ref, b_ref, step_ref, *refs
):
    states, sent, (weighted_ref, rows_ref, cols_ref, through_ref) = refs[:2], refs[2:4], refs[4:]
    heads = step_ref.shape[0]
    keep = (1 - resets_ref[0, 0]).astype(F32)
    head_id = lax.broadcasted_iota(jnp.int32, (heads, Q), 0)
    lane = lax.broadcasted_iota(jnp.int32, (heads, Q), 1)
    rate = jnp.zeros((heads, Q), F32)
    for head in range(heads):
        rate = jnp.where(head_id == head, rate_ref[head], rate)
    log = -step_ref[...] * rate
    shift = 1
    while shift < Q:
        log = log + jnp.where(lane >= shift, pltpu.roll(log, shift, 1), 0.0)
        shift *= 2
    rows_ref[...] = log
    cols = log.T
    cols_ref[...] = cols
    first = first_head()
    for pair in range(heads // 2):
        at = slice(pair * PAIR, (pair + 1) * PAIR)
        log_pair = spread(cols, pair, first)
        last = log_pair[Q - 1 : Q, :]
        weighted_ref[:, at] = (x_ref[:, at].astype(F32) * jnp.exp(last - log_pair)).astype(BF)
        through_ref[:, at] = jnp.broadcast_to(keep * jnp.exp(last), (8, PAIR))
    state = dot(b_ref[...], weighted_ref[...], 0, 0)
    middle = state.shape[1] // 2
    for number in range(2):
        half = state[:, number * middle : (number + 1) * middle]
        states[number][...] = half
        sent[number][...] = half.astype(BF)


def local_output_kernel(skip_ref, x_ref, b_ref, c_ref, rows_ref, cols_ref, out_ref):
    heads = rows_ref.shape[0]
    scores = dot(c_ref[...], b_ref[...], 1, 1)
    at_row = lax.broadcasted_iota(jnp.int32, (HALF, HALF), 0)
    at_lane = lax.broadcasted_iota(jnp.int32, (HALF, HALF), 1)
    causal = at_row >= at_lane
    first = first_head()
    zero = jnp.zeros((Q, PAIR), BF)
    for pair in range(heads // 2):
        at = slice(pair * PAIR, (pair + 1) * PAIR)
        x_pair = x_ref[:, at]
        skip = gains(skip_ref, 2 * pair) * x_pair.astype(F32)
        top, bottom = skip[:HALF], skip[HALF:]
        for side in range(2):
            head = 2 * pair + side
            x_head = jnp.where(first, x_pair, zero) if side == 0 else jnp.where(first, zero, x_pair)
            col = cols_ref[:, head : head + 1]
            row = rows_ref[head : head + 1, :]

            def mix(i, j):
                span = col[i * HALF : (i + 1) * HALF] - row[:, j * HALF : (j + 1) * HALF]
                weight = jnp.exp(jnp.minimum(span, 0.0))
                if i == j:
                    weight = jnp.where(causal, weight, 0.0)
                return (weight * scores[i * HALF : (i + 1) * HALF, j * HALF : (j + 1) * HALF]).astype(BF)

            top += dot(mix(0, 0), x_head[:HALF], 1, 0)
            bottom += dot(jnp.concatenate([mix(1, 0), mix(1, 1)], axis=1), x_head, 1, 0)
        out_ref[:HALF, at] = top
        out_ref[HALF:, at] = bottom


def output_kernel(
    start, ids_ref, resets_ref, local_ref, c_ref, cols_ref, through_ref, before_ref, left_ref, right_ref, out_ref, state_ref
):
    first = first_head()
    cols = cols_ref[...]
    keep = (1 - resets_ref[0, 0]).astype(F32)
    part = slice(start, start + out_ref.shape[1])
    partner = jnp.concatenate([left_ref[...], right_ref[...]], axis=1)[:, part].astype(F32)
    before = before_ref[:, part].astype(F32)
    state = jnp.where(ids_ref[CORE] == 1, through_ref[:1, part] * before + partner, before)
    state_ref[...] = (keep * state).astype(BF)
    for pair in range(out_ref.shape[1] // PAIR):
        at = slice(pair * PAIR, (pair + 1) * PAIR)
        whole = slice(start + pair * PAIR, start + (pair + 1) * PAIR)
        term = dot(c_ref[...], state_ref[:, at], 1, 0)
        decay = jnp.exp(spread(cols, start // PAIR + pair, first))
        out_ref[:, at] = (local_ref[:, whole] + decay * term).astype(BF)


def block_of(ids_ref, grad_ref, slot):
    depth = grad_ref.shape[1] // 4
    return grad_ref[:, pl.ds(pl.multiple_of(ids_ref[slot] * depth, depth), depth)]


def send_kernel(ids_ref, grad_ref, out_ref):
    depth = out_ref.shape[1] // 2
    for half in range(2):
        out_ref[:, half * depth : (half + 1) * depth] = block_of(ids_ref, grad_ref, PARITY + half)


def own_kernel(ids_ref, grad_ref, *halves):
    depth = halves[0].shape[1] // 2
    for slot in range(4):
        halves[slot // 2][:, slot % 2 * depth : (slot % 2 + 1) * depth] = block_of(ids_ref, grad_ref, slot)


def assemble_kernel(ids_ref, *refs):
    pieces, blocks = refs[:-4], refs[-4:]
    depth = blocks[0].shape[1]
    even = ids_ref[ODD] == 0
    for number, out_ref in enumerate(blocks):
        taken = slice(number // 2 * depth, (number // 2 + 1) * depth)
        for other in range(len(pieces) // 2):
            near, far = pieces[2 * other], pieces[2 * other + 1]
            first, second = (near, far) if number % 2 == 0 else (far, near)
            rows = slice(other * Q, (other + 1) * Q)
            out_ref[rows, :] = jnp.where(even, first[:, taken], second[:, taken])


def head_partial_kernel(cuts, mine_ref, other_ref, *refs):
    came, weights, outs = refs[:4], refs[4:9], refs[9:]
    depth = weights[0].shape[0]
    middle = weights[3].shape[0]
    for number in reversed(range(1 + (len(outs) - 1) // cuts)):
        total = None
        for block in range(4):
            rows = slice((number - 1) * Q, number * Q)
            if number == 0:
                grad = (mine_ref, other_ref)[block // 2][:, block % 2 * depth : (block % 2 + 1) * depth]
            else:
                grad = came[block][rows, :]
            if block < 3:
                term = dot(grad, weights[block][...], 1, 0)
            else:
                term = dot(grad[:, :middle], weights[3][...], 1, 0) + dot(grad[:, middle:], weights[4][...], 1, 0)
            total = term if total is None else total + term
        if number == 0:
            outs[0][...] = total
            continue
        width = total.shape[1] // cuts
        for cut in range(cuts):
            part = total[:, cut * width : (cut + 1) * width]
            outs[1 + (number - 1) * cuts + cut][...] = part.astype(BF)


def adjoint_kernel(others, cuts, offset, resets_ref, own_ref, *refs):
    parts, (c_ref, cols_ref, head_ref, weighted_ref, adjoint_ref, sent_ref) = refs[: others * cuts], refs[others * cuts :]
    first = first_head()
    cols = cols_ref[...]
    width = own_ref.shape[1] // cuts
    keep = (1 - resets_ref[0, 0]).astype(F32)
    for pair in range(head_ref.shape[1] // PAIR):
        at = slice(pair * PAIR, (pair + 1) * PAIR)
        total = own_ref[:, at]
        cut, place = pair * PAIR // width, pair * PAIR % width
        for other in range(others):
            total = total + parts[other * cuts + cut][:, place : place + PAIR].astype(F32)
        head = total.astype(BF)
        head_ref[:, at] = head
        weighted_ref[:, at] = (head.astype(F32) * jnp.exp(spread(cols, offset + pair, first))).astype(BF)
    adjoint = keep * dot(c_ref[...], weighted_ref[...], 0, 0)
    adjoint_ref[...] = adjoint
    sent_ref[...] = adjoint.astype(BF)


def chip_total_kernel(last, parts, ids_ref, through_ref, partner_through_ref, *refs):
    owns, partners, entering, out_ref = refs[:parts], refs[parts : 2 * parts], refs[2 * parts : -1], refs[-1]
    leaves = ids_ref[CORE] == last
    width = owns[0].shape[1]
    for part in range(parts):
        at = slice(part * width, (part + 1) * width)
        own, partner = owns[part][...], partners[part][...].astype(F32)
        mine, theirs = through_ref[:1, at], partner_through_ref[:1, at]
        total = jnp.where(leaves, mine * partner + own, theirs * own + partner)
        for value in entering:
            total += mine * theirs * value[:, at].astype(F32)
        out_ref[:, at] = total.astype(BF)


def local_grads_kernel(
    offset, skip_ref, x_ref, grad_ref, b_ref, c_ref, rows_ref, cols_ref, weighted_ref, *refs
):
    states, (in_ref, paired_ref, c_out_ref) = refs[:-3], refs[-3:]
    heads = x_ref.shape[1] // P_SIZE
    scores = dot(b_ref[...], c_ref[...], 1, 1)
    at_row = lax.broadcasted_iota(jnp.int32, (HALF, HALF), 0)
    at_lane = lax.broadcasted_iota(jnp.int32, (HALF, HALF), 1)
    causal = at_lane >= at_row
    first = first_head()
    zero = jnp.zeros((Q, PAIR), BF)
    paired_ref[...] = jnp.zeros_like(paired_ref)
    for pair in range(heads // 2):
        at = slice(pair * PAIR, (pair + 1) * PAIR)
        x_pair = x_ref[:, at]
        g_pair = grad_ref[:, at]
        skip = gains(skip_ref, offset + 2 * pair) * g_pair.astype(F32)
        top, bottom = skip[:HALF], skip[HALF:]
        for side in range(2):
            head = offset + 2 * pair + side
            g_head = jnp.where(first, g_pair, zero) if side == 0 else jnp.where(first, zero, g_pair)
            col = cols_ref[:, head : head + 1]
            row = rows_ref[head : head + 1, :]

            def weigh(j, i):
                span = row[:, i * HALF : (i + 1) * HALF] - col[j * HALF : (j + 1) * HALF]
                weight = jnp.exp(jnp.minimum(span, 0.0))
                return jnp.where(causal, weight, 0.0) if i == j else weight

            early = jnp.concatenate([weigh(0, 0), weigh(0, 1)], axis=1)
            late = weigh(1, 1)
            top += dot((early * scores[:HALF]).astype(BF), g_head, 1, 0)
            bottom += dot((late * scores[HALF:, HALF:]).astype(BF), g_head[HALF:], 1, 0)
            paired_ref[:HALF, :] += early * dot(x_pair[:HALF], g_head, 1, 1)
            paired_ref[HALF:, HALF:] += late * dot(x_pair[HALF:], g_head[HALF:], 1, 1)
        in_ref[:HALF, at] = top
        in_ref[HALF:, at] = bottom
    start, total = 0, None
    for state in states:
        width = state.shape[1]
        term = dot(weighted_ref[:, start : start + width], state[...], 1, 1)
        total = term if total is None else total + term
        start += width
    c_out_ref[...] = total


def group_sums_kernel(parts, b_ref, c_ref, *refs):
    pairs, c_parts, (grad_b_ref, grad_c_ref) = refs[:parts], refs[parts : 2 * parts], refs[2 * parts :]
    paired = functools.reduce(jnp.add, [ref[...] for ref in pairs]).astype(BF)
    grad_b_ref[...] = dot(paired, c_ref[...], 1, 0)
    grad_c_ref[...] = functools.reduce(jnp.add, [ref[...] for ref in c_parts], dot(paired, b_ref[...], 0, 0))


def final_kernel(parts, ids_ref, b_ref, cols_ref, sums_ref, weighted_ref, through_ref, after_ref, *refs):
    locals_, partners, (in_ref, grad_b_ref) = refs[:parts], refs[parts : 2 * parts], refs[2 * parts :]
    first = first_head()
    cols = cols_ref[...]
    grad_b = sums_ref[...]
    width = locals_[0].shape[1]
    for part in range(parts):
        here = slice(part * width, (part + 1) * width)
        entering = after_ref[:, here].astype(F32)
        inner = through_ref[:1, here] * entering + partners[part][...].astype(F32)
        adjoint = jnp.where(ids_ref[CORE] == 1, entering, inner).astype(BF)
        grad_b += dot(weighted_ref[:, here], adjoint, 1, 1)
        for number in range(width // PAIR):
            at = slice(number * PAIR, (number + 1) * PAIR)
            pair = part * (width // PAIR) + number
            log_pair = spread(cols, pair, first)
            to_end = jnp.exp(log_pair[Q - 1 : Q, :] - log_pair)
            term = dot(b_ref[...], adjoint[:, at], 1, 0)
            in_ref[:, pair * PAIR : (pair + 1) * PAIR] = (locals_[part][:, at] + to_end * term).astype(BF)
    grad_b_ref[...] = grad_b


def add_kernel(parts, *refs):
    start = 0
    for kept, came in zip(refs[:parts], refs[parts:-1]):
        width = kept.shape[1]
        refs[-1][:, start : start + width] = kept[...] + came[...].astype(F32)
        start += width


def weight_partial_kernel(chips, *refs):
    owns, came, refs = refs[:2], (refs[2:4], refs[4:6]), refs[6:]
    outputs, (sent_ref, kept_ref) = refs[: 2 * chips], refs[2 * chips :]
    depth = sent_ref.shape[0]
    for slot, target in ((1, sent_ref), (0, kept_ref)):
        total = None
        for number, output in enumerate(outputs):
            core, by = number // chips, number % chips
            if by == 0:
                grad = owns[core][:, slot * depth : (slot + 1) * depth]
            else:
                grad = came[core][slot][(by - 1) * Q : by * Q, :]
            term = dot(grad, output[...], 0, 0)
            total = term if total is None else total + term
        target[...] = total.astype(target.dtype)


def body(
    ssm_input, b_input, c_input, step_size, decay_rate, skip_gain, resets, out_grad, out_weight
):
    seq, dp, planes = lax.axis_size("seq"), lax.axis_size("dp"), lax.axis_size("tensor")
    chips = seq // 2
    me = lax.axis_index(("seq", "tensor", "dp"))
    heads = decay_rate.shape[0]
    wide = heads * P_SIZE
    widths = [wide * share // sum(SHARES) // PAIR * PAIR for share in SHARES]
    starts = [sum(widths[:part]) for part in range(len(widths))]
    depth = out_weight.shape[0]
    span = 4 * depth
    assert ssm_input.shape[1] == Q and dp == 2 and seq % 2 == 0 and seq > 2 and planes % 2 == 0
    def later(value, other):
        return lax.optimization_barrier((value, other))[0]

    across = [(i, i ^ 1) for i in range(seq)]

    def core_swap(value):
        return lax.ppermute(value, "seq", across)

    def chip_shift(value, by):
        return lax.ppermute(value, "seq", [(i, (i + 2 * by) % seq) for i in range(seq)])

    def plane_swap(value):
        return lax.ppermute(value, "tensor", [(i, i ^ 1) for i in range(planes)])

    def dialogue_swap(value):
        return lax.ppermute(value, "dp", [(0, 1), (1, 0)])

    x, b_rows, c_rows, steps, incoming = (
        ssm_input[0], b_input[0], c_input[0], step_size[0], out_grad[0]
    )
    table = []
    for at in range(seq * planes * dp):
        chip, core, odd, dialogue = at // (2 * planes * dp), at // (planes * dp) % 2, at // dp % 2, at % dp
        order = [core * 2 + dialogue, core * 2 + 1 - dialogue, (1 - core) * 2 + dialogue, (1 - core) * 2 + 1 - dialogue]
        table.append(order + [order[odd], order[2 + odd], core, odd] + [(chip + by) % chips for by in range(chips)])
    ids = lax.dynamic_index_in_dim(np.array(table, np.int32), me, keepdims=False)
    back_width, back_heads = wide // BACK, heads // BACK
    back_of = lambda array, part: columns_of(array, back_width, part)

    to_send = [
        column_call(send_kernel, CHIP + by, ids, incoming, [], span, [((Q, 2 * depth), BF)])
        for by in range(1, chips)
    ]

    weight_other = dialogue_swap(out_weight)
    weight_core = core_swap(out_weight)

    near = [chip_shift(to_send[by - 1][0], by) for by in range(1, chips)]
    pieces = []
    for piece in near:
        pieces += [piece, plane_swap(piece)]

    *both, weighted_in, log_rows, log_cols, through = call(
        tables_kernel,
        (decay_rate, resets),
        (x, b_rows, steps),
        [((N, wide // 2), F32)] * 2 + [((N, wide // 2), BF)] * 2 + [((Q, wide), BF)]
        + [((heads, Q), F32), ((Q, heads), F32), ((8, wide), F32)],
        after=[weight_core, *[sent[0] for sent in to_send]],
    )
    local_output, = call(
        local_output_kernel,
        (skip_gain,),
        (x, b_rows, c_rows, log_rows, log_cols),
        [((Q, wide), F32)],
    )
    state_partner = [core_swap(half) for half in both[2:]]
    through_partner = core_swap(through)
    mine, other = column_call(
        own_kernel, CHIP, ids, incoming, [], span, [((Q, span // 2), BF)] * 2, after=[through]
    )
    partner = core_swap(other)
    before = []
    for hop in range(1, chips):
        total, = call(
            functools.partial(chip_total_kernel, 1, 2),
            (ids,),
            (through, through_partner, *both[:2], *state_partner, *before),
            [((N, wide), BF)],
            after=[local_output] if hop == 1 else (),
        )
        before = [lax.ppermute(total, "seq", [(i, i + 2) for i in range(seq - 2)])]
    outputs, swapped, states = [], [], []
    for start, width in zip(starts, widths):
        output, state_in = call(
            functools.partial(output_kernel, start),
            (ids, resets),
            (local_output, c_rows, log_cols, through_partner, *before, *state_partner),
            [((Q, width), BF), ((N, width), BF)],
            after=outputs[-1][:1] if outputs else [partner],
        )
        states.append(state_in)
        outputs.append([output] + [chip_shift(output, by) for by in range(1, chips)])
        swapped.append(core_swap(output))

    came = call(
        assemble_kernel, (ids,), pieces, [(((chips - 1) * Q, depth), BF)] * 4, after=[outputs[-1][0]],
    )
    partner_came = [core_swap(block) for block in came[2:]]
    weight_late = later(weight_other, outputs[-1][0])
    weights = [out_weight, weight_other, weight_core]
    weights += [core_swap(weight_late[: depth // 2]), core_swap(weight_late[depth // 2 :])]

    partials, returned = [], []
    for part in range(BACK):
        partials.append(
            call(
                functools.partial(head_partial_kernel, CUTS),
                (),
                (mine, other, *came, *[back_of(weight, part) for weight in weights]),
                [((Q, back_width), F32)] + [((Q, back_width // CUTS), BF)] * (CUTS * (chips - 1)),
                after=[] if part == 0 else [partials[-1][0]],
            )
        )
        returned.append(
            [chip_shift(partials[part][1 + i], -(1 + i // CUTS)) for i in range(CUTS * (chips - 1))]
        )

    sent, kept = [], []
    for part, width in enumerate(widths):
        pieces = [later(piece, sent[-1]) if sent else piece for piece in outputs[part][1:]]
        own, partial = call(
            functools.partial(weight_partial_kernel, chips),
            (),
            (mine, partner, *came[:2], *partner_came, *outputs[part], swapped[part], *map(core_swap, pieces)),
            [((depth, width), BF), ((depth, width), F32)],
            after=[partial[0] for partial in partials] + sent[-1:],
        )
        sent.append(own)
        kept.append(partial)
    sums = [dialogue_swap(value) for value in sent]
    grad_weight, = call(
        functools.partial(add_kernel, len(widths)),
        (),
        (*kept, *sums),
        [((depth, wide), F32)],
    )

    locals_, pairs, c_parts, adjoints, partners = [], [], [], [], []
    for part in range(BACK):
        head_grad, weighted_grad, adjoint, adjoint_sent = call(
            functools.partial(adjoint_kernel, chips - 1, CUTS, part * back_heads // 2),
            (resets,),
            (partials[part][0], *returned[part], c_rows, log_cols),
            [((Q, back_width), BF), ((Q, back_width), BF), ((N, back_width), F32), ((N, back_width), BF)],
            after=[sums[0], *sent, *locals_],
        )
        adjoints.append(adjoint)
        partners.append(core_swap(adjoint_sent))
        local_in, paired, c_part = call(
            functools.partial(local_grads_kernel, part * back_heads),
            (skip_gain,),
            (back_of(x, part), head_grad, b_rows, c_rows, log_rows, log_cols, weighted_grad)
            + tuple(states),
            [((Q, back_width), F32), ((Q, Q), F32), ((Q, N), F32)],
        )
        locals_.append(local_in)
        pairs.append(paired)
        c_parts.append(c_part)
    entering = []
    for hop in range(1, chips):
        total, = call(
            functools.partial(chip_total_kernel, 0, BACK),
            (ids,),
            (through, through_partner, *adjoints, *partners, *entering),
            [((N, wide), BF)],
        )
        entering = [lax.ppermute(total, "seq", [(i, i - 2) for i in range(2, seq)])]
    grad_b, grad_c = call(
        functools.partial(group_sums_kernel, BACK),
        (),
        (b_rows, c_rows, *pairs, *c_parts),
        [((Q, N), F32), ((Q, N), F32)],
    )
    grad_in, grad_b = call(
        functools.partial(final_kernel, BACK),
        (ids,),
        (b_rows, log_cols, grad_b, weighted_in, through_partner, *entering, *locals_, *partners),
        [((Q, wide), BF), ((Q, N), F32)],
    )
    return grad_in[None], grad_b[None], grad_c[None], grad_weight


def solution(mesh):
    in_specs = (
        P("dp", "seq", "tensor"),
        P("dp", "seq", "tensor"),
        P("dp", "seq", "tensor"),
        P("dp", "tensor", "seq"),
        P("tensor"),
        P("tensor"),
        P("dp", "seq"),
        P("dp", "seq", None),
        P(("seq", "dp"), "tensor"),
    )
    out_specs = (
        P("dp", "seq", "tensor"),
        P("dp", "seq", "tensor"),
        P("dp", "seq", "tensor"),
        P(("seq", "dp"), "tensor"),
    )
    return jax.shard_map(body, mesh=mesh, in_specs=in_specs, out_specs=out_specs, check_vma=False)
```

```python
import functools

import jax
import jax.numpy as jnp
import numpy as np
from jax import lax
from jax.experimental import pallas as pl
from jax.experimental.pallas import tpu as pltpu
from jax.sharding import PartitionSpec as P

P_SIZE = 64
N = 128
Q = 256
HALF = 128
PAIR = 2 * P_SIZE
SHARES = (6, 10)
PARITY, CORE, ODD, CHIP = 4, 6, 7, 8
BF = jnp.bfloat16
F32 = jnp.float32

SMEM = pl.BlockSpec(memory_space=pltpu.SMEM)
ANY = pl.BlockSpec(memory_space=pl.ANY)
FREE = pl.CostEstimate(flops=0, bytes_accessed=0, transcendentals=0)
LIMIT = pltpu.CompilerParams(vmem_limit_bytes=16 * 2**20)


def name_of(kernel):
    return getattr(kernel, "func", kernel).__name__


def whole(shape):
    return pl.BlockSpec(shape, lambda *_: (0,) * len(shape))


def call(kernel, scalars, arrays, outs, after=(), aliases=None):
    pairs = [item if isinstance(item, tuple) else (item, whole(item.shape)) for item in arrays]
    outs = [item if len(item) == 3 else (*item, whole(item[0])) for item in outs]
    count = len(scalars)

    def run(*refs):
        kernel(*refs[: count + len(pairs)], *refs[count + len(pairs) + len(after) :])

    return pl.pallas_call(
        run,
        grid=(1,),
        out_shape=[jax.ShapeDtypeStruct(shape, kind) for shape, kind, _ in outs],
        in_specs=[SMEM] * count + [spec for _, spec in pairs] + [ANY] * len(after),
        out_specs=[spec for _, _, spec in outs],
        input_output_aliases=aliases or {},
        cost_estimate=FREE,
        compiler_params=LIMIT,
        name=name_of(kernel),
    )(*scalars, *[array for array, _ in pairs], *after)


def column_call(kernel, at, ids, grads, others, span, outs, after=()):
    def run(*refs):
        kernel(*refs[: 2 + len(others)], *refs[2 + len(others) + len(after) :])

    return pl.pallas_call(
        run,
        out_shape=[jax.ShapeDtypeStruct(shape, kind) for shape, kind in outs],
        grid_spec=pltpu.PrefetchScalarGridSpec(
            num_scalar_prefetch=1,
            grid=(1,),
            in_specs=[pl.BlockSpec((Q, span), lambda i, ids_ref: (0, ids_ref[at]))]
            + [whole(other.shape) for other in others]
            + [ANY] * len(after),
            out_specs=[whole(shape) for shape, _ in outs],
        ),
        cost_estimate=FREE,
        compiler_params=LIMIT,
        name=name_of(kernel),
    )(ids, grads, *others, *after)


def dot(a, b, left, right):
    return lax.dot_general(a, b, (((left,), (right,)), ((), ())), preferred_element_type=F32)


def first_head(rows=Q):
    return lax.broadcasted_iota(jnp.int32, (rows, PAIR), 1) < P_SIZE


def spread(table, pair, first):
    return jnp.where(first, table[:, 2 * pair : 2 * pair + 1], table[:, 2 * pair + 1 : 2 * pair + 2])


def gains(skip_ref, head):
    first = lax.broadcasted_iota(jnp.int32, (1, PAIR), 1) < P_SIZE
    return jnp.where(first, skip_ref[head], skip_ref[head + 1])


def tables_kernel(
    rate_ref, resets_ref, x_ref, b_ref, step_ref, *refs
):
    states, sent, (weighted_ref, rows_ref, cols_ref, through_ref) = refs[:2], refs[2:4], refs[4:]
    heads = step_ref.shape[0]
    keep = (1 - resets_ref[0, 0]).astype(F32)
    head_id = lax.broadcasted_iota(jnp.int32, (heads, Q), 0)
    lane = lax.broadcasted_iota(jnp.int32, (heads, Q), 1)
    rate = jnp.zeros((heads, Q), F32)
    for head in range(heads):
        rate = jnp.where(head_id == head, rate_ref[head], rate)
    log = -step_ref[...] * rate
    shift = 1
    while shift < Q:
        log = log + jnp.where(lane >= shift, pltpu.roll(log, shift, 1), 0.0)
        shift *= 2
    rows_ref[...] = log
    cols = log.T
    cols_ref[...] = cols
    first = first_head()
    for pair in range(heads // 2):
        at = slice(pair * PAIR, (pair + 1) * PAIR)
        log_pair = spread(cols, pair, first)
        last = log_pair[Q - 1 : Q, :]
        weighted_ref[:, at] = (x_ref[:, at].astype(F32) * jnp.exp(last - log_pair)).astype(BF)
        through_ref[:, at] = jnp.broadcast_to(keep * jnp.exp(last), (8, PAIR))
    state = dot(b_ref[...], weighted_ref[...], 0, 0)
    middle = state.shape[1] // 2
    for number in range(2):
        half = state[:, number * middle : (number + 1) * middle]
        states[number][...] = half
        sent[number][...] = half.astype(BF)


def local_output_kernel(skip_ref, x_ref, b_ref, c_ref, rows_ref, cols_ref, out_ref):
    heads = rows_ref.shape[0]
    scores = dot(c_ref[...], b_ref[...], 1, 1)
    at_row = lax.broadcasted_iota(jnp.int32, (HALF, HALF), 0)
    at_lane = lax.broadcasted_iota(jnp.int32, (HALF, HALF), 1)
    causal = at_row >= at_lane
    first = first_head()
    zero = jnp.zeros((Q, PAIR), BF)
    for pair in range(heads // 2):
        at = slice(pair * PAIR, (pair + 1) * PAIR)
        x_pair = x_ref[:, at]
        skip = gains(skip_ref, 2 * pair) * x_pair.astype(F32)
        top, bottom = skip[:HALF], skip[HALF:]
        for side in range(2):
            head = 2 * pair + side
            x_head = jnp.where(first, x_pair, zero) if side == 0 else jnp.where(first, zero, x_pair)
            col = cols_ref[:, head : head + 1]
            row = rows_ref[head : head + 1, :]

            def mix(i, j):
                span = col[i * HALF : (i + 1) * HALF] - row[:, j * HALF : (j + 1) * HALF]
                weight = jnp.exp(jnp.minimum(span, 0.0))
                if i == j:
                    weight = jnp.where(causal, weight, 0.0)
                return (weight * scores[i * HALF : (i + 1) * HALF, j * HALF : (j + 1) * HALF]).astype(BF)

            top += dot(mix(0, 0), x_head[:HALF], 1, 0)
            bottom += dot(jnp.concatenate([mix(1, 0), mix(1, 1)], axis=1), x_head, 1, 0)
        out_ref[:HALF, at] = top
        out_ref[HALF:, at] = bottom


def output_kernel(
    start, ids_ref, resets_ref, local_ref, c_ref, cols_ref, through_ref, before_ref, left_ref, right_ref, out_ref, state_ref
):
    first = first_head()
    cols = cols_ref[...]
    keep = (1 - resets_ref[0, 0]).astype(F32)
    part = slice(start, start + out_ref.shape[1])
    partner = jnp.concatenate([left_ref[...], right_ref[...]], axis=1)[:, part].astype(F32)
    before = before_ref[:, part].astype(F32)
    state = jnp.where(ids_ref[CORE] == 1, through_ref[:1, part] * before + partner, before)
    state_ref[...] = (keep * state).astype(BF)
    for pair in range(out_ref.shape[1] // PAIR):
        at = slice(pair * PAIR, (pair + 1) * PAIR)
        whole = slice(start + pair * PAIR, start + (pair + 1) * PAIR)
        term = dot(c_ref[...], state_ref[:, at], 1, 0)
        decay = jnp.exp(spread(cols, start // PAIR + pair, first))
        out_ref[:, at] = (local_ref[:, whole] + decay * term).astype(BF)


def block_of(ids_ref, grad_ref, slot):
    depth = grad_ref.shape[1] // 4
    return grad_ref[:, pl.ds(pl.multiple_of(ids_ref[slot] * depth, depth), depth)]


def send_kernel(ids_ref, grad_ref, out_ref):
    depth = out_ref.shape[1] // 2
    for half in range(2):
        out_ref[:, half * depth : (half + 1) * depth] = block_of(ids_ref, grad_ref, PARITY + half)


def own_kernel(ids_ref, grad_ref, *halves):
    depth = halves[0].shape[1] // 2
    for slot in range(4):
        halves[slot // 2][:, slot % 2 * depth : (slot % 2 + 1) * depth] = block_of(ids_ref, grad_ref, slot)


def assemble_kernel(ids_ref, *refs):
    pieces, blocks = refs[:-4], refs[-4:]
    depth = blocks[0].shape[1]
    even = ids_ref[ODD] == 0
    for number, out_ref in enumerate(blocks):
        taken = slice(number // 2 * depth, (number // 2 + 1) * depth)
        for other in range(len(pieces) // 2):
            near, far = pieces[2 * other], pieces[2 * other + 1]
            first, second = (near, far) if number % 2 == 0 else (far, near)
            rows = slice(other * Q, (other + 1) * Q)
            out_ref[rows, :] = jnp.where(even, first[:, taken], second[:, taken])


def head_partial_kernel(mine_ref, other_ref, *refs):
    came, weights, outs = refs[:4], refs[4:9], refs[9:]
    depth = weights[0].shape[0]
    middle = weights[3].shape[0]
    for number in reversed(range(len(outs))):
        total = None
        for block in range(4):
            rows = slice((number - 1) * Q, number * Q)
            if number == 0:
                grad = (mine_ref, other_ref)[block // 2][:, block % 2 * depth : (block % 2 + 1) * depth]
            else:
                grad = came[block][rows, :]
            if block < 3:
                term = dot(grad, weights[block][...], 1, 0)
            else:
                term = dot(grad[:, :middle], weights[3][...], 1, 0) + dot(grad[:, middle:], weights[4][...], 1, 0)
            total = term if total is None else total + term
        outs[number][...] = total.astype(outs[number].dtype)


def adjoint_kernel(others, resets_ref, own_ref, *refs):
    parts, (c_ref, cols_ref, head_ref, weighted_ref, *halves) = refs[:others], refs[others:]
    first = first_head()
    cols = cols_ref[...]
    keep = (1 - resets_ref[0, 0]).astype(F32)
    for pair in range(head_ref.shape[1] // PAIR):
        at = slice(pair * PAIR, (pair + 1) * PAIR)
        total = own_ref[:, at]
        for part in parts:
            total = total + part[:, at].astype(F32)
        head = total.astype(BF)
        head_ref[:, at] = head
        weighted_ref[:, at] = (head.astype(F32) * jnp.exp(spread(cols, pair, first))).astype(BF)
    adjoint = keep * dot(c_ref[...], weighted_ref[...], 0, 0)
    middle = adjoint.shape[1] // 2
    for number in range(2):
        half = adjoint[:, number * middle : (number + 1) * middle]
        halves[number][...] = half
        halves[2][:, number * middle : (number + 1) * middle] = half.astype(BF)


def chip_total_kernel(last, parts, ids_ref, through_ref, partner_through_ref, *refs):
    owns, partners, entering, out_ref = refs[:2], refs[2 : 2 + parts], refs[2 + parts : -1], refs[-1]
    leaves = ids_ref[CORE] == last
    width = owns[0].shape[1]
    halved = out_ref.shape[1] < 2 * width
    partner_state = jnp.concatenate([ref[...] for ref in partners], axis=1)
    totals = []
    for part in range(2):
        at = slice(part * width, (part + 1) * width)
        own, partner = owns[part][...], partner_state[:, at].astype(F32)
        mine, theirs = through_ref[:1, at], partner_through_ref[:1, at]
        total = jnp.where(leaves, mine * partner + own, theirs * own + partner)
        for value in entering:
            came = value[...] if halved else value[:, at]
            total += mine * theirs * came.astype(F32)
        if halved:
            totals.append(total)
        else:
            out_ref[:, at] = total.astype(BF)
    if halved:
        out_ref[...] = jnp.where(ids_ref[CORE] == 0, totals[0], totals[1]).astype(BF)


def local_grads_kernel(
    skip_ref, x_ref, grad_ref, b_ref, c_ref, rows_ref, cols_ref, weighted_ref, *refs
):
    states, (in_ref, paired_ref, c_out_ref) = refs[:-3], refs[-3:]
    heads = x_ref.shape[1] // P_SIZE
    scores = dot(b_ref[...], c_ref[...], 1, 1)
    at_row = lax.broadcasted_iota(jnp.int32, (HALF, HALF), 0)
    at_lane = lax.broadcasted_iota(jnp.int32, (HALF, HALF), 1)
    causal = at_lane >= at_row
    first = first_head()
    zero = jnp.zeros((Q, PAIR), BF)
    paired_ref[...] = jnp.zeros_like(paired_ref)
    for pair in range(heads // 2):
        at = slice(pair * PAIR, (pair + 1) * PAIR)
        x_pair = x_ref[:, at]
        g_pair = grad_ref[:, at]
        skip = gains(skip_ref, 2 * pair) * g_pair.astype(F32)
        top, bottom = skip[:HALF], skip[HALF:]
        for side in range(2):
            head = 2 * pair + side
            g_head = jnp.where(first, g_pair, zero) if side == 0 else jnp.where(first, zero, g_pair)
            col = cols_ref[:, head : head + 1]
            row = rows_ref[head : head + 1, :]

            def weigh(j, i):
                span = row[:, i * HALF : (i + 1) * HALF] - col[j * HALF : (j + 1) * HALF]
                weight = jnp.exp(jnp.minimum(span, 0.0))
                return jnp.where(causal, weight, 0.0) if i == j else weight

            early = jnp.concatenate([weigh(0, 0), weigh(0, 1)], axis=1)
            late = weigh(1, 1)
            top += dot((early * scores[:HALF]).astype(BF), g_head, 1, 0)
            bottom += dot((late * scores[HALF:, HALF:]).astype(BF), g_head[HALF:], 1, 0)
            paired_ref[:HALF, :] += early * dot(x_pair[:HALF], g_head, 1, 1)
            paired_ref[HALF:, HALF:] += late * dot(x_pair[HALF:], g_head[HALF:], 1, 1)
        in_ref[:HALF, at] = top
        in_ref[HALF:, at] = bottom
    start, total = 0, None
    for state in states:
        width = state.shape[1]
        term = dot(weighted_ref[:, start : start + width], state[...], 1, 1)
        total = term if total is None else total + term
        start += width
    c_out_ref[...] = total


def group_sums_kernel(b_ref, c_ref, paired_ref, c_part_ref, grad_b_ref, grad_c_ref):
    paired = paired_ref[...].astype(BF)
    grad_b_ref[...] = dot(paired, c_ref[...], 1, 0)
    grad_c_ref[...] = c_part_ref[...] + dot(paired, b_ref[...], 0, 0)


def final_kernel(ids_ref, b_ref, cols_ref, sums_ref, weighted_ref, through_ref, local_ref, *refs):
    entered, partner_ref, (in_ref, grad_b_ref, token_ref) = refs[:2], refs[2], refs[3:]
    token_ref[...] = jnp.zeros_like(token_ref)
    first = first_head()
    cols = cols_ref[...]
    grad_b = sums_ref[...]
    core = ids_ref[CORE]
    width = partner_ref.shape[1] // 2
    for half in range(2):
        here = slice(half * width, (half + 1) * width)
        entering = jnp.where(core == half, entered[0][...].astype(F32), entered[1][...].astype(F32))
        inner = through_ref[:1, here] * entering + partner_ref[:, here].astype(F32)
        adjoint = jnp.where(core == 1, entering, inner).astype(BF)
        grad_b += dot(weighted_ref[:, here], adjoint, 1, 1)
        for number in range(width // PAIR):
            pair = half * (width // PAIR) + number
            at = slice(pair * PAIR, (pair + 1) * PAIR)
            log_pair = spread(cols, pair, first)
            to_end = jnp.exp(log_pair[Q - 1 : Q, :] - log_pair)
            term = dot(b_ref[...], adjoint[:, number * PAIR : (number + 1) * PAIR], 1, 0)
            in_ref[:, at] = (local_ref[:, at] + to_end * term).astype(BF)
    grad_b_ref[...] = grad_b


def add_kernel(parts, *refs):
    kept, came, out_ref = refs[:parts], refs[parts:-1], refs[-1]
    for group, change in ((kept, False), (came, True)):
        start = 0
        for ref in group:
            at = slice(start, start + ref.shape[1])
            out_ref[:, at] = out_ref[:, at] + ref[...].astype(F32) if change else ref[...]
            start += ref.shape[1]


def weight_partial_kernel(chips, pieces, *refs):
    owns, came, refs = refs[:2], (refs[2:4], refs[4:6]), refs[6:]
    outputs, kept_ref, sent = refs[: -1 - pieces], refs[-1 - pieces], refs[-pieces:]
    depth = kept_ref.shape[0]
    outputs = [ref[...] for ref in outputs]
    if len(outputs) > 2 * chips:
        cut = outputs[chips + 1 :]
        outputs = outputs[: chips + 1] + [jnp.concatenate(cut[i : i + 2], axis=1) for i in range(0, len(cut), 2)]
    for slot in (1, 0):
        total = None
        for number, output in enumerate(outputs):
            core, by = number // chips, number % chips
            if by == 0:
                grad = owns[core][:, slot * depth : (slot + 1) * depth]
            else:
                grad = came[core][slot][(by - 1) * Q : by * Q, :]
            term = dot(grad, output, 0, 0)
            total = term if total is None else total + term
        if slot == 0:
            kept_ref[...] = total
            continue
        start = 0
        for ref in sent:
            ref[...] = total[:, start : start + ref.shape[1]].astype(BF)
            start += ref.shape[1]


def body(
    ssm_input, b_input, c_input, step_size, decay_rate, skip_gain, resets, out_grad, out_weight
):
    seq, dp, planes = lax.axis_size("seq"), lax.axis_size("dp"), lax.axis_size("tensor")
    chips = seq // 2
    me = lax.axis_index(("seq", "tensor", "dp"))
    heads = decay_rate.shape[0]
    wide = heads * P_SIZE
    widths = [wide * share // sum(SHARES) // PAIR * PAIR for share in SHARES]
    starts = [sum(widths[:part]) for part in range(len(widths))]
    depth = out_weight.shape[0]
    span = 4 * depth
    assert ssm_input.shape[1] == Q and dp == 2 and seq % 2 == 0 and seq > 2 and planes % 2 == 0
    def later(value, other):
        return lax.optimization_barrier((value, other))[0]

    across = [(i, i ^ 1) for i in range(seq)]

    def core_swap(value):
        return lax.ppermute(value, "seq", across)

    def chip_shift(value, by):
        return lax.ppermute(value, "seq", [(i, (i + 2 * by) % seq) for i in range(seq)])

    def plane_swap(value):
        return lax.ppermute(value, "tensor", [(i, i ^ 1) for i in range(planes)])

    def dialogue_swap(value):
        return lax.ppermute(value, "dp", [(0, 1), (1, 0)])

    x, b_rows, c_rows, steps, incoming = (
        ssm_input[0], b_input[0], c_input[0], step_size[0], out_grad[0]
    )
    table = []
    for at in range(seq * planes * dp):
        chip, core, odd, dialogue = at // (2 * planes * dp), at // (planes * dp) % 2, at // dp % 2, at % dp
        order = [core * 2 + dialogue, core * 2 + 1 - dialogue, (1 - core) * 2 + dialogue, (1 - core) * 2 + 1 - dialogue]
        table.append(order + [order[odd], order[2 + odd], core, odd] + [(chip + by) % chips for by in range(chips)])
    ids = lax.dynamic_index_in_dim(np.array(table, np.int32), me, keepdims=False)

    to_send = [
        column_call(send_kernel, CHIP + by, ids, incoming, [], span, [((Q, 2 * depth), BF)])
        for by in range(1, chips)
    ]

    weight_other = dialogue_swap(out_weight)
    weight_core = core_swap(out_weight)

    near = [chip_shift(to_send[by - 1][0], by) for by in range(1, chips)]
    pieces = []
    for piece in near:
        pieces += [piece, plane_swap(piece)]

    *both, weighted_in, log_rows, log_cols, through = call(
        tables_kernel,
        (decay_rate, resets),
        (x, b_rows, steps),
        [((N, wide // 2), F32)] * 2 + [((N, wide // 2), BF)] * 2 + [((Q, wide), BF)]
        + [((heads, Q), F32), ((Q, heads), F32), ((8, wide), F32)],
        after=[weight_core, *[sent[0] for sent in to_send]],
    )
    local_output, = call(
        local_output_kernel,
        (skip_gain,),
        (x, b_rows, c_rows, log_rows, log_cols),
        [((Q, wide), F32)],
    )
    state_partner = [core_swap(half) for half in both[2:]]
    through_partner = core_swap(through)
    mine, other = column_call(
        own_kernel, CHIP, ids, incoming, [], span, [((Q, span // 2), BF)] * 2, after=[through]
    )
    partner = core_swap(other)
    before = []
    for hop in range(1, chips):
        total, = call(
            functools.partial(chip_total_kernel, 1, 2),
            (ids,),
            (through, through_partner, *both[:2], *state_partner, *before),
            [((N, wide), BF)],
            after=[local_output] if hop == 1 else (),
        )
        before = [lax.ppermute(total, "seq", [(i, i + 2) for i in range(seq - 2)])]
    outputs, swapped, states = [], [], []
    for start, width in zip(starts, widths):
        output, state_in = call(
            functools.partial(output_kernel, start),
            (ids, resets),
            (local_output, c_rows, log_cols, through_partner, *before, *state_partner),
            [((Q, width), BF), ((N, width), BF)],
            after=outputs[-1][:1] if outputs else [partner],
        )
        states.append(state_in)
        outputs.append([output] + [chip_shift(output, by) for by in range(1, chips)])
        swapped.append(core_swap(output))

    came = call(
        assemble_kernel, (ids,), pieces, [(((chips - 1) * Q, depth), BF)] * 4, after=[outputs[-1][0]],
    )
    partner_came = [core_swap(block) for block in came[2:]]
    weight_late = later(weight_other, outputs[-1][0])
    weights = [out_weight, weight_other, weight_core]
    weights += [core_swap(weight_late[: depth // 2]), core_swap(weight_late[depth // 2 :])]

    partials = call(
        head_partial_kernel,
        (),
        (mine, other, *came, *weights),
        [((Q, wide), F32)] + [((Q, wide), BF)] * (chips - 1),
    )
    returned = [chip_shift(partials[by], -by) for by in range(1, chips)]

    sent, kept, sums = [], [], []
    for part, width in enumerate(widths):
        pieces = [later(piece, sent[-1] if sent else partials[0]) for piece in outputs[part][1:]]
        cut = width // 2 if width > wide // 2 else width
        swaps = [core_swap(piece[:, at : at + cut]) for piece in pieces for at in range(0, width, cut)]
        sizes = [width]
        partial, *own = call(
            functools.partial(weight_partial_kernel, chips, len(sizes)),
            (),
            (mine, partner, *came[:2], *partner_came, *outputs[part], swapped[part], *swaps),
            [((depth, width), F32)] + [((depth, size), BF) for size in sizes],
            after=[partials[0], *sent[-1:]],
        )
        sent.append(own[0])
        kept.append(partial)
        sums += [dialogue_swap(value) for value in own]

    head_grad, weighted_grad, *both = call(
        functools.partial(adjoint_kernel, chips - 1),
        (resets,),
        (partials[0], *returned, c_rows, log_cols),
        [((Q, wide), BF), ((Q, wide), BF)] + [((N, wide // 2), F32)] * 2 + [((N, wide), BF)],
        after=[sums[0], *sent],
    )
    adjoint_partner = core_swap(both[2])
    local_in, paired, c_part = call(
        local_grads_kernel,
        (skip_gain,),
        (x, head_grad, b_rows, c_rows, log_rows, log_cols, weighted_grad, *states),
        [((Q, wide), F32), ((Q, Q), F32), ((Q, N), F32)],
    )
    entering = []
    for hop in range(1, chips):
        total, = call(
            functools.partial(chip_total_kernel, 0, 1),
            (ids,),
            (through, through_partner, *both[:2], adjoint_partner, *entering),
            [((N, wide // 2), BF)],
        )
        entering = [lax.ppermute(total, "seq", [(i, i - 2) for i in range(2, seq)])]
    grad_b, grad_c = call(
        group_sums_kernel,
        (),
        (b_rows, c_rows, paired, c_part),
        [((Q, N), F32), ((Q, N), F32)],
    )
    grad_in, grad_b, token = call(
        final_kernel,
        (ids,),
        (b_rows, log_cols, grad_b, weighted_in, through_partner, local_in)
        + (*entering, core_swap(later(entering[0], grad_c)), adjoint_partner),
        [((Q, wide), BF), ((Q, N), F32), ((8, 128), F32)],
    )
    grad_weight, = call(
        functools.partial(add_kernel, len(widths)),
        (),
        (*kept, *sums),
        [((depth, wide), F32)],
        after=[token],
    )
    return grad_in[None], grad_b[None], grad_c[None], grad_weight


def solution(mesh):
    in_specs = (
        P("dp", "seq", "tensor"),
        P("dp", "seq", "tensor"),
        P("dp", "seq", "tensor"),
        P("dp", "tensor", "seq"),
        P("tensor"),
        P("tensor"),
        P("dp", "seq"),
        P("dp", "seq", None),
        P(("seq", "dp"), "tensor"),
    )
    out_specs = (
        P("dp", "seq", "tensor"),
        P("dp", "seq", "tensor"),
        P("dp", "seq", "tensor"),
        P(("seq", "dp"), "tensor"),
    )
    return jax.shard_map(body, mesh=mesh, in_specs=in_specs, out_specs=out_specs, check_vma=False)
```

```python
import functools

import jax
import jax.numpy as jnp
from jax import lax
from jax.experimental import pallas as pl
from jax.experimental.pallas import tpu as pltpu
from jax.sharding import PartitionSpec as P

P_SIZE = 64
N = 128
Q = 256
HALF = 128
PAIR = 2 * P_SIZE
SHARES = (6, 10)
PARITY, CORE, ODD, CHIP = 4, 6, 7, 8
THROUGH, KEEP, CORE_ROW, SKIP, ODD_ROW = (slice(row, row + 1) for row in range(5))
BF = jnp.bfloat16
F32 = jnp.float32

SMEM = pl.BlockSpec(memory_space=pltpu.SMEM)
ANY = pl.BlockSpec(memory_space=pl.ANY)
FREE = pl.CostEstimate(flops=0, bytes_accessed=0, transcendentals=0)
LIMIT = pltpu.CompilerParams(vmem_limit_bytes=16 * 2**20)


def name_of(kernel):
    return getattr(kernel, "func", kernel).__name__


def whole(shape):
    return pl.BlockSpec(shape, lambda *_: (0,) * len(shape))


def call(kernel, scalars, arrays, outs, after=(), aliases=None):
    pairs = [item if isinstance(item, tuple) else (item, whole(item.shape)) for item in arrays]
    outs = [item if len(item) == 3 else (*item, whole(item[0])) for item in outs]
    count = len(scalars)
    views = [item.view if isinstance(item, Ids) else (lambda ref: ref) for item in scalars]
    scalars = [item.number if isinstance(item, Ids) else item for item in scalars]

    def run(*refs):
        seen = [view(ref) for view, ref in zip(views, refs)]
        kernel(*seen, *refs[count : count + len(pairs)], *refs[count + len(pairs) + len(after) :])

    return pl.pallas_call(
        run,
        grid=(1,),
        out_shape=[jax.ShapeDtypeStruct(shape, kind) for shape, kind, _ in outs],
        in_specs=[SMEM] * count + [spec for _, spec in pairs] + [ANY] * len(after),
        out_specs=[spec for _, _, spec in outs],
        input_output_aliases=aliases or {},
        cost_estimate=FREE,
        compiler_params=LIMIT,
        name=name_of(kernel),
    )(*scalars, *[array for array, _ in pairs], *after)


class Ids:
    def __init__(self, number, chips, planes, dp):
        self.number, self.sizes = number, (chips, planes, dp)

    def view(self, ref):
        seen = Ids(None, *self.sizes)
        seen.ref = ref
        return seen

    def __getitem__(self, place):
        chips, planes, dp = self.sizes
        at = self.ref[0]
        chip, core, odd, dialogue = at // (2 * planes * dp), at // (planes * dp) % 2, at // dp % 2, at % dp
        if place >= CHIP:
            return (chip + place - CHIP) % chips
        if place in (CORE, ODD):
            return core if place == CORE else odd
        if place >= PARITY:
            half, second = place - PARITY, odd
        else:
            half, second = place // 2, place % 2
        own = core if half == 0 else 1 - core
        return own * 2 + (dialogue + second) % 2


def column_call(kernel, at, ids, grads, others, span, outs, after=()):
    def run(ids_ref, *refs):
        kernel(ids.view(ids_ref), *refs[: 1 + len(others)], *refs[1 + len(others) + len(after) :])

    return pl.pallas_call(
        run,
        out_shape=[jax.ShapeDtypeStruct(shape, kind) for shape, kind in outs],
        grid_spec=pltpu.PrefetchScalarGridSpec(
            num_scalar_prefetch=1,
            grid=(1,),
            in_specs=[pl.BlockSpec((Q, span), lambda i, ids_ref: (0, ids.view(ids_ref)[at]))]
            + [whole(other.shape) for other in others]
            + [ANY] * len(after),
            out_specs=[whole(shape) for shape, _ in outs],
        ),
        cost_estimate=FREE,
        compiler_params=LIMIT,
        name=name_of(kernel),
    )(ids.number, grads, *others, *after)


def dot(a, b, left, right):
    return lax.dot_general(a, b, (((left,), (right,)), ((), ())), preferred_element_type=F32)


def first_head(rows=Q):
    return lax.broadcasted_iota(jnp.int32, (rows, PAIR), 1) < P_SIZE


def spread(table, pair, first):
    return jnp.where(first, table[:, 2 * pair : 2 * pair + 1], table[:, 2 * pair + 1 : 2 * pair + 2])


def gains(skip_ref, head):
    first = lax.broadcasted_iota(jnp.int32, (1, PAIR), 1) < P_SIZE
    return jnp.where(first, skip_ref[head], skip_ref[head + 1])


def tables_kernel(
    ids_ref, rate_ref, resets_ref, skip_ref, x_ref, b_ref, step_ref, *refs
):
    states, sent, (weighted_ref, rows_ref, cols_ref, table_ref) = refs[:2], refs[2:4], refs[4:]
    heads = step_ref.shape[0]
    keep = (1 - resets_ref[0, 0]).astype(F32)
    head_id = lax.broadcasted_iota(jnp.int32, (heads, Q), 0)
    lane = lax.broadcasted_iota(jnp.int32, (heads, Q), 1)
    rate = jnp.zeros((heads, Q), F32)
    for head in range(heads):
        rate = jnp.where(head_id == head, rate_ref[head], rate)
    log = -step_ref[...] * rate
    shift = 1
    while shift < Q:
        log = log + jnp.where(lane >= shift, pltpu.roll(log, shift, 1), 0.0)
        shift *= 2
    rows_ref[...] = log
    cols = log.T
    cols_ref[...] = cols
    first = first_head()
    for pair in range(heads // 2):
        at = slice(pair * PAIR, (pair + 1) * PAIR)
        log_pair = spread(cols, pair, first)
        last = log_pair[Q - 1 : Q, :]
        weighted_ref[:, at] = (x_ref[:, at].astype(F32) * jnp.exp(last - log_pair)).astype(BF)
        table_ref[THROUGH, at] = keep * jnp.exp(last)
        table_ref[SKIP, at] = gains(skip_ref, 2 * pair)
    ones = jnp.ones((1, table_ref.shape[1]), F32)
    table_ref[KEEP, :] = keep * ones
    table_ref[CORE_ROW, :] = ids_ref[CORE].astype(F32) * ones
    table_ref[ODD_ROW, :] = ids_ref[ODD].astype(F32) * ones
    table_ref[5:, :] = jnp.zeros((3, table_ref.shape[1]), F32)
    state = dot(b_ref[...], weighted_ref[...], 0, 0)
    middle = state.shape[1] // 2
    for number in range(2):
        half = state[:, number * middle : (number + 1) * middle]
        states[number][...] = half
        sent[number][...] = half.astype(BF)


def local_output_kernel(table_ref, x_ref, b_ref, c_ref, rows_ref, cols_ref, out_ref):
    heads = rows_ref.shape[0]
    scores = dot(c_ref[...], b_ref[...], 1, 1)
    at_row = lax.broadcasted_iota(jnp.int32, (HALF, HALF), 0)
    at_lane = lax.broadcasted_iota(jnp.int32, (HALF, HALF), 1)
    causal = at_row >= at_lane
    first = first_head()
    zero = jnp.zeros((Q, PAIR), BF)
    for pair in range(heads // 2):
        at = slice(pair * PAIR, (pair + 1) * PAIR)
        x_pair = x_ref[:, at]
        skip = table_ref[SKIP, at] * x_pair.astype(F32)
        top, bottom = skip[:HALF], skip[HALF:]
        for side in range(2):
            head = 2 * pair + side
            x_head = jnp.where(first, x_pair, zero) if side == 0 else jnp.where(first, zero, x_pair)
            col = cols_ref[:, head : head + 1]
            row = rows_ref[head : head + 1, :]

            def mix(i, j):
                span = col[i * HALF : (i + 1) * HALF] - row[:, j * HALF : (j + 1) * HALF]
                weight = jnp.exp(jnp.minimum(span, 0.0))
                if i == j:
                    weight = jnp.where(causal, weight, 0.0)
                return (weight * scores[i * HALF : (i + 1) * HALF, j * HALF : (j + 1) * HALF]).astype(BF)

            top += dot(mix(0, 0), x_head[:HALF], 1, 0)
            bottom += dot(jnp.concatenate([mix(1, 0), mix(1, 1)], axis=1), x_head, 1, 0)
        out_ref[:HALF, at] = top
        out_ref[HALF:, at] = bottom


def output_kernel(starts, table_ref, local_ref, c_ref, cols_ref, through_ref, before_ref, *refs):
    partners, outs, states = refs[:2], refs[2 : 2 + len(starts)], refs[2 + len(starts) :]
    first = first_head()
    cols = cols_ref[...]
    partner = jnp.concatenate([ref[...] for ref in partners], axis=1)
    for start, out_ref, state_ref in zip(starts, outs, states):
        part = slice(start, start + out_ref.shape[1])
        before = before_ref[:, part].astype(F32)
        after = through_ref[THROUGH, part] * before + partner[:, part].astype(F32)
        state = jnp.where(table_ref[CORE_ROW, part] == 1.0, after, before)
        state_ref[...] = (table_ref[KEEP, part] * state).astype(BF)
        for pair in range(out_ref.shape[1] // PAIR):
            at = slice(pair * PAIR, (pair + 1) * PAIR)
            whole = slice(start + pair * PAIR, start + (pair + 1) * PAIR)
            term = dot(c_ref[...], state_ref[:, at], 1, 0)
            decay = jnp.exp(spread(cols, start // PAIR + pair, first))
            out_ref[:, at] = (local_ref[:, whole] + decay * term).astype(BF)


def block_of(ids_ref, grad_ref, slot):
    depth = grad_ref.shape[1] // 4
    return grad_ref[:, pl.ds(pl.multiple_of(ids_ref[slot] * depth, depth), depth)]


def send_kernel(ids_ref, grad_ref, out_ref):
    depth = out_ref.shape[1] // 2
    for half in range(2):
        out_ref[:, half * depth : (half + 1) * depth] = block_of(ids_ref, grad_ref, PARITY + half)


def own_kernel(ids_ref, grad_ref, *halves):
    depth = halves[0].shape[1] // 2
    for slot in range(4):
        halves[slot // 2][:, slot % 2 * depth : (slot % 2 + 1) * depth] = block_of(ids_ref, grad_ref, slot)


def assemble_kernel(table_ref, *refs):
    pieces, blocks = refs[:-4], refs[-4:]
    depth = blocks[0].shape[1]
    even = table_ref[ODD_ROW, :depth] == 0.0
    for number, out_ref in enumerate(blocks):
        taken = slice(number // 2 * depth, (number // 2 + 1) * depth)
        for other in range(len(pieces) // 2):
            near, far = pieces[2 * other], pieces[2 * other + 1]
            first, second = (near, far) if number % 2 == 0 else (far, near)
            rows = slice(other * Q, (other + 1) * Q)
            out_ref[rows, :] = jnp.where(even, first[:, taken], second[:, taken])


def head_partial_kernel(mine_ref, other_ref, *refs):
    came, weights, outs = refs[:4], refs[4:9], refs[9:]
    depth = weights[0].shape[0]
    middle = weights[3].shape[0]
    for number in reversed(range(len(outs))):
        total = None
        for block in range(4):
            rows = slice((number - 1) * Q, number * Q)
            if number == 0:
                grad = (mine_ref, other_ref)[block // 2][:, block % 2 * depth : (block % 2 + 1) * depth]
            else:
                grad = came[block][rows, :]
            if block < 3:
                term = dot(grad, weights[block][...], 1, 0)
            else:
                term = dot(grad[:, :middle], weights[3][...], 1, 0) + dot(grad[:, middle:], weights[4][...], 1, 0)
            total = term if total is None else total + term
        outs[number][...] = total.astype(outs[number].dtype)


def adjoint_kernel(others, table_ref, own_ref, *refs):
    parts, (c_ref, cols_ref, head_ref, weighted_ref, *halves) = refs[:others], refs[others:]
    first = first_head()
    cols = cols_ref[...]
    for pair in range(head_ref.shape[1] // PAIR):
        at = slice(pair * PAIR, (pair + 1) * PAIR)
        total = own_ref[:, at]
        for part in parts:
            total = total + part[:, at].astype(F32)
        head = total.astype(BF)
        head_ref[:, at] = head
        weighted_ref[:, at] = (head.astype(F32) * jnp.exp(spread(cols, pair, first))).astype(BF)
    adjoint = table_ref[KEEP, :] * dot(c_ref[...], weighted_ref[...], 0, 0)
    middle = adjoint.shape[1] // 2
    for number in range(2):
        half = adjoint[:, number * middle : (number + 1) * middle]
        halves[number][...] = half
        halves[2][:, number * middle : (number + 1) * middle] = half.astype(BF)


def chip_total_kernel(last, parts, through_ref, partner_through_ref, *refs):
    owns, partners, entering, out_ref = refs[:2], refs[2 : 2 + parts], refs[2 + parts : -1], refs[-1]
    width = owns[0].shape[1]
    halved = out_ref.shape[1] < 2 * width
    partner_state = jnp.concatenate([ref[...] for ref in partners], axis=1)
    totals = []
    for part in range(2):
        at = slice(part * width, (part + 1) * width)
        own, partner = owns[part][...], partner_state[:, at].astype(F32)
        mine, theirs = through_ref[THROUGH, at], partner_through_ref[THROUGH, at]
        leaves = through_ref[CORE_ROW, at] == float(last)
        total = jnp.where(leaves, mine * partner + own, theirs * own + partner)
        for value in entering:
            came = value[...] if halved else value[:, at]
            total += mine * theirs * came.astype(F32)
        if halved:
            totals.append(total)
        else:
            out_ref[:, at] = total.astype(BF)
    if halved:
        first_core = through_ref[CORE_ROW, :width] == 0.0
        out_ref[...] = jnp.where(first_core, totals[0], totals[1]).astype(BF)


def local_grads_kernel(
    table_ref, x_ref, grad_ref, b_ref, c_ref, rows_ref, cols_ref, weighted_ref, *refs
):
    states, (in_ref, paired_ref, c_out_ref) = refs[:-3], refs[-3:]
    heads = x_ref.shape[1] // P_SIZE
    scores = dot(b_ref[...], c_ref[...], 1, 1)
    at_row = lax.broadcasted_iota(jnp.int32, (HALF, HALF), 0)
    at_lane = lax.broadcasted_iota(jnp.int32, (HALF, HALF), 1)
    causal = at_lane >= at_row
    first = first_head()
    zero = jnp.zeros((Q, PAIR), BF)
    paired_ref[...] = jnp.zeros_like(paired_ref)
    for pair in range(heads // 2):
        at = slice(pair * PAIR, (pair + 1) * PAIR)
        x_pair = x_ref[:, at]
        g_pair = grad_ref[:, at]
        skip = table_ref[SKIP, at] * g_pair.astype(F32)
        top, bottom = skip[:HALF], skip[HALF:]
        for side in range(2):
            head = 2 * pair + side
            g_head = jnp.where(first, g_pair, zero) if side == 0 else jnp.where(first, zero, g_pair)
            col = cols_ref[:, head : head + 1]
            row = rows_ref[head : head + 1, :]

            def weigh(j, i):
                span = row[:, i * HALF : (i + 1) * HALF] - col[j * HALF : (j + 1) * HALF]
                weight = jnp.exp(jnp.minimum(span, 0.0))
                return jnp.where(causal, weight, 0.0) if i == j else weight

            early = jnp.concatenate([weigh(0, 0), weigh(0, 1)], axis=1)
            late = weigh(1, 1)
            top += dot((early * scores[:HALF]).astype(BF), g_head, 1, 0)
            bottom += dot((late * scores[HALF:, HALF:]).astype(BF), g_head[HALF:], 1, 0)
            paired_ref[:HALF, :] += early * dot(x_pair[:HALF], g_head, 1, 1)
            paired_ref[HALF:, HALF:] += late * dot(x_pair[HALF:], g_head[HALF:], 1, 1)
        in_ref[:HALF, at] = top
        in_ref[HALF:, at] = bottom
    start, total = 0, None
    for state in states:
        width = state.shape[1]
        term = dot(weighted_ref[:, start : start + width], state[...], 1, 1)
        total = term if total is None else total + term
        start += width
    c_out_ref[...] = total


def group_sums_kernel(b_ref, c_ref, paired_ref, c_part_ref, grad_b_ref, grad_c_ref):
    paired = paired_ref[...].astype(BF)
    grad_b_ref[...] = dot(paired, c_ref[...], 1, 0)
    grad_c_ref[...] = c_part_ref[...] + dot(paired, b_ref[...], 0, 0)


def final_kernel(table_ref, b_ref, cols_ref, sums_ref, weighted_ref, through_ref, local_ref, *refs):
    entered, partner_ref, (in_ref, grad_b_ref, token_ref) = refs[:2], refs[2], refs[3:]
    token_ref[...] = jnp.zeros_like(token_ref)
    first = first_head()
    cols = cols_ref[...]
    grad_b = sums_ref[...]
    width = partner_ref.shape[1] // 2
    for half in range(2):
        here = slice(half * width, (half + 1) * width)
        core = table_ref[CORE_ROW, here]
        entering = jnp.where(core == float(half), entered[0][...].astype(F32), entered[1][...].astype(F32))
        inner = through_ref[THROUGH, here] * entering + partner_ref[:, here].astype(F32)
        adjoint = jnp.where(core == 1.0, entering, inner).astype(BF)
        grad_b += dot(weighted_ref[:, here], adjoint, 1, 1)
        for number in range(width // PAIR):
            pair = half * (width // PAIR) + number
            at = slice(pair * PAIR, (pair + 1) * PAIR)
            log_pair = spread(cols, pair, first)
            to_end = jnp.exp(log_pair[Q - 1 : Q, :] - log_pair)
            term = dot(b_ref[...], adjoint[:, number * PAIR : (number + 1) * PAIR], 1, 0)
            in_ref[:, at] = (local_ref[:, at] + to_end * term).astype(BF)
    grad_b_ref[...] = grad_b


def add_kernel(parts, *refs):
    kept, came, out_ref = refs[:parts], refs[parts:-1], refs[-1]
    for group, change in ((kept, False), (came, True)):
        start = 0
        for ref in group:
            at = slice(start, start + ref.shape[1])
            out_ref[:, at] = out_ref[:, at] + ref[...].astype(F32) if change else ref[...]
            start += ref.shape[1]


def weight_partial_kernel(chips, pieces, *refs):
    owns, came, refs = refs[:2], (refs[2:4], refs[4:6]), refs[6:]
    outputs, kept_ref, sent = refs[: -1 - pieces], refs[-1 - pieces], refs[-pieces:]
    depth = kept_ref.shape[0]
    outputs = [ref[...] for ref in outputs]
    if len(outputs) > 2 * chips:
        cut = outputs[chips + 1 :]
        outputs = outputs[: chips + 1] + [jnp.concatenate(cut[i : i + 2], axis=1) for i in range(0, len(cut), 2)]
    for slot in (1, 0):
        total = None
        for number, output in enumerate(outputs):
            core, by = number // chips, number % chips
            if by == 0:
                grad = owns[core][:, slot * depth : (slot + 1) * depth]
            else:
                grad = came[core][slot][(by - 1) * Q : by * Q, :]
            term = dot(grad, output, 0, 0)
            total = term if total is None else total + term
        if slot == 0:
            kept_ref[...] = total
            continue
        start = 0
        for ref in sent:
            ref[...] = total[:, start : start + ref.shape[1]].astype(BF)
            start += ref.shape[1]


def body(
    ssm_input, b_input, c_input, step_size, decay_rate, skip_gain, resets, out_grad, out_weight
):
    seq, dp, planes = lax.axis_size("seq"), lax.axis_size("dp"), lax.axis_size("tensor")
    chips = seq // 2
    me = lax.axis_index(("seq", "tensor", "dp"))
    heads = decay_rate.shape[0]
    wide = heads * P_SIZE
    widths = [wide * share // sum(SHARES) // PAIR * PAIR for share in SHARES]
    starts = [sum(widths[:part]) for part in range(len(widths))]
    depth = out_weight.shape[0]
    span = 4 * depth
    assert ssm_input.shape[1] == Q and dp == 2 and seq % 2 == 0 and seq > 2 and planes % 2 == 0
    def later(value, other):
        return lax.optimization_barrier((value, other))[0]

    across = [(i, i ^ 1) for i in range(seq)]

    def core_swap(value):
        return lax.ppermute(value, "seq", across)

    def chip_shift(value, by):
        return lax.ppermute(value, "seq", [(i, (i + 2 * by) % seq) for i in range(seq)])

    def plane_swap(value):
        return lax.ppermute(value, "tensor", [(i, i ^ 1) for i in range(planes)])

    def dialogue_swap(value):
        return lax.ppermute(value, "dp", [(0, 1), (1, 0)])

    x, b_rows, c_rows, steps, incoming = (
        ssm_input[0], b_input[0], c_input[0], step_size[0], out_grad[0]
    )
    ids = Ids(me.astype(jnp.int32).reshape(1), chips, planes, dp)

    to_send = [
        column_call(send_kernel, CHIP + by, ids, incoming, [], span, [((Q, 2 * depth), BF)])
        for by in range(1, chips)
    ]

    weight_other = dialogue_swap(out_weight)
    weight_core = core_swap(out_weight)

    near = [chip_shift(to_send[by - 1][0], by) for by in range(1, chips)]
    pieces = []
    for piece in near:
        pieces += [piece, plane_swap(piece)]

    *both, weighted_in, log_rows, log_cols, through = call(
        tables_kernel,
        (ids, decay_rate, resets, skip_gain),
        (x, b_rows, steps),
        [((N, wide // 2), F32)] * 2 + [((N, wide // 2), BF)] * 2 + [((Q, wide), BF)]
        + [((heads, Q), F32), ((Q, heads), F32), ((8, wide), F32)],
        after=[weight_core, *[sent[0] for sent in to_send]],
    )
    local_output, = call(
        local_output_kernel,
        (),
        (through, x, b_rows, c_rows, log_rows, log_cols),
        [((Q, wide), F32)],
    )
    state_partner = [core_swap(half) for half in both[2:]]
    through_partner = core_swap(through)
    mine, other = column_call(
        own_kernel, CHIP, ids, incoming, [], span, [((Q, span // 2), BF)] * 2, after=[through]
    )
    partner = core_swap(other)
    before = []
    for hop in range(1, chips):
        total, = call(
            functools.partial(chip_total_kernel, 1, 2),
            (),
            (through, through_partner, *both[:2], *state_partner, *before),
            [((N, wide), BF)],
            after=[local_output] if hop == 1 else (),
        )
        before = [lax.ppermute(total, "seq", [(i, i + 2) for i in range(seq - 2)])]
    results = call(
        functools.partial(output_kernel, starts),
        (),
        (through, local_output, c_rows, log_cols, through_partner, *before, *state_partner),
        [((Q, width), BF) for width in widths] + [((N, width), BF) for width in widths],
        after=[partner],
    )
    outputs, states = results[: len(widths)], results[len(widths) :]
    swapped = [core_swap(output) for output in outputs]
    outputs = [[output] + [chip_shift(output, by) for by in range(1, chips)] for output in outputs]

    came = call(
        assemble_kernel, (), (through, *pieces), [(((chips - 1) * Q, depth), BF)] * 4, after=[outputs[-1][0]],
    )
    partner_came = [core_swap(block) for block in came[2:]]
    weight_late = later(weight_other, outputs[-1][0])
    weights = [out_weight, weight_other, weight_core]
    weights += [core_swap(weight_late[: depth // 2]), core_swap(weight_late[depth // 2 :])]

    partials = call(
        head_partial_kernel,
        (),
        (mine, other, *came, *weights),
        [((Q, wide), F32)] + [((Q, wide), BF)] * (chips - 1),
    )
    returned = [chip_shift(partials[by], -by) for by in range(1, chips)]

    sent, kept, sums = [], [], []
    for part, width in enumerate(widths):
        pieces = [later(piece, sent[-1] if sent else partials[0]) for piece in outputs[part][1:]]
        cut = width // 2 if width > wide // 2 else width
        swaps = [core_swap(piece[:, at : at + cut]) for piece in pieces for at in range(0, width, cut)]
        sizes = [width]
        partial, *own = call(
            functools.partial(weight_partial_kernel, chips, len(sizes)),
            (),
            (mine, partner, *came[:2], *partner_came, *outputs[part], swapped[part], *swaps),
            [((depth, width), F32)] + [((depth, size), BF) for size in sizes],
            after=[partials[0], *sent[-1:]],
        )
        sent.append(own[0])
        kept.append(partial)
        sums += [dialogue_swap(value) for value in own]

    head_grad, weighted_grad, *both = call(
        functools.partial(adjoint_kernel, chips - 1),
        (),
        (through, partials[0], *returned, c_rows, log_cols),
        [((Q, wide), BF), ((Q, wide), BF)] + [((N, wide // 2), F32)] * 2 + [((N, wide), BF)],
        after=[sums[0], *sent],
    )
    adjoint_partner = core_swap(both[2])
    local_in, paired, c_part = call(
        local_grads_kernel,
        (),
        (through, x, head_grad, b_rows, c_rows, log_rows, log_cols, weighted_grad, *states),
        [((Q, wide), F32), ((Q, Q), F32), ((Q, N), F32)],
    )
    entering = []
    for hop in range(1, chips):
        total, = call(
            functools.partial(chip_total_kernel, 0, 1),
            (),
            (through, through_partner, *both[:2], adjoint_partner, *entering),
            [((N, wide // 2), BF)],
        )
        entering = [lax.ppermute(total, "seq", [(i, i - 2) for i in range(2, seq)])]
    grad_b, grad_c = call(
        group_sums_kernel,
        (),
        (b_rows, c_rows, paired, c_part),
        [((Q, N), F32), ((Q, N), F32)],
    )
    grad_in, grad_b, token = call(
        final_kernel,
        (),
        (through, b_rows, log_cols, grad_b, weighted_in, through_partner, local_in)
        + (*entering, core_swap(later(entering[0], grad_c)), adjoint_partner),
        [((Q, wide), BF), ((Q, N), F32), ((8, 128), F32)],
    )
    grad_weight, = call(
        functools.partial(add_kernel, len(widths)),
        (),
        (*kept, *sums),
        [((depth, wide), F32)],
        after=[token],
    )
    return grad_in[None], grad_b[None], grad_c[None], grad_weight


def solution(mesh):
    in_specs = (
        P("dp", "seq", "tensor"),
        P("dp", "seq", "tensor"),
        P("dp", "seq", "tensor"),
        P("dp", "tensor", "seq"),
        P("tensor"),
        P("tensor"),
        P("dp", "seq"),
        P("dp", "seq", None),
        P(("seq", "dp"), "tensor"),
    )
    out_specs = (
        P("dp", "seq", "tensor"),
        P("dp", "seq", "tensor"),
        P("dp", "seq", "tensor"),
        P(("seq", "dp"), "tensor"),
    )
    return jax.shard_map(body, mesh=mesh, in_specs=in_specs, out_specs=out_specs, check_vma=False)
```

```python
import functools

import jax
import jax.numpy as jnp
from jax import lax
from jax.experimental import pallas as pl
from jax.experimental.pallas import tpu as pltpu
from jax.sharding import PartitionSpec as P

P_SIZE = 64
N = 128
Q = 256
HALF = 128
PAIR = 2 * P_SIZE
SHARES = (6, 10)
PARITY, CORE, ODD, CHIP = 4, 6, 7, 8
THROUGH, KEEP, CORE_ROW, SKIP, ODD_ROW = (slice(row, row + 1) for row in range(5))
BF = jnp.bfloat16
F32 = jnp.float32

SMEM = pl.BlockSpec(memory_space=pltpu.SMEM)
ANY = pl.BlockSpec(memory_space=pl.ANY)
FREE = pl.CostEstimate(flops=0, bytes_accessed=0, transcendentals=0)
LIMIT = pltpu.CompilerParams(vmem_limit_bytes=16 * 2**20)


def name_of(kernel):
    return getattr(kernel, "func", kernel).__name__


def whole(shape):
    return pl.BlockSpec(shape, lambda *_: (0,) * len(shape))


def call(kernel, scalars, arrays, outs, after=(), aliases=None):
    pairs = [item if isinstance(item, tuple) else (item, whole(item.shape)) for item in arrays]
    outs = [item if len(item) == 3 else (*item, whole(item[0])) for item in outs]
    count = len(scalars)
    views = [item.view if isinstance(item, Ids) else (lambda ref: ref) for item in scalars]
    scalars = [item.number if isinstance(item, Ids) else item for item in scalars]

    def run(*refs):
        seen = [view(ref) for view, ref in zip(views, refs)]
        kernel(*seen, *refs[count : count + len(pairs)], *refs[count + len(pairs) + len(after) :])

    return pl.pallas_call(
        run,
        grid=(1,),
        out_shape=[jax.ShapeDtypeStruct(shape, kind) for shape, kind, _ in outs],
        in_specs=[SMEM] * count + [spec for _, spec in pairs] + [ANY] * len(after),
        out_specs=[spec for _, _, spec in outs],
        input_output_aliases=aliases or {},
        cost_estimate=FREE,
        compiler_params=LIMIT,
        name=name_of(kernel),
    )(*scalars, *[array for array, _ in pairs], *after)


class Ids:
    def __init__(self, number, chips, planes, dp):
        self.number, self.sizes = number, (chips, planes, dp)

    def view(self, ref):
        seen = Ids(None, *self.sizes)
        seen.ref = ref
        return seen

    def __getitem__(self, place):
        chips, planes, dp = self.sizes
        at = self.ref[0]
        chip, core, odd, dialogue = at // (2 * planes * dp), at // (planes * dp) % 2, at // dp % 2, at % dp
        if place >= CHIP:
            return (chip + place - CHIP) % chips
        if place in (CORE, ODD):
            return core if place == CORE else odd
        if place >= PARITY:
            half, second = place - PARITY, odd
        else:
            half, second = place // 2, place % 2
        own = core if half == 0 else 1 - core
        return own * 2 + (dialogue + second) % 2


def column_call(kernel, at, ids, grads, others, span, outs, after=()):
    def run(ids_ref, *refs):
        kernel(ids.view(ids_ref), *refs[: 1 + len(others)], *refs[1 + len(others) + len(after) :])

    return pl.pallas_call(
        run,
        out_shape=[jax.ShapeDtypeStruct(shape, kind) for shape, kind in outs],
        grid_spec=pltpu.PrefetchScalarGridSpec(
            num_scalar_prefetch=1,
            grid=(1,),
            in_specs=[pl.BlockSpec((Q, span), lambda i, ids_ref: (0, ids.view(ids_ref)[at]))]
            + [whole(other.shape) for other in others]
            + [ANY] * len(after),
            out_specs=[whole(shape) for shape, _ in outs],
        ),
        cost_estimate=FREE,
        compiler_params=LIMIT,
        name=name_of(kernel),
    )(ids.number, grads, *others, *after)


def dot(a, b, left, right):
    return lax.dot_general(a, b, (((left,), (right,)), ((), ())), preferred_element_type=F32)


def first_head(rows=Q):
    return lax.broadcasted_iota(jnp.int32, (rows, PAIR), 1) < P_SIZE


def spread(table, pair, first):
    return jnp.where(first, table[:, 2 * pair : 2 * pair + 1], table[:, 2 * pair + 1 : 2 * pair + 2])


def gains(skip_ref, head):
    first = lax.broadcasted_iota(jnp.int32, (1, PAIR), 1) < P_SIZE
    return jnp.where(first, skip_ref[head], skip_ref[head + 1])


def tables_kernel(
    ids_ref, rate_ref, resets_ref, skip_ref, x_ref, b_ref, step_ref, *refs
):
    states, sent, (weighted_ref, rows_ref, cols_ref, table_ref, from_ref, end_ref) = refs[:2], refs[2:4], refs[4:]
    heads = step_ref.shape[0]
    keep = (1 - resets_ref[0, 0]).astype(F32)
    head_id = lax.broadcasted_iota(jnp.int32, (heads, Q), 0)
    lane = lax.broadcasted_iota(jnp.int32, (heads, Q), 1)
    rate = jnp.zeros((heads, Q), F32)
    for head in range(heads):
        rate = jnp.where(head_id == head, rate_ref[head], rate)
    log = -step_ref[...] * rate
    shift = 1
    while shift < Q:
        log = log + jnp.where(lane >= shift, pltpu.roll(log, shift, 1), 0.0)
        shift *= 2
    rows_ref[...] = log
    cols = log.T
    cols_ref[...] = cols
    first = first_head()
    for pair in range(heads // 2):
        at = slice(pair * PAIR, (pair + 1) * PAIR)
        log_pair = spread(cols, pair, first)
        last = log_pair[Q - 1 : Q, :]
        to_end = jnp.exp(last - log_pair)
        end_ref[:, at] = to_end
        from_ref[:, at] = jnp.exp(log_pair)
        weighted_ref[:, at] = (x_ref[:, at].astype(F32) * to_end).astype(BF)
        table_ref[THROUGH, at] = keep * jnp.exp(last)
        table_ref[SKIP, at] = gains(skip_ref, 2 * pair)
    ones = jnp.ones((1, table_ref.shape[1]), F32)
    table_ref[KEEP, :] = keep * ones
    table_ref[CORE_ROW, :] = ids_ref[CORE].astype(F32) * ones
    table_ref[ODD_ROW, :] = ids_ref[ODD].astype(F32) * ones
    table_ref[5:, :] = jnp.zeros((3, table_ref.shape[1]), F32)
    state = dot(b_ref[...], weighted_ref[...], 0, 0)
    middle = state.shape[1] // 2
    for number in range(2):
        half = state[:, number * middle : (number + 1) * middle]
        states[number][...] = half
        sent[number][...] = half.astype(BF)


def local_output_kernel(table_ref, x_ref, b_ref, c_ref, rows_ref, cols_ref, out_ref):
    heads = rows_ref.shape[0]
    scores = dot(c_ref[...], b_ref[...], 1, 1)
    at_row = lax.broadcasted_iota(jnp.int32, (HALF, HALF), 0)
    at_lane = lax.broadcasted_iota(jnp.int32, (HALF, HALF), 1)
    causal = at_row >= at_lane
    first = first_head()
    zero = jnp.zeros((Q, PAIR), BF)
    for pair in range(heads // 2):
        at = slice(pair * PAIR, (pair + 1) * PAIR)
        x_pair = x_ref[:, at]
        skip = table_ref[SKIP, at] * x_pair.astype(F32)
        top, bottom = skip[:HALF], skip[HALF:]
        for side in range(2):
            head = 2 * pair + side
            x_head = jnp.where(first, x_pair, zero) if side == 0 else jnp.where(first, zero, x_pair)
            col = cols_ref[:, head : head + 1]
            row = rows_ref[head : head + 1, :]

            def mix(i, j):
                span = col[i * HALF : (i + 1) * HALF] - row[:, j * HALF : (j + 1) * HALF]
                weight = jnp.exp(jnp.minimum(span, 0.0))
                if i == j:
                    weight = jnp.where(causal, weight, 0.0)
                return (weight * scores[i * HALF : (i + 1) * HALF, j * HALF : (j + 1) * HALF]).astype(BF)

            top += dot(mix(0, 0), x_head[:HALF], 1, 0)
            bottom += dot(jnp.concatenate([mix(1, 0), mix(1, 1)], axis=1), x_head, 1, 0)
        out_ref[:HALF, at] = top
        out_ref[HALF:, at] = bottom


def output_kernel(starts, table_ref, local_ref, c_ref, from_ref, through_ref, before_ref, *refs):
    partners, outs, states = refs[:2], refs[2 : 2 + len(starts)], refs[2 + len(starts) :]
    partner = jnp.concatenate([ref[...] for ref in partners], axis=1)
    for start, out_ref, state_ref in zip(starts, outs, states):
        part = slice(start, start + out_ref.shape[1])
        before = before_ref[:, part].astype(F32)
        after = through_ref[THROUGH, part] * before + partner[:, part].astype(F32)
        state = jnp.where(table_ref[CORE_ROW, part] == 1.0, after, before)
        state_ref[...] = (table_ref[KEEP, part] * state).astype(BF)
        for pair in range(out_ref.shape[1] // PAIR):
            at = slice(pair * PAIR, (pair + 1) * PAIR)
            whole = slice(start + pair * PAIR, start + (pair + 1) * PAIR)
            term = dot(c_ref[...], state_ref[:, at], 1, 0)
            out_ref[:, at] = (local_ref[:, whole] + from_ref[:, whole] * term).astype(BF)


def block_of(ids_ref, grad_ref, slot):
    depth = grad_ref.shape[1] // 4
    return grad_ref[:, pl.ds(pl.multiple_of(ids_ref[slot] * depth, depth), depth)]


def send_kernel(ids_ref, grad_ref, out_ref):
    depth = out_ref.shape[1] // 2
    for half in range(2):
        out_ref[:, half * depth : (half + 1) * depth] = block_of(ids_ref, grad_ref, PARITY + half)


def own_kernel(ids_ref, grad_ref, *halves):
    depth = halves[0].shape[1] // 2
    for slot in range(4):
        halves[slot // 2][:, slot % 2 * depth : (slot % 2 + 1) * depth] = block_of(ids_ref, grad_ref, slot)


def assemble_kernel(table_ref, *refs):
    pieces, blocks = refs[:-4], refs[-4:]
    depth = blocks[0].shape[1]
    even = table_ref[ODD_ROW, :depth] == 0.0
    for number, out_ref in enumerate(blocks):
        taken = slice(number // 2 * depth, (number // 2 + 1) * depth)
        for other in range(len(pieces) // 2):
            near, far = pieces[2 * other], pieces[2 * other + 1]
            first, second = (near, far) if number % 2 == 0 else (far, near)
            rows = slice(other * Q, (other + 1) * Q)
            out_ref[rows, :] = jnp.where(even, first[:, taken], second[:, taken])


def head_partial_kernel(mine_ref, other_ref, *refs):
    came, weights, outs = refs[:4], refs[4:9], refs[9:]
    depth = weights[0].shape[0]
    middle = weights[3].shape[0]
    for number in reversed(range(len(outs))):
        total = None
        for block in range(4):
            rows = slice((number - 1) * Q, number * Q)
            if number == 0:
                grad = (mine_ref, other_ref)[block // 2][:, block % 2 * depth : (block % 2 + 1) * depth]
            else:
                grad = came[block][rows, :]
            if block < 3:
                term = dot(grad, weights[block][...], 1, 0)
            else:
                term = dot(grad[:, :middle], weights[3][...], 1, 0) + dot(grad[:, middle:], weights[4][...], 1, 0)
            total = term if total is None else total + term
        outs[number][...] = total.astype(outs[number].dtype)


def adjoint_kernel(others, table_ref, own_ref, *refs):
    parts, (c_ref, from_ref, head_ref, weighted_ref, *halves) = refs[:others], refs[others:]
    for pair in range(head_ref.shape[1] // PAIR):
        at = slice(pair * PAIR, (pair + 1) * PAIR)
        total = own_ref[:, at]
        for part in parts:
            total = total + part[:, at].astype(F32)
        head = total.astype(BF)
        head_ref[:, at] = head
        weighted_ref[:, at] = (head.astype(F32) * from_ref[:, at]).astype(BF)
    adjoint = table_ref[KEEP, :] * dot(c_ref[...], weighted_ref[...], 0, 0)
    middle = adjoint.shape[1] // 2
    for number in range(2):
        half = adjoint[:, number * middle : (number + 1) * middle]
        halves[number][...] = half
        halves[2][:, number * middle : (number + 1) * middle] = half.astype(BF)


def chip_total_kernel(last, parts, through_ref, partner_through_ref, *refs):
    owns, partners, entering, out_ref = refs[:2], refs[2 : 2 + parts], refs[2 + parts : -1], refs[-1]
    width = owns[0].shape[1]
    halved = out_ref.shape[1] < 2 * width
    partner_state = jnp.concatenate([ref[...] for ref in partners], axis=1)
    totals = []
    for part in range(2):
        at = slice(part * width, (part + 1) * width)
        own, partner = owns[part][...], partner_state[:, at].astype(F32)
        mine, theirs = through_ref[THROUGH, at], partner_through_ref[THROUGH, at]
        leaves = through_ref[CORE_ROW, at] == float(last)
        total = jnp.where(leaves, mine * partner + own, theirs * own + partner)
        for value in entering:
            came = value[...] if halved else value[:, at]
            total += mine * theirs * came.astype(F32)
        if halved:
            totals.append(total)
        else:
            out_ref[:, at] = total.astype(BF)
    if halved:
        first_core = through_ref[CORE_ROW, :width] == 0.0
        out_ref[...] = jnp.where(first_core, totals[0], totals[1]).astype(BF)


def local_grads_kernel(
    table_ref, x_ref, grad_ref, b_ref, c_ref, rows_ref, cols_ref, weighted_ref, *refs
):
    states, (in_ref, paired_ref, c_out_ref) = refs[:-3], refs[-3:]
    heads = x_ref.shape[1] // P_SIZE
    scores = dot(b_ref[...], c_ref[...], 1, 1)
    at_row = lax.broadcasted_iota(jnp.int32, (HALF, HALF), 0)
    at_lane = lax.broadcasted_iota(jnp.int32, (HALF, HALF), 1)
    causal = at_lane >= at_row
    first = first_head()
    zero = jnp.zeros((Q, PAIR), BF)
    paired_ref[...] = jnp.zeros_like(paired_ref)
    for pair in range(heads // 2):
        at = slice(pair * PAIR, (pair + 1) * PAIR)
        x_pair = x_ref[:, at]
        g_pair = grad_ref[:, at]
        skip = table_ref[SKIP, at] * g_pair.astype(F32)
        top, bottom = skip[:HALF], skip[HALF:]
        for side in range(2):
            head = 2 * pair + side
            g_head = jnp.where(first, g_pair, zero) if side == 0 else jnp.where(first, zero, g_pair)
            col = cols_ref[:, head : head + 1]
            row = rows_ref[head : head + 1, :]

            def weigh(j, i):
                span = row[:, i * HALF : (i + 1) * HALF] - col[j * HALF : (j + 1) * HALF]
                weight = jnp.exp(jnp.minimum(span, 0.0))
                return jnp.where(causal, weight, 0.0) if i == j else weight

            early = jnp.concatenate([weigh(0, 0), weigh(0, 1)], axis=1)
            late = weigh(1, 1)
            top += dot((early * scores[:HALF]).astype(BF), g_head, 1, 0)
            bottom += dot((late * scores[HALF:, HALF:]).astype(BF), g_head[HALF:], 1, 0)
            paired_ref[:HALF, :] += early * dot(x_pair[:HALF], g_head, 1, 1)
            paired_ref[HALF:, HALF:] += late * dot(x_pair[HALF:], g_head[HALF:], 1, 1)
        in_ref[:HALF, at] = top
        in_ref[HALF:, at] = bottom
    start, total = 0, None
    for state in states:
        width = state.shape[1]
        term = dot(weighted_ref[:, start : start + width], state[...], 1, 1)
        total = term if total is None else total + term
        start += width
    c_out_ref[...] = total


def group_sums_kernel(b_ref, c_ref, paired_ref, c_part_ref, grad_b_ref, grad_c_ref):
    paired = paired_ref[...].astype(BF)
    grad_b_ref[...] = dot(paired, c_ref[...], 1, 0)
    grad_c_ref[...] = c_part_ref[...] + dot(paired, b_ref[...], 0, 0)


def final_kernel(table_ref, b_ref, end_ref, sums_ref, weighted_ref, through_ref, local_ref, *refs):
    entered, partner_ref, (in_ref, grad_b_ref, token_ref) = refs[:2], refs[2], refs[3:]
    token_ref[...] = jnp.zeros_like(token_ref)
    grad_b = sums_ref[...]
    width = partner_ref.shape[1] // 2
    for half in range(2):
        here = slice(half * width, (half + 1) * width)
        core = table_ref[CORE_ROW, here]
        entering = jnp.where(core == float(half), entered[0][...].astype(F32), entered[1][...].astype(F32))
        inner = through_ref[THROUGH, here] * entering + partner_ref[:, here].astype(F32)
        adjoint = jnp.where(core == 1.0, entering, inner).astype(BF)
        grad_b += dot(weighted_ref[:, here], adjoint, 1, 1)
        for number in range(width // PAIR):
            pair = half * (width // PAIR) + number
            at = slice(pair * PAIR, (pair + 1) * PAIR)
            term = dot(b_ref[...], adjoint[:, number * PAIR : (number + 1) * PAIR], 1, 0)
            in_ref[:, at] = (local_ref[:, at] + end_ref[:, at] * term).astype(BF)
    grad_b_ref[...] = grad_b


def add_kernel(parts, *refs):
    kept, came, out_ref = refs[:parts], refs[parts:-1], refs[-1]
    for group, change in ((kept, False), (came, True)):
        start = 0
        for ref in group:
            at = slice(start, start + ref.shape[1])
            out_ref[:, at] = out_ref[:, at] + ref[...].astype(F32) if change else ref[...]
            start += ref.shape[1]


def weight_partial_kernel(chips, pieces, *refs):
    owns, came, refs = refs[:2], (refs[2:4], refs[4:6]), refs[6:]
    outputs, kept_ref, sent = refs[: -1 - pieces], refs[-1 - pieces], refs[-pieces:]
    depth = kept_ref.shape[0]
    outputs = [ref[...] for ref in outputs]
    if len(outputs) > 2 * chips:
        cut = outputs[chips + 1 :]
        outputs = outputs[: chips + 1] + [jnp.concatenate(cut[i : i + 2], axis=1) for i in range(0, len(cut), 2)]
    for slot in (1, 0):
        total = None
        for number, output in enumerate(outputs):
            core, by = number // chips, number % chips
            if by == 0:
                grad = owns[core][:, slot * depth : (slot + 1) * depth]
            else:
                grad = came[core][slot][(by - 1) * Q : by * Q, :]
            term = dot(grad, output, 0, 0)
            total = term if total is None else total + term
        if slot == 0:
            kept_ref[...] = total
            continue
        start = 0
        for ref in sent:
            ref[...] = total[:, start : start + ref.shape[1]].astype(BF)
            start += ref.shape[1]


def body(
    ssm_input, b_input, c_input, step_size, decay_rate, skip_gain, resets, out_grad, out_weight
):
    seq, dp, planes = lax.axis_size("seq"), lax.axis_size("dp"), lax.axis_size("tensor")
    chips = seq // 2
    me = lax.axis_index(("seq", "tensor", "dp"))
    heads = decay_rate.shape[0]
    wide = heads * P_SIZE
    widths = [wide * share // sum(SHARES) // PAIR * PAIR for share in SHARES]
    starts = [sum(widths[:part]) for part in range(len(widths))]
    depth = out_weight.shape[0]
    span = 4 * depth
    assert ssm_input.shape[1] == Q and dp == 2 and seq % 2 == 0 and seq > 2 and planes % 2 == 0
    def later(value, other):
        return lax.optimization_barrier((value, other))[0]

    across = [(i, i ^ 1) for i in range(seq)]

    def core_swap(value):
        return lax.ppermute(value, "seq", across)

    def chip_shift(value, by):
        return lax.ppermute(value, "seq", [(i, (i + 2 * by) % seq) for i in range(seq)])

    def plane_swap(value):
        return lax.ppermute(value, "tensor", [(i, i ^ 1) for i in range(planes)])

    def dialogue_swap(value):
        return lax.ppermute(value, "dp", [(0, 1), (1, 0)])

    x, b_rows, c_rows, steps, incoming = (
        ssm_input[0], b_input[0], c_input[0], step_size[0], out_grad[0]
    )
    ids = Ids(me.astype(jnp.int32).reshape(1), chips, planes, dp)

    to_send = [
        column_call(send_kernel, CHIP + by, ids, incoming, [], span, [((Q, 2 * depth), BF)])
        for by in range(1, chips)
    ]

    weight_other = dialogue_swap(out_weight)
    weight_core = core_swap(out_weight)

    near = [chip_shift(to_send[by - 1][0], by) for by in range(1, chips)]
    pieces = []
    for piece in near:
        pieces += [piece, plane_swap(piece)]

    *both, weighted_in, log_rows, log_cols, through, from_start, to_end = call(
        tables_kernel,
        (ids, decay_rate, resets, skip_gain),
        (x, b_rows, steps),
        [((N, wide // 2), F32)] * 2 + [((N, wide // 2), BF)] * 2 + [((Q, wide), BF)]
        + [((heads, Q), F32), ((Q, heads), F32), ((8, wide), F32)]
        + [((Q, wide), F32)] * 2,
        after=[weight_core, *[sent[0] for sent in to_send]],
    )
    local_output, = call(
        local_output_kernel,
        (),
        (through, x, b_rows, c_rows, log_rows, log_cols),
        [((Q, wide), F32)],
    )
    state_partner = [core_swap(half) for half in both[2:]]
    through_partner = core_swap(through)
    mine, other = column_call(
        own_kernel, CHIP, ids, incoming, [], span, [((Q, span // 2), BF)] * 2, after=[through]
    )
    partner = core_swap(other)
    before = []
    for hop in range(1, chips):
        total, = call(
            functools.partial(chip_total_kernel, 1, 2),
            (),
            (through, through_partner, *both[:2], *state_partner, *before),
            [((N, wide), BF)],
            after=[local_output] if hop == 1 else (),
        )
        before = [lax.ppermute(total, "seq", [(i, i + 2) for i in range(seq - 2)])]
    results = call(
        functools.partial(output_kernel, starts),
        (),
        (through, local_output, c_rows, from_start, through_partner, *before, *state_partner),
        [((Q, width), BF) for width in widths] + [((N, width), BF) for width in widths],
        after=[partner],
    )
    outputs, states = results[: len(widths)], results[len(widths) :]
    swapped = [core_swap(output) for output in outputs]
    outputs = [[output] + [chip_shift(output, by) for by in range(1, chips)] for output in outputs]

    came = call(
        assemble_kernel, (), (through, *pieces), [(((chips - 1) * Q, depth), BF)] * 4, after=[outputs[-1][0]],
    )
    partner_came = [core_swap(block) for block in came[2:]]
    weight_late = later(weight_other, outputs[-1][0])
    weights = [out_weight, weight_other, weight_core]
    weights += [core_swap(weight_late[: depth // 2]), core_swap(weight_late[depth // 2 :])]

    partials = call(
        head_partial_kernel,
        (),
        (mine, other, *came, *weights),
        [((Q, wide), F32)] + [((Q, wide), BF)] * (chips - 1),
    )
    returned = [chip_shift(partials[by], -by) for by in range(1, chips)]

    sent, kept, sums = [], [], []
    for part, width in enumerate(widths):
        pieces = [later(piece, sent[-1] if sent else partials[0]) for piece in outputs[part][1:]]
        cut = width // 2 if width > wide // 2 else width
        swaps = [core_swap(piece[:, at : at + cut]) for piece in pieces for at in range(0, width, cut)]
        sizes = [width]
        partial, *own = call(
            functools.partial(weight_partial_kernel, chips, len(sizes)),
            (),
            (mine, partner, *came[:2], *partner_came, *outputs[part], swapped[part], *swaps),
            [((depth, width), F32)] + [((depth, size), BF) for size in sizes],
            after=[partials[0], *sent[-1:]],
        )
        sent.append(own[0])
        kept.append(partial)
        sums += [dialogue_swap(value) for value in own]

    head_grad, weighted_grad, *both = call(
        functools.partial(adjoint_kernel, chips - 1),
        (),
        (through, partials[0], *returned, c_rows, from_start),
        [((Q, wide), BF), ((Q, wide), BF)] + [((N, wide // 2), F32)] * 2 + [((N, wide), BF)],
        after=[sums[0], *sent],
    )
    adjoint_partner = core_swap(both[2])
    local_in, paired, c_part = call(
        local_grads_kernel,
        (),
        (through, x, head_grad, b_rows, c_rows, log_rows, log_cols, weighted_grad, *states),
        [((Q, wide), F32), ((Q, Q), F32), ((Q, N), F32)],
    )
    entering = []
    for hop in range(1, chips):
        total, = call(
            functools.partial(chip_total_kernel, 0, 1),
            (),
            (through, through_partner, *both[:2], adjoint_partner, *entering),
            [((N, wide // 2), BF)],
        )
        entering = [lax.ppermute(total, "seq", [(i, i - 2) for i in range(2, seq)])]
    grad_b, grad_c = call(
        group_sums_kernel,
        (),
        (b_rows, c_rows, paired, c_part),
        [((Q, N), F32), ((Q, N), F32)],
    )
    grad_in, grad_b, token = call(
        final_kernel,
        (),
        (through, b_rows, to_end, grad_b, weighted_in, through_partner, local_in)
        + (*entering, core_swap(later(entering[0], grad_c)), adjoint_partner),
        [((Q, wide), BF), ((Q, N), F32), ((8, 128), F32)],
    )
    grad_weight, = call(
        functools.partial(add_kernel, len(widths)),
        (),
        (*kept, *sums),
        [((depth, wide), F32)],
        after=[token],
    )
    return grad_in[None], grad_b[None], grad_c[None], grad_weight


def solution(mesh):
    in_specs = (
        P("dp", "seq", "tensor"),
        P("dp", "seq", "tensor"),
        P("dp", "seq", "tensor"),
        P("dp", "tensor", "seq"),
        P("tensor"),
        P("tensor"),
        P("dp", "seq"),
        P("dp", "seq", None),
        P(("seq", "dp"), "tensor"),
    )
    out_specs = (
        P("dp", "seq", "tensor"),
        P("dp", "seq", "tensor"),
        P("dp", "seq", "tensor"),
        P(("seq", "dp"), "tensor"),
    )
    return jax.shard_map(body, mesh=mesh, in_specs=in_specs, out_specs=out_specs, check_vma=False)
```

```python
import functools

import jax
import jax.numpy as jnp
from jax import lax
from jax.experimental import pallas as pl
from jax.experimental.pallas import tpu as pltpu
from jax.sharding import PartitionSpec as P

P_SIZE = 64
N = 128
Q = 256
HALF = 128
PAIR = 2 * P_SIZE
SHARES = (6, 10)
PARITY, CORE, ODD, CHIP = 4, 6, 7, 8
THROUGH, KEEP, CORE_ROW, SKIP, ODD_ROW = (slice(row, row + 1) for row in range(5))
BF = jnp.bfloat16
F32 = jnp.float32

SMEM = pl.BlockSpec(memory_space=pltpu.SMEM)
ANY = pl.BlockSpec(memory_space=pl.ANY)
FREE = pl.CostEstimate(flops=0, bytes_accessed=0, transcendentals=0)
LIMIT = pltpu.CompilerParams(vmem_limit_bytes=16 * 2**20)


def name_of(kernel):
    return getattr(kernel, "func", kernel).__name__


def whole(shape):
    return pl.BlockSpec(shape, lambda *_: (0,) * len(shape))


def call(kernel, scalars, arrays, outs, after=(), aliases=None):
    pairs = [item if isinstance(item, tuple) else (item, whole(item.shape)) for item in arrays]
    outs = [item if len(item) == 3 else (*item, whole(item[0])) for item in outs]
    count = len(scalars)
    views = [item.view if isinstance(item, Ids) else (lambda ref: ref) for item in scalars]
    scalars = [item.number if isinstance(item, Ids) else item for item in scalars]

    def run(*refs):
        seen = [view(ref) for view, ref in zip(views, refs)]
        kernel(*seen, *refs[count : count + len(pairs)], *refs[count + len(pairs) + len(after) :])

    return pl.pallas_call(
        run,
        grid=(1,),
        out_shape=[jax.ShapeDtypeStruct(shape, kind) for shape, kind, _ in outs],
        in_specs=[SMEM] * count + [spec for _, spec in pairs] + [ANY] * len(after),
        out_specs=[spec for _, _, spec in outs],
        input_output_aliases=aliases or {},
        cost_estimate=FREE,
        compiler_params=LIMIT,
        name=name_of(kernel),
    )(*scalars, *[array for array, _ in pairs], *after)


class Ids:
    def __init__(self, number, chips, planes, dp):
        self.number, self.sizes = number, (chips, planes, dp)

    def view(self, ref):
        seen = Ids(None, *self.sizes)
        seen.ref = ref
        return seen

    def __getitem__(self, place):
        chips, planes, dp = self.sizes
        at = self.ref[0]
        chip, core, odd, dialogue = at // (2 * planes * dp), at // (planes * dp) % 2, at // dp % 2, at % dp
        if place >= CHIP:
            return (chip + place - CHIP) % chips
        if place in (CORE, ODD):
            return core if place == CORE else odd
        if place >= PARITY:
            half, second = place - PARITY, odd
        else:
            half, second = place // 2, place % 2
        own = core if half == 0 else 1 - core
        return own * 2 + (dialogue + second) % 2


def column_call(kernel, at, ids, grads, others, span, outs, after=()):
    def run(ids_ref, *refs):
        kernel(ids.view(ids_ref), *refs[: 1 + len(others)], *refs[1 + len(others) + len(after) :])

    return pl.pallas_call(
        run,
        out_shape=[jax.ShapeDtypeStruct(shape, kind) for shape, kind in outs],
        grid_spec=pltpu.PrefetchScalarGridSpec(
            num_scalar_prefetch=1,
            grid=(1,),
            in_specs=[pl.BlockSpec((Q, span), lambda i, ids_ref: (0, ids.view(ids_ref)[at]))]
            + [whole(other.shape) for other in others]
            + [ANY] * len(after),
            out_specs=[whole(shape) for shape, _ in outs],
        ),
        cost_estimate=FREE,
        compiler_params=LIMIT,
        name=name_of(kernel),
    )(ids.number, grads, *others, *after)


def dot(a, b, left, right):
    return lax.dot_general(a, b, (((left,), (right,)), ((), ())), preferred_element_type=F32)


def first_head(rows=Q):
    return lax.broadcasted_iota(jnp.int32, (rows, PAIR), 1) < P_SIZE


def spread(table, pair, first):
    return jnp.where(first, table[:, 2 * pair : 2 * pair + 1], table[:, 2 * pair + 1 : 2 * pair + 2])


def gains(skip_ref, head):
    first = lax.broadcasted_iota(jnp.int32, (1, PAIR), 1) < P_SIZE
    return jnp.where(first, skip_ref[head], skip_ref[head + 1])


def tables_kernel(
    ids_ref, rate_ref, resets_ref, skip_ref, x_ref, b_ref, step_ref, *refs
):
    states, sent, (weighted_ref, rows_ref, cols_ref, table_ref, from_ref, end_ref) = refs[:2], refs[2:4], refs[4:]
    heads = step_ref.shape[0]
    keep = (1 - resets_ref[0, 0]).astype(F32)
    head_id = lax.broadcasted_iota(jnp.int32, (heads, Q), 0)
    lane = lax.broadcasted_iota(jnp.int32, (heads, Q), 1)
    rate = jnp.zeros((heads, Q), F32)
    for head in range(heads):
        rate = jnp.where(head_id == head, rate_ref[head], rate)
    log = -step_ref[...] * rate
    shift = 1
    while shift < Q:
        log = log + jnp.where(lane >= shift, pltpu.roll(log, shift, 1), 0.0)
        shift *= 2
    rows_ref[...] = log
    cols = log.T
    cols_ref[...] = cols
    first = first_head()
    for pair in range(heads // 2):
        at = slice(pair * PAIR, (pair + 1) * PAIR)
        log_pair = spread(cols, pair, first)
        last = log_pair[Q - 1 : Q, :]
        to_end = jnp.exp(last - log_pair)
        end_ref[:, at] = to_end
        from_ref[:, at] = jnp.exp(log_pair)
        weighted_ref[:, at] = (x_ref[:, at].astype(F32) * to_end).astype(BF)
        table_ref[THROUGH, at] = keep * jnp.exp(last)
        table_ref[SKIP, at] = gains(skip_ref, 2 * pair)
    ones = jnp.ones((1, table_ref.shape[1]), F32)
    table_ref[KEEP, :] = keep * ones
    table_ref[CORE_ROW, :] = ids_ref[CORE].astype(F32) * ones
    table_ref[ODD_ROW, :] = ids_ref[ODD].astype(F32) * ones
    table_ref[5:, :] = jnp.zeros((3, table_ref.shape[1]), F32)
    state = dot(b_ref[...], weighted_ref[...], 0, 0)
    middle = state.shape[1] // 2
    for number in range(2):
        half = state[:, number * middle : (number + 1) * middle]
        states[number][...] = half
        sent[number][...] = half.astype(BF)


def local_output_kernel(table_ref, x_ref, b_ref, c_ref, rows_ref, cols_ref, out_ref):
    heads = rows_ref.shape[0]
    scores = dot(c_ref[...], b_ref[...], 1, 1)
    at_row = lax.broadcasted_iota(jnp.int32, (HALF, HALF), 0)
    at_lane = lax.broadcasted_iota(jnp.int32, (HALF, HALF), 1)
    causal = at_row >= at_lane
    first = first_head()
    zero = jnp.zeros((Q, PAIR), BF)
    for pair in range(heads // 2):
        at = slice(pair * PAIR, (pair + 1) * PAIR)
        x_pair = x_ref[:, at]
        skip = table_ref[SKIP, at] * x_pair.astype(F32)
        top, bottom = skip[:HALF], skip[HALF:]
        for side in range(2):
            head = 2 * pair + side
            x_head = jnp.where(first, x_pair, zero) if side == 0 else jnp.where(first, zero, x_pair)
            col = cols_ref[:, head : head + 1]
            row = rows_ref[head : head + 1, :]

            def mix(i, j):
                span = col[i * HALF : (i + 1) * HALF] - row[:, j * HALF : (j + 1) * HALF]
                weight = jnp.exp(jnp.minimum(span, 0.0))
                if i == j:
                    weight = jnp.where(causal, weight, 0.0)
                return (weight * scores[i * HALF : (i + 1) * HALF, j * HALF : (j + 1) * HALF]).astype(BF)

            top += dot(mix(0, 0), x_head[:HALF], 1, 0)
            bottom += dot(jnp.concatenate([mix(1, 0), mix(1, 1)], axis=1), x_head, 1, 0)
        out_ref[:HALF, at] = top
        out_ref[HALF:, at] = bottom


def output_kernel(starts, table_ref, local_ref, c_ref, from_ref, through_ref, before_ref, *refs):
    partners, outs, states = refs[:2], refs[2 : 2 + len(starts)], refs[2 + len(starts) :]
    partner = jnp.concatenate([ref[...] for ref in partners], axis=1)
    for start, out_ref, state_ref in zip(starts, outs, states):
        part = slice(start, start + out_ref.shape[1])
        before = before_ref[:, part].astype(F32)
        after = through_ref[THROUGH, part] * before + partner[:, part].astype(F32)
        state = jnp.where(table_ref[CORE_ROW, part] == 1.0, after, before)
        state_ref[...] = (table_ref[KEEP, part] * state).astype(BF)
        for pair in range(out_ref.shape[1] // PAIR):
            at = slice(pair * PAIR, (pair + 1) * PAIR)
            whole = slice(start + pair * PAIR, start + (pair + 1) * PAIR)
            term = dot(c_ref[...], state_ref[:, at], 1, 0)
            out_ref[:, at] = (local_ref[:, whole] + from_ref[:, whole] * term).astype(BF)


def block_of(ids_ref, grad_ref, slot):
    depth = grad_ref.shape[1] // 4
    return grad_ref[:, pl.ds(pl.multiple_of(ids_ref[slot] * depth, depth), depth)]


def send_kernel(ids_ref, grad_ref, out_ref):
    depth = out_ref.shape[1] // 2
    for half in range(2):
        out_ref[:, half * depth : (half + 1) * depth] = block_of(ids_ref, grad_ref, PARITY + half)


def own_kernel(ids_ref, grad_ref, *halves):
    depth = halves[0].shape[1] // 2
    for slot in range(4):
        halves[slot // 2][:, slot % 2 * depth : (slot % 2 + 1) * depth] = block_of(ids_ref, grad_ref, slot)


def assemble_kernel(table_ref, *refs):
    pieces, blocks = refs[:-4], refs[-4:]
    depth = blocks[0].shape[1]
    even = table_ref[ODD_ROW, :depth] == 0.0
    for number, out_ref in enumerate(blocks):
        taken = slice(number // 2 * depth, (number // 2 + 1) * depth)
        for other in range(len(pieces) // 2):
            near, far = pieces[2 * other], pieces[2 * other + 1]
            first, second = (near, far) if number % 2 == 0 else (far, near)
            rows = slice(other * Q, (other + 1) * Q)
            out_ref[rows, :] = jnp.where(even, first[:, taken], second[:, taken])


def head_partial_kernel(mine_ref, other_ref, *refs):
    came, weights, outs = refs[:4], refs[4:9], refs[9:]
    depth = weights[0].shape[0]
    middle = weights[3].shape[0]
    for number in reversed(range(len(outs))):
        total = None
        for block in range(4):
            rows = slice((number - 1) * Q, number * Q)
            if number == 0:
                grad = (mine_ref, other_ref)[block // 2][:, block % 2 * depth : (block % 2 + 1) * depth]
            else:
                grad = came[block][rows, :]
            if block < 3:
                term = dot(grad, weights[block][...], 1, 0)
            else:
                term = dot(grad[:, :middle], weights[3][...], 1, 0) + dot(grad[:, middle:], weights[4][...], 1, 0)
            total = term if total is None else total + term
        outs[number][...] = total.astype(outs[number].dtype)


def adjoint_kernel(others, table_ref, own_ref, *refs):
    parts, (c_ref, from_ref, head_ref, weighted_ref, *halves) = refs[:others], refs[others:]
    for pair in range(head_ref.shape[1] // PAIR):
        at = slice(pair * PAIR, (pair + 1) * PAIR)
        total = own_ref[:, at]
        for part in parts:
            total = total + part[:, at].astype(F32)
        head = total.astype(BF)
        head_ref[:, at] = head
        weighted_ref[:, at] = (head.astype(F32) * from_ref[:, at]).astype(BF)
    adjoint = table_ref[KEEP, :] * dot(c_ref[...], weighted_ref[...], 0, 0)
    middle = adjoint.shape[1] // 2
    for number in range(2):
        half = adjoint[:, number * middle : (number + 1) * middle]
        halves[number][...] = half
        halves[2][:, number * middle : (number + 1) * middle] = half.astype(BF)


def chip_total_kernel(last, parts, through_ref, partner_through_ref, *refs):
    owns, partners, entering, out_ref = refs[:2], refs[2 : 2 + parts], refs[2 + parts : -1], refs[-1]
    width = owns[0].shape[1]
    halved = out_ref.shape[1] < 2 * width
    partner_state = jnp.concatenate([ref[...] for ref in partners], axis=1)
    totals = []
    for part in range(2):
        at = slice(part * width, (part + 1) * width)
        own, partner = owns[part][...], partner_state[:, at].astype(F32)
        mine, theirs = through_ref[THROUGH, at], partner_through_ref[THROUGH, at]
        leaves = through_ref[CORE_ROW, at] == float(last)
        total = jnp.where(leaves, mine * partner + own, theirs * own + partner)
        for value in entering:
            came = value[...] if halved else value[:, at]
            total += mine * theirs * came.astype(F32)
        if halved:
            totals.append(total)
        else:
            out_ref[:, at] = total.astype(BF)
    if halved:
        first_core = through_ref[CORE_ROW, :width] == 0.0
        out_ref[...] = jnp.where(first_core, totals[0], totals[1]).astype(BF)


def local_grads_kernel(
    table_ref, x_ref, grad_ref, b_ref, c_ref, rows_ref, cols_ref, weighted_ref, *refs
):
    states, (in_ref, paired_ref, c_out_ref) = refs[:-3], refs[-3:]
    heads = x_ref.shape[1] // P_SIZE
    scores = dot(b_ref[...], c_ref[...], 1, 1)
    at_row = lax.broadcasted_iota(jnp.int32, (HALF, HALF), 0)
    at_lane = lax.broadcasted_iota(jnp.int32, (HALF, HALF), 1)
    causal = at_lane >= at_row
    first = first_head()
    zero = jnp.zeros((Q, PAIR), BF)
    paired_ref[...] = jnp.zeros_like(paired_ref)
    for pair in range(heads // 2):
        at = slice(pair * PAIR, (pair + 1) * PAIR)
        x_pair = x_ref[:, at]
        g_pair = grad_ref[:, at]
        skip = table_ref[SKIP, at] * g_pair.astype(F32)
        top, bottom = skip[:HALF], skip[HALF:]
        for side in range(2):
            head = 2 * pair + side
            g_head = jnp.where(first, g_pair, zero) if side == 0 else jnp.where(first, zero, g_pair)
            col = cols_ref[:, head : head + 1]
            row = rows_ref[head : head + 1, :]

            def weigh(j, i):
                span = row[:, i * HALF : (i + 1) * HALF] - col[j * HALF : (j + 1) * HALF]
                weight = jnp.exp(jnp.minimum(span, 0.0))
                return jnp.where(causal, weight, 0.0) if i == j else weight

            early = jnp.concatenate([weigh(0, 0), weigh(0, 1)], axis=1)
            late = weigh(1, 1)
            top += dot((early * scores[:HALF]).astype(BF), g_head, 1, 0)
            bottom += dot((late * scores[HALF:, HALF:]).astype(BF), g_head[HALF:], 1, 0)
            paired_ref[:HALF, :] += early * dot(x_pair[:HALF], g_head, 1, 1)
            paired_ref[HALF:, HALF:] += late * dot(x_pair[HALF:], g_head[HALF:], 1, 1)
        in_ref[:HALF, at] = top
        in_ref[HALF:, at] = bottom
    start, total = 0, None
    for state in states:
        width = state.shape[1]
        term = dot(weighted_ref[:, start : start + width], state[...], 1, 1)
        total = term if total is None else total + term
        start += width
    c_out_ref[...] = total


def group_sums_kernel(b_ref, c_ref, paired_ref, c_part_ref, grad_b_ref, grad_c_ref):
    paired = paired_ref[...].astype(BF)
    grad_b_ref[...] = dot(paired, c_ref[...], 1, 0)
    grad_c_ref[...] = c_part_ref[...] + dot(paired, b_ref[...], 0, 0)


def final_kernel(table_ref, b_ref, end_ref, sums_ref, weighted_ref, through_ref, local_ref, *refs):
    entered, partner_ref, (in_ref, grad_b_ref, token_ref) = refs[:2], refs[2], refs[3:]
    token_ref[...] = jnp.zeros_like(token_ref)
    grad_b = sums_ref[...]
    width = partner_ref.shape[1] // 2
    for half in range(2):
        here = slice(half * width, (half + 1) * width)
        core = table_ref[CORE_ROW, here]
        entering = jnp.where(core == float(half), entered[0][...].astype(F32), entered[1][...].astype(F32))
        inner = through_ref[THROUGH, here] * entering + partner_ref[:, here].astype(F32)
        adjoint = jnp.where(core == 1.0, entering, inner).astype(BF)
        grad_b += dot(weighted_ref[:, here], adjoint, 1, 1)
        for number in range(width // PAIR):
            pair = half * (width // PAIR) + number
            at = slice(pair * PAIR, (pair + 1) * PAIR)
            term = dot(b_ref[...], adjoint[:, number * PAIR : (number + 1) * PAIR], 1, 0)
            in_ref[:, at] = (local_ref[:, at] + end_ref[:, at] * term).astype(BF)
    grad_b_ref[...] = grad_b


def add_kernel(parts, *refs):
    kept, came, out_ref = refs[:parts], refs[parts:-1], refs[-1]
    for group, change in ((kept, False), (came, True)):
        start = 0
        for ref in group:
            at = slice(start, start + ref.shape[1])
            out_ref[:, at] = out_ref[:, at] + ref[...].astype(F32) if change else ref[...]
            start += ref.shape[1]


def weight_partial_kernel(chips, pieces, *refs):
    owns, came, refs = refs[:2], (refs[2:4], refs[4:6]), refs[6:]
    outputs, kept_ref, sent = refs[: -1 - pieces], refs[-1 - pieces], refs[-pieces:]
    depth = kept_ref.shape[0]
    outputs = [ref[...] for ref in outputs]
    if len(outputs) > 2 * chips:
        cut = outputs[chips + 1 :]
        outputs = outputs[: chips + 1] + [jnp.concatenate(cut[i : i + 2], axis=1) for i in range(0, len(cut), 2)]
    for slot in (1, 0):
        total = None
        for number, output in enumerate(outputs):
            core, by = number // chips, number % chips
            if by == 0:
                grad = owns[core][:, slot * depth : (slot + 1) * depth]
            else:
                grad = came[core][slot][(by - 1) * Q : by * Q, :]
            term = dot(grad, output, 0, 0)
            total = term if total is None else total + term
        if slot == 0:
            kept_ref[...] = total
            continue
        start = 0
        for ref in sent:
            ref[...] = total[:, start : start + ref.shape[1]].astype(BF)
            start += ref.shape[1]


def body(
    ssm_input, b_input, c_input, step_size, decay_rate, skip_gain, resets, out_grad, out_weight
):
    seq, dp, planes = lax.axis_size("seq"), lax.axis_size("dp"), lax.axis_size("tensor")
    chips = seq // 2
    me = lax.axis_index(("seq", "tensor", "dp"))
    heads = decay_rate.shape[0]
    wide = heads * P_SIZE
    widths = [wide * share // sum(SHARES) // PAIR * PAIR for share in SHARES]
    starts = [sum(widths[:part]) for part in range(len(widths))]
    depth = out_weight.shape[0]
    span = 4 * depth
    assert ssm_input.shape[1] == Q and dp == 2 and seq % 2 == 0 and seq > 2 and planes % 2 == 0
    def later(value, other):
        return lax.optimization_barrier((value, other))[0]

    across = [(i, i ^ 1) for i in range(seq)]

    def core_swap(value):
        return lax.ppermute(value, "seq", across)

    def chip_shift(value, by):
        return lax.ppermute(value, "seq", [(i, (i + 2 * by) % seq) for i in range(seq)])

    def plane_swap(value):
        return lax.ppermute(value, "tensor", [(i, i ^ 1) for i in range(planes)])

    def dialogue_swap(value):
        return lax.ppermute(value, "dp", [(0, 1), (1, 0)])

    x, b_rows, c_rows, steps, incoming = (
        ssm_input[0], b_input[0], c_input[0], step_size[0], out_grad[0]
    )
    ids = Ids(me.astype(jnp.int32).reshape(1), chips, planes, dp)

    to_send = [
        column_call(send_kernel, CHIP + by, ids, incoming, [], span, [((Q, 2 * depth), BF)])
        for by in range(1, chips)
    ]

    weight_other = dialogue_swap(out_weight)
    weight_core = core_swap(out_weight)

    near = [chip_shift(to_send[by - 1][0], by) for by in range(1, chips)]
    pieces = []
    for piece in near:
        pieces += [piece, plane_swap(piece)]

    *both, weighted_in, log_rows, log_cols, through, from_start, to_end = call(
        tables_kernel,
        (ids, decay_rate, resets, skip_gain),
        (x, b_rows, steps),
        [((N, wide // 2), F32)] * 2 + [((N, wide // 2), BF)] * 2 + [((Q, wide), BF)]
        + [((heads, Q), F32), ((Q, heads), F32), ((8, wide), F32)]
        + [((Q, wide), F32)] * 2,
        after=[weight_core, *[sent[0] for sent in to_send]],
    )
    local_output, = call(
        local_output_kernel,
        (),
        (through, x, b_rows, c_rows, log_rows, log_cols),
        [((Q, wide), F32)],
    )
    state_partner = [core_swap(half) for half in both[2:]]
    through_partner = core_swap(through)
    mine, other = column_call(
        own_kernel, CHIP, ids, incoming, [], span, [((Q, span // 2), BF)] * 2, after=[through]
    )
    partner = core_swap(other)
    before = []
    for hop in range(1, chips):
        total, = call(
            functools.partial(chip_total_kernel, 1, 2),
            (),
            (through, through_partner, *both[:2], *state_partner, *before),
            [((N, wide), BF)],
            after=[local_output] if hop == 1 else (),
        )
        before = [lax.ppermute(total, "seq", [(i, i + 2) for i in range(seq - 2)])]
    results = call(
        functools.partial(output_kernel, starts),
        (),
        (through, local_output, c_rows, from_start, through_partner, *before, *state_partner),
        [((Q, width), BF) for width in widths] + [((N, width), BF) for width in widths],
        after=[partner],
    )
    outputs, states = results[: len(widths)], results[len(widths) :]
    swapped = [core_swap(output) for output in outputs]
    outputs = [[output] + [chip_shift(output, by) for by in range(1, chips)] for output in outputs]

    came = call(
        assemble_kernel, (), (through, *pieces), [(((chips - 1) * Q, depth), BF)] * 4, after=[outputs[-1][0]],
    )
    partner_came = [core_swap(block) for block in came[2:]]
    weight_late = later(weight_other, outputs[-1][0])
    weights = [out_weight, weight_other, weight_core]
    weights += [core_swap(weight_late[: depth // 2]), core_swap(weight_late[depth // 2 :])]

    partials = call(
        head_partial_kernel,
        (),
        (mine, other, *came, *weights),
        [((Q, wide), F32)] + [((Q, wide), BF)] * (chips - 1),
    )
    returned = [chip_shift(partials[by], -by) for by in range(1, chips)]

    sent, kept, sums = [], [], []
    for part, width in enumerate(widths):
        pieces = [later(piece, sent[-1] if sent else partials[0]) for piece in outputs[part][1:]]
        cut = width // 2 if width > wide // 2 else width
        swaps = [core_swap(piece[:, at : at + cut]) for piece in pieces for at in range(0, width, cut)]
        sizes = [width]
        partial, *own = call(
            functools.partial(weight_partial_kernel, chips, len(sizes)),
            (),
            (mine, partner, *came[:2], *partner_came, *outputs[part], swapped[part], *swaps),
            [((depth, width), F32)] + [((depth, size), BF) for size in sizes],
            after=[partials[0], *sent[-1:]],
        )
        sent.append(own[0])
        kept.append(partial)
        sums += [dialogue_swap(value) for value in own]

    head_grad, weighted_grad, *both = call(
        functools.partial(adjoint_kernel, chips - 1),
        (),
        (through, partials[0], *returned, c_rows, from_start),
        [((Q, wide), BF), ((Q, wide), BF)] + [((N, wide // 2), F32)] * 2 + [((N, wide), BF)],
        after=[sums[0], *sent],
    )
    adjoint_partner = core_swap(both[2])
    local_in, paired, c_part = call(
        local_grads_kernel,
        (),
        (through, x, head_grad, b_rows, c_rows, log_rows, log_cols, weighted_grad, *states),
        [((Q, wide), F32), ((Q, Q), F32), ((Q, N), F32)],
    )
    entering = []
    for hop in range(1, chips):
        total, = call(
            functools.partial(chip_total_kernel, 0, 1),
            (),
            (through, through_partner, *both[:2], adjoint_partner, *entering),
            [((N, wide // 2), BF)],
        )
        entering = [lax.ppermute(total, "seq", [(i, i - 2) for i in range(2, seq)])]
    grad_b, grad_c = call(
        group_sums_kernel,
        (),
        (b_rows, c_rows, paired, c_part),
        [((Q, N), F32), ((Q, N), F32)],
    )
    grad_in, grad_b, token = call(
        final_kernel,
        (),
        (through, b_rows, to_end, grad_b, weighted_in, through_partner, local_in)
        + (*entering, core_swap(later(entering[0], grad_c)), adjoint_partner),
        [((Q, wide), BF), ((Q, N), F32), ((8, 128), F32)],
    )
    step = depth // 2
    grad_weight = pl.pallas_call(
        lambda *refs: add_kernel(len(widths), *refs[:-2], refs[-1]),
        grid=(depth // step,),
        out_shape=jax.ShapeDtypeStruct((depth, wide), F32),
        in_specs=[pl.BlockSpec((step, item.shape[1]), lambda i: (i, 0)) for item in (*kept, *sums)] + [ANY],
        out_specs=pl.BlockSpec((step, wide), lambda i: (i, 0)),
        cost_estimate=FREE,
        compiler_params=LIMIT,
        name="add_kernel",
    )(*kept, *sums, token)
    return grad_in[None], grad_b[None], grad_c[None], grad_weight


def solution(mesh):
    in_specs = (
        P("dp", "seq", "tensor"),
        P("dp", "seq", "tensor"),
        P("dp", "seq", "tensor"),
        P("dp", "tensor", "seq"),
        P("tensor"),
        P("tensor"),
        P("dp", "seq"),
        P("dp", "seq", None),
        P(("seq", "dp"), "tensor"),
    )
    out_specs = (
        P("dp", "seq", "tensor"),
        P("dp", "seq", "tensor"),
        P("dp", "seq", "tensor"),
        P(("seq", "dp"), "tensor"),
    )
    return jax.shard_map(body, mesh=mesh, in_specs=in_specs, out_specs=out_specs, check_vma=False)
```

```python
import functools

import jax
import jax.numpy as jnp
from jax import lax
from jax.experimental import pallas as pl
from jax.experimental.pallas import tpu as pltpu
from jax.sharding import PartitionSpec as P

P_SIZE = 64
N = 128
Q = 256
HALF = 128
PAIR = 2 * P_SIZE
SHARES = (6, 10)
PARITY, CORE, ODD, CHIP = 4, 6, 7, 8
THROUGH, KEEP, CORE_ROW, SKIP, ODD_ROW = (slice(row, row + 1) for row in range(5))
BF = jnp.bfloat16
F32 = jnp.float32

SMEM = pl.BlockSpec(memory_space=pltpu.SMEM)
ANY = pl.BlockSpec(memory_space=pl.ANY)
FREE = pl.CostEstimate(flops=0, bytes_accessed=0, transcendentals=0)
LIMIT = pltpu.CompilerParams(vmem_limit_bytes=16 * 2**20)


def name_of(kernel):
    return getattr(kernel, "func", kernel).__name__


def whole(shape):
    return pl.BlockSpec(shape, lambda *_: (0,) * len(shape))


def call(kernel, scalars, arrays, outs, after=(), aliases=None):
    pairs = [item if isinstance(item, tuple) else (item, whole(item.shape)) for item in arrays]
    outs = [item if len(item) == 3 else (*item, whole(item[0])) for item in outs]
    count = len(scalars)
    views = [item.view if isinstance(item, Ids) else (lambda ref: ref) for item in scalars]
    scalars = [item.number if isinstance(item, Ids) else item for item in scalars]

    def run(*refs):
        seen = [view(ref) for view, ref in zip(views, refs)]
        kernel(*seen, *refs[count : count + len(pairs)], *refs[count + len(pairs) + len(after) :])

    return pl.pallas_call(
        run,
        grid=(1,),
        out_shape=[jax.ShapeDtypeStruct(shape, kind) for shape, kind, _ in outs],
        in_specs=[SMEM] * count + [spec for _, spec in pairs] + [ANY] * len(after),
        out_specs=[spec for _, _, spec in outs],
        input_output_aliases=aliases or {},
        cost_estimate=FREE,
        compiler_params=LIMIT,
        name=name_of(kernel),
    )(*scalars, *[array for array, _ in pairs], *after)


class Ids:
    def __init__(self, number, chips, planes, dp):
        self.number, self.sizes = number, (chips, planes, dp)

    def view(self, ref):
        seen = Ids(None, *self.sizes)
        seen.ref = ref
        return seen

    def __getitem__(self, place):
        chips, planes, dp = self.sizes
        at = self.ref[0]
        chip, core, odd, dialogue = at // (2 * planes * dp), at // (planes * dp) % 2, at // dp % 2, at % dp
        if place >= CHIP:
            return (chip + place - CHIP) % chips
        if place in (CORE, ODD):
            return core if place == CORE else odd
        if place >= PARITY:
            half, second = place - PARITY, odd
        else:
            half, second = place // 2, place % 2
        own = core if half == 0 else 1 - core
        return own * 2 + (dialogue + second) % 2


def column_call(kernel, at, ids, grads, others, span, outs, after=()):
    def run(ids_ref, *refs):
        kernel(ids.view(ids_ref), *refs[: 1 + len(others)], *refs[1 + len(others) + len(after) :])

    return pl.pallas_call(
        run,
        out_shape=[jax.ShapeDtypeStruct(shape, kind) for shape, kind in outs],
        grid_spec=pltpu.PrefetchScalarGridSpec(
            num_scalar_prefetch=1,
            grid=(1,),
            in_specs=[pl.BlockSpec((Q, span), lambda i, ids_ref: (0, ids.view(ids_ref)[at]))]
            + [whole(other.shape) for other in others]
            + [ANY] * len(after),
            out_specs=[whole(shape) for shape, _ in outs],
        ),
        cost_estimate=FREE,
        compiler_params=LIMIT,
        name=name_of(kernel),
    )(ids.number, grads, *others, *after)


def dot(a, b, left, right):
    return lax.dot_general(a, b, (((left,), (right,)), ((), ())), preferred_element_type=F32)


def first_head(rows=Q):
    return lax.broadcasted_iota(jnp.int32, (rows, PAIR), 1) < P_SIZE


def spread(table, pair, first):
    return jnp.where(first, table[:, 2 * pair : 2 * pair + 1], table[:, 2 * pair + 1 : 2 * pair + 2])


def gains(skip_ref, head):
    first = lax.broadcasted_iota(jnp.int32, (1, PAIR), 1) < P_SIZE
    return jnp.where(first, skip_ref[head], skip_ref[head + 1])


def tables_kernel(
    ids_ref, rate_ref, resets_ref, skip_ref, x_ref, b_ref, step_ref, *refs
):
    states, sent, (weighted_ref, rows_ref, cols_ref, table_ref, from_ref, end_ref) = refs[:2], refs[2:4], refs[4:]
    heads = step_ref.shape[0]
    keep = (1 - resets_ref[0, 0]).astype(F32)
    head_id = lax.broadcasted_iota(jnp.int32, (heads, Q), 0)
    lane = lax.broadcasted_iota(jnp.int32, (heads, Q), 1)
    rate = jnp.zeros((heads, Q), F32)
    for head in range(heads):
        rate = jnp.where(head_id == head, rate_ref[head], rate)
    log = -step_ref[...] * rate
    shift = 1
    while shift < Q:
        log = log + jnp.where(lane >= shift, pltpu.roll(log, shift, 1), 0.0)
        shift *= 2
    rows_ref[...] = log
    cols = log.T
    cols_ref[...] = cols
    first = first_head()
    for pair in range(heads // 2):
        at = slice(pair * PAIR, (pair + 1) * PAIR)
        log_pair = spread(cols, pair, first)
        last = log_pair[Q - 1 : Q, :]
        to_end = jnp.exp(last - log_pair)
        end_ref[:, at] = to_end
        from_ref[:, at] = jnp.exp(log_pair)
        weighted_ref[:, at] = (x_ref[:, at].astype(F32) * to_end).astype(BF)
        table_ref[THROUGH, at] = keep * jnp.exp(last)
        table_ref[SKIP, at] = gains(skip_ref, 2 * pair)
    ones = jnp.ones((1, table_ref.shape[1]), F32)
    table_ref[KEEP, :] = keep * ones
    table_ref[CORE_ROW, :] = ids_ref[CORE].astype(F32) * ones
    table_ref[ODD_ROW, :] = ids_ref[ODD].astype(F32) * ones
    table_ref[5:, :] = jnp.zeros((3, table_ref.shape[1]), F32)
    state = dot(b_ref[...], weighted_ref[...], 0, 0)
    middle = state.shape[1] // 2
    for number in range(2):
        half = state[:, number * middle : (number + 1) * middle]
        states[number][...] = half
        sent[number][...] = half.astype(BF)


def local_output_kernel(table_ref, x_ref, b_ref, c_ref, rows_ref, cols_ref, out_ref):
    heads = rows_ref.shape[0]
    scores = dot(c_ref[...], b_ref[...], 1, 1)
    at_row = lax.broadcasted_iota(jnp.int32, (HALF, HALF), 0)
    at_lane = lax.broadcasted_iota(jnp.int32, (HALF, HALF), 1)
    causal = at_row >= at_lane
    first = first_head()
    zero = jnp.zeros((Q, PAIR), BF)
    for pair in range(heads // 2):
        at = slice(pair * PAIR, (pair + 1) * PAIR)
        x_pair = x_ref[:, at]
        skip = table_ref[SKIP, at] * x_pair.astype(F32)
        top, bottom = skip[:HALF], skip[HALF:]
        for side in range(2):
            head = 2 * pair + side
            x_head = jnp.where(first, x_pair, zero) if side == 0 else jnp.where(first, zero, x_pair)
            col = cols_ref[:, head : head + 1]
            row = rows_ref[head : head + 1, :]

            def mix(i, j):
                span = col[i * HALF : (i + 1) * HALF] - row[:, j * HALF : (j + 1) * HALF]
                weight = jnp.exp(jnp.minimum(span, 0.0))
                if i == j:
                    weight = jnp.where(causal, weight, 0.0)
                return (weight * scores[i * HALF : (i + 1) * HALF, j * HALF : (j + 1) * HALF]).astype(BF)

            top += dot(mix(0, 0), x_head[:HALF], 1, 0)
            bottom += dot(jnp.concatenate([mix(1, 0), mix(1, 1)], axis=1), x_head, 1, 0)
        out_ref[:HALF, at] = top
        out_ref[HALF:, at] = bottom


def output_kernel(starts, table_ref, local_ref, c_ref, from_ref, through_ref, before_ref, *refs):
    partners, outs, states = refs[:2], refs[2 : 2 + len(starts)], refs[2 + len(starts) :]
    partner = jnp.concatenate([ref[...] for ref in partners], axis=1)
    for start, out_ref, state_ref in zip(starts, outs, states):
        part = slice(start, start + out_ref.shape[1])
        before = before_ref[:, part].astype(F32)
        after = through_ref[THROUGH, part] * before + partner[:, part].astype(F32)
        state = jnp.where(table_ref[CORE_ROW, part] == 1.0, after, before)
        state_ref[...] = (table_ref[KEEP, part] * state).astype(BF)
        for pair in range(out_ref.shape[1] // PAIR):
            at = slice(pair * PAIR, (pair + 1) * PAIR)
            whole = slice(start + pair * PAIR, start + (pair + 1) * PAIR)
            term = dot(c_ref[...], state_ref[:, at], 1, 0)
            out_ref[:, at] = (local_ref[:, whole] + from_ref[:, whole] * term).astype(BF)


def block_of(ids_ref, grad_ref, slot):
    depth = grad_ref.shape[1] // 4
    return grad_ref[:, pl.ds(pl.multiple_of(ids_ref[slot] * depth, depth), depth)]


def send_kernel(ids_ref, grad_ref, out_ref):
    depth = out_ref.shape[1] // 2
    for half in range(2):
        out_ref[:, half * depth : (half + 1) * depth] = block_of(ids_ref, grad_ref, PARITY + half)


def own_kernel(ids_ref, grad_ref, *halves):
    depth = halves[0].shape[1] // 2
    for slot in range(4):
        halves[slot // 2][:, slot % 2 * depth : (slot % 2 + 1) * depth] = block_of(ids_ref, grad_ref, slot)


def assemble_kernel(table_ref, *refs):
    pieces, blocks = refs[:-4], refs[-4:]
    depth = blocks[0].shape[1]
    even = table_ref[ODD_ROW, :depth] == 0.0
    for number, out_ref in enumerate(blocks):
        taken = slice(number // 2 * depth, (number // 2 + 1) * depth)
        for other in range(len(pieces) // 2):
            near, far = pieces[2 * other], pieces[2 * other + 1]
            first, second = (near, far) if number % 2 == 0 else (far, near)
            rows = slice(other * Q, (other + 1) * Q)
            out_ref[rows, :] = jnp.where(even, first[:, taken], second[:, taken])


def head_partial_kernel(mine_ref, other_ref, *refs):
    came, weights, outs = refs[:4], refs[4:9], refs[9:]
    depth = weights[0].shape[0]
    middle = weights[3].shape[0]
    for number in reversed(range(len(outs))):
        total = None
        for block in range(4):
            rows = slice((number - 1) * Q, number * Q)
            if number == 0:
                grad = (mine_ref, other_ref)[block // 2][:, block % 2 * depth : (block % 2 + 1) * depth]
            else:
                grad = came[block][rows, :]
            if block < 3:
                term = dot(grad, weights[block][...], 1, 0)
            else:
                term = dot(grad[:, :middle], weights[3][...], 1, 0) + dot(grad[:, middle:], weights[4][...], 1, 0)
            total = term if total is None else total + term
        outs[number][...] = total.astype(outs[number].dtype)


def adjoint_kernel(others, table_ref, own_ref, *refs):
    parts, (c_ref, from_ref, head_ref, weighted_ref, *halves) = refs[:others], refs[others:]
    for pair in range(head_ref.shape[1] // PAIR):
        at = slice(pair * PAIR, (pair + 1) * PAIR)
        total = own_ref[:, at]
        for part in parts:
            total = total + part[:, at].astype(F32)
        head = total.astype(BF)
        head_ref[:, at] = head
        weighted_ref[:, at] = (head.astype(F32) * from_ref[:, at]).astype(BF)
    adjoint = table_ref[KEEP, :] * dot(c_ref[...], weighted_ref[...], 0, 0)
    middle = adjoint.shape[1] // 2
    for number in range(2):
        half = adjoint[:, number * middle : (number + 1) * middle]
        halves[number][...] = half
        halves[2][:, number * middle : (number + 1) * middle] = half.astype(BF)


def chip_total_kernel(last, parts, through_ref, partner_through_ref, *refs):
    owns, partners, entering, out_ref = refs[:2], refs[2 : 2 + parts], refs[2 + parts : -1], refs[-1]
    width = owns[0].shape[1]
    halved = out_ref.shape[1] < 2 * width
    partner_state = jnp.concatenate([ref[...] for ref in partners], axis=1)
    totals = []
    for part in range(2):
        at = slice(part * width, (part + 1) * width)
        own, partner = owns[part][...], partner_state[:, at].astype(F32)
        mine, theirs = through_ref[THROUGH, at], partner_through_ref[THROUGH, at]
        leaves = through_ref[CORE_ROW, at] == float(last)
        total = jnp.where(leaves, mine * partner + own, theirs * own + partner)
        for value in entering:
            came = value[...] if halved else value[:, at]
            total += mine * theirs * came.astype(F32)
        if halved:
            totals.append(total)
        else:
            out_ref[:, at] = total.astype(BF)
    if halved:
        first_core = through_ref[CORE_ROW, :width] == 0.0
        out_ref[...] = jnp.where(first_core, totals[0], totals[1]).astype(BF)


def local_grads_kernel(
    table_ref, x_ref, grad_ref, b_ref, c_ref, rows_ref, cols_ref, weighted_ref, *refs
):
    states, (in_ref, paired_ref, c_out_ref) = refs[:-3], refs[-3:]
    heads = x_ref.shape[1] // P_SIZE
    scores = dot(b_ref[...], c_ref[...], 1, 1)
    at_row = lax.broadcasted_iota(jnp.int32, (HALF, HALF), 0)
    at_lane = lax.broadcasted_iota(jnp.int32, (HALF, HALF), 1)
    causal = at_lane >= at_row
    first = first_head()
    zero = jnp.zeros((Q, PAIR), BF)
    paired_ref[...] = jnp.zeros_like(paired_ref)
    for pair in range(heads // 2):
        at = slice(pair * PAIR, (pair + 1) * PAIR)
        x_pair = x_ref[:, at]
        g_pair = grad_ref[:, at]
        skip = table_ref[SKIP, at] * g_pair.astype(F32)
        top, bottom = skip[:HALF], skip[HALF:]
        for side in range(2):
            head = 2 * pair + side
            g_head = jnp.where(first, g_pair, zero) if side == 0 else jnp.where(first, zero, g_pair)
            col = cols_ref[:, head : head + 1]
            row = rows_ref[head : head + 1, :]

            def weigh(j, i):
                span = row[:, i * HALF : (i + 1) * HALF] - col[j * HALF : (j + 1) * HALF]
                weight = jnp.exp(jnp.minimum(span, 0.0))
                return jnp.where(causal, weight, 0.0) if i == j else weight

            early = jnp.concatenate([weigh(0, 0), weigh(0, 1)], axis=1)
            late = weigh(1, 1)
            top += dot((early * scores[:HALF]).astype(BF), g_head, 1, 0)
            bottom += dot((late * scores[HALF:, HALF:]).astype(BF), g_head[HALF:], 1, 0)
            paired_ref[:HALF, :] += early * dot(x_pair[:HALF], g_head, 1, 1)
            paired_ref[HALF:, HALF:] += late * dot(x_pair[HALF:], g_head[HALF:], 1, 1)
        in_ref[:HALF, at] = top
        in_ref[HALF:, at] = bottom
    start, total = 0, None
    for state in states:
        width = state.shape[1]
        term = dot(weighted_ref[:, start : start + width], state[...], 1, 1)
        total = term if total is None else total + term
        start += width
    c_out_ref[...] = total


def group_sums_kernel(b_ref, c_ref, paired_ref, c_part_ref, grad_b_ref, grad_c_ref):
    paired = paired_ref[...].astype(BF)
    grad_b_ref[...] = dot(paired, c_ref[...], 1, 0)
    grad_c_ref[...] = c_part_ref[...] + dot(paired, b_ref[...], 0, 0)


def final_kernel(table_ref, b_ref, end_ref, sums_ref, weighted_ref, through_ref, local_ref, *refs):
    entered, partner_ref, (in_ref, grad_b_ref) = refs[:2], refs[2], refs[3:]
    grad_b = sums_ref[...]
    width = partner_ref.shape[1] // 2
    for half in range(2):
        here = slice(half * width, (half + 1) * width)
        core = table_ref[CORE_ROW, here]
        entering = jnp.where(core == float(half), entered[0][...].astype(F32), entered[1][...].astype(F32))
        inner = through_ref[THROUGH, here] * entering + partner_ref[:, here].astype(F32)
        adjoint = jnp.where(core == 1.0, entering, inner).astype(BF)
        grad_b += dot(weighted_ref[:, here], adjoint, 1, 1)
        for number in range(width // PAIR):
            pair = half * (width // PAIR) + number
            at = slice(pair * PAIR, (pair + 1) * PAIR)
            term = dot(b_ref[...], adjoint[:, number * PAIR : (number + 1) * PAIR], 1, 0)
            in_ref[:, at] = (local_ref[:, at] + end_ref[:, at] * term).astype(BF)
    grad_b_ref[...] = grad_b


def add_kernel(parts, *refs):
    kept, came, out_ref = refs[:parts], refs[parts:-1], refs[-1]
    for group, change in ((kept, False), (came, True)):
        start = 0
        for ref in group:
            at = slice(start, start + ref.shape[1])
            out_ref[:, at] = out_ref[:, at] + ref[...].astype(F32) if change else ref[...]
            start += ref.shape[1]


def last_kernel(parts, *refs):
    add_kernel(parts, *refs[-3 - 2 * parts : -3], refs[-1])
    final_kernel(*refs[: -3 - 2 * parts], *refs[-3:-1])


def weight_partial_kernel(chips, pieces, *refs):
    owns, came, refs = refs[:2], (refs[2:4], refs[4:6]), refs[6:]
    outputs, kept_ref, sent = refs[: -1 - pieces], refs[-1 - pieces], refs[-pieces:]
    depth = kept_ref.shape[0]
    outputs = [ref[...] for ref in outputs]
    if len(outputs) > 2 * chips:
        cut = outputs[chips + 1 :]
        outputs = outputs[: chips + 1] + [jnp.concatenate(cut[i : i + 2], axis=1) for i in range(0, len(cut), 2)]
    for slot in (1, 0):
        total = None
        for number, output in enumerate(outputs):
            core, by = number // chips, number % chips
            if by == 0:
                grad = owns[core][:, slot * depth : (slot + 1) * depth]
            else:
                grad = came[core][slot][(by - 1) * Q : by * Q, :]
            term = dot(grad, output, 0, 0)
            total = term if total is None else total + term
        if slot == 0:
            kept_ref[...] = total
            continue
        start = 0
        for ref in sent:
            ref[...] = total[:, start : start + ref.shape[1]].astype(BF)
            start += ref.shape[1]


def body(
    ssm_input, b_input, c_input, step_size, decay_rate, skip_gain, resets, out_grad, out_weight
):
    seq, dp, planes = lax.axis_size("seq"), lax.axis_size("dp"), lax.axis_size("tensor")
    chips = seq // 2
    me = lax.axis_index(("seq", "tensor", "dp"))
    heads = decay_rate.shape[0]
    wide = heads * P_SIZE
    widths = [wide * share // sum(SHARES) // PAIR * PAIR for share in SHARES]
    starts = [sum(widths[:part]) for part in range(len(widths))]
    depth = out_weight.shape[0]
    span = 4 * depth
    assert ssm_input.shape[1] == Q and dp == 2 and seq % 2 == 0 and seq > 2 and planes % 2 == 0
    def later(value, other):
        return lax.optimization_barrier((value, other))[0]

    across = [(i, i ^ 1) for i in range(seq)]

    def core_swap(value):
        return lax.ppermute(value, "seq", across)

    def chip_shift(value, by):
        return lax.ppermute(value, "seq", [(i, (i + 2 * by) % seq) for i in range(seq)])

    def plane_swap(value):
        return lax.ppermute(value, "tensor", [(i, i ^ 1) for i in range(planes)])

    def dialogue_swap(value):
        return lax.ppermute(value, "dp", [(0, 1), (1, 0)])

    x, b_rows, c_rows, steps, incoming = (
        ssm_input[0], b_input[0], c_input[0], step_size[0], out_grad[0]
    )
    ids = Ids(me.astype(jnp.int32).reshape(1), chips, planes, dp)

    to_send = [
        column_call(send_kernel, CHIP + by, ids, incoming, [], span, [((Q, 2 * depth), BF)])
        for by in range(1, chips)
    ]

    weight_other = dialogue_swap(out_weight)
    weight_core = core_swap(out_weight)

    near = [chip_shift(to_send[by - 1][0], by) for by in range(1, chips)]
    pieces = []
    for piece in near:
        pieces += [piece, plane_swap(piece)]

    *both, weighted_in, log_rows, log_cols, through, from_start, to_end = call(
        tables_kernel,
        (ids, decay_rate, resets, skip_gain),
        (x, b_rows, steps),
        [((N, wide // 2), F32)] * 2 + [((N, wide // 2), BF)] * 2 + [((Q, wide), BF)]
        + [((heads, Q), F32), ((Q, heads), F32), ((8, wide), F32)]
        + [((Q, wide), F32)] * 2,
        after=[weight_core, *[sent[0] for sent in to_send]],
    )
    local_output, = call(
        local_output_kernel,
        (),
        (through, x, b_rows, c_rows, log_rows, log_cols),
        [((Q, wide), F32)],
    )
    state_partner = [core_swap(half) for half in both[2:]]
    through_partner = core_swap(through)
    mine, other = column_call(
        own_kernel, CHIP, ids, incoming, [], span, [((Q, span // 2), BF)] * 2, after=[through]
    )
    partner = core_swap(other)
    before = []
    for hop in range(1, chips):
        total, = call(
            functools.partial(chip_total_kernel, 1, 2),
            (),
            (through, through_partner, *both[:2], *state_partner, *before),
            [((N, wide), BF)],
            after=[local_output] if hop == 1 else (),
        )
        before = [lax.ppermute(total, "seq", [(i, i + 2) for i in range(seq - 2)])]
    results = call(
        functools.partial(output_kernel, starts),
        (),
        (through, local_output, c_rows, from_start, through_partner, *before, *state_partner),
        [((Q, width), BF) for width in widths] + [((N, width), BF) for width in widths],
        after=[partner],
    )
    outputs, states = results[: len(widths)], results[len(widths) :]
    swapped = [core_swap(output) for output in outputs]
    outputs = [[output] + [chip_shift(output, by) for by in range(1, chips)] for output in outputs]

    came = call(
        assemble_kernel, (), (through, *pieces), [(((chips - 1) * Q, depth), BF)] * 4, after=[outputs[-1][0]],
    )
    partner_came = [core_swap(block) for block in came[2:]]
    weight_late = later(weight_other, outputs[-1][0])
    weights = [out_weight, weight_other, weight_core]
    weights += [core_swap(weight_late[: depth // 2]), core_swap(weight_late[depth // 2 :])]

    partials = call(
        head_partial_kernel,
        (),
        (mine, other, *came, *weights),
        [((Q, wide), F32)] + [((Q, wide), BF)] * (chips - 1),
    )
    returned = [chip_shift(partials[by], -by) for by in range(1, chips)]

    sent, kept, sums = [], [], []
    for part, width in enumerate(widths):
        pieces = [later(piece, sent[-1] if sent else partials[0]) for piece in outputs[part][1:]]
        cut = width // 2 if width > wide // 2 else width
        swaps = [core_swap(piece[:, at : at + cut]) for piece in pieces for at in range(0, width, cut)]
        sizes = [width]
        partial, *own = call(
            functools.partial(weight_partial_kernel, chips, len(sizes)),
            (),
            (mine, partner, *came[:2], *partner_came, *outputs[part], swapped[part], *swaps),
            [((depth, width), F32)] + [((depth, size), BF) for size in sizes],
            after=[partials[0], *sent[-1:]],
        )
        sent.append(own[0])
        kept.append(partial)
        sums += [dialogue_swap(value) for value in own]

    head_grad, weighted_grad, *both = call(
        functools.partial(adjoint_kernel, chips - 1),
        (),
        (through, partials[0], *returned, c_rows, from_start),
        [((Q, wide), BF), ((Q, wide), BF)] + [((N, wide // 2), F32)] * 2 + [((N, wide), BF)],
        after=[sums[0], *sent],
    )
    adjoint_partner = core_swap(both[2])
    local_in, paired, c_part = call(
        local_grads_kernel,
        (),
        (through, x, head_grad, b_rows, c_rows, log_rows, log_cols, weighted_grad, *states),
        [((Q, wide), F32), ((Q, Q), F32), ((Q, N), F32)],
    )
    entering = []
    for hop in range(1, chips):
        total, = call(
            functools.partial(chip_total_kernel, 0, 1),
            (),
            (through, through_partner, *both[:2], adjoint_partner, *entering),
            [((N, wide // 2), BF)],
        )
        entering = [lax.ppermute(total, "seq", [(i, i - 2) for i in range(2, seq)])]
    grad_b, grad_c = call(
        group_sums_kernel,
        (),
        (b_rows, c_rows, paired, c_part),
        [((Q, N), F32), ((Q, N), F32)],
    )
    grad_in, grad_b, grad_weight = call(
        functools.partial(last_kernel, len(widths)),
        (),
        (through, b_rows, to_end, grad_b, weighted_in, through_partner, local_in)
        + (*entering, core_swap(later(entering[0], grad_c)), adjoint_partner)
        + (*kept, *sums),
        [((Q, wide), BF), ((Q, N), F32), ((depth, wide), F32)],
    )
    return grad_in[None], grad_b[None], grad_c[None], grad_weight


def solution(mesh):
    in_specs = (
        P("dp", "seq", "tensor"),
        P("dp", "seq", "tensor"),
        P("dp", "seq", "tensor"),
        P("dp", "tensor", "seq"),
        P("tensor"),
        P("tensor"),
        P("dp", "seq"),
        P("dp", "seq", None),
        P(("seq", "dp"), "tensor"),
    )
    out_specs = (
        P("dp", "seq", "tensor"),
        P("dp", "seq", "tensor"),
        P("dp", "seq", "tensor"),
        P(("seq", "dp"), "tensor"),
    )
    return jax.shard_map(body, mesh=mesh, in_specs=in_specs, out_specs=out_specs, check_vma=False)
```
